32 devices in a mesh: parts: 2 (over y), blk: 4 (over z), grp: 2 (over x), sub: 2 (over core).
Axes of the slice: x: 2, y: 2, z: 4, core: 2. Of those that a mesh axis runs over, the one named last changes fastest.
Arguments:
- features: bfloat16 [128, 8192], P(None, ('parts', 'blk', 'grp', 'sub')), parts along dimension 1, may hold values from -6 to 6
- lengthscale: float32 [256], P('parts'), parts along dimension 0, may hold values from 4 to 12
- noise_var: float32 [8192], P(('parts', 'blk', 'grp', 'sub')), parts along dimension 0, may hold values from 0.05 to 1
- probes: float32 [16, 8192], P(None, ('parts', 'blk', 'grp', 'sub')), parts along dimension 1, may hold values from -24 to 24
Outputs:
- solution: float32 [16, 8192], P(None, ('parts', 'blk', 'grp', 'sub')), parts along dimension 1
- residual: float32 [16, 8192], P(None, ('parts', 'blk', 'grp', 'sub')), parts along dimension 1
- direction: float32 [16, 8192], P(None, ('parts', 'blk', 'grp', 'sub')), parts along dimension 1
The draws below stay inside these ranges and needn't reach their ends.
There are 2 independent parts, one for each index of `parts`. The reference program is written for one: setup_inputs(seed, part) draws one part's arguments, and reference() takes and returns one part's arrays. A program takes and returns all parts, laid end to end along the dimension named above; each array names one. Nothing has to cross between parts.
All inputs are finite; a program needn't handle non-finite values.
Results may differ from the reference program's by a relative error of at most 0.005.
Values may be sent and summed in bfloat16 or wider, within the bound.
No kernel may reach another device: no remote copies, remote signals or barrier semaphores. Data moves between devices by JAX's collectives and lax.ppermute only.
A program may use at most 64 MiB of HBM per device.

```python
import math
import jax
import jax.numpy as jnp
from jax import lax

F = 128
P_SIZE = 16
ROWS = 4096


def draw_features(key, part):
    key = jax.random.fold_in(key, 11)
    key_member, key_center, key_noise = jax.random.split(key, 3)
    groups = max(ROWS // 16, 1)
    member = jax.random.randint(key_member, (ROWS,), 0, groups)
    centers = jnp.clip(jax.random.normal(key_center, (F, groups), jnp.float32), -4.0, 4.0)
    noise = jnp.clip(jax.random.normal(key_noise, (F, ROWS), jnp.float32), -4.0, 4.0)
    values = 1.04 * centers[:, member] + 0.39 * noise
    return values.astype(jnp.float32).astype(jnp.bfloat16)


def draw_probes(key, part):
    key = jax.random.fold_in(key, 23)
    key_spread = jax.random.fold_in(key, 0)
    key_values = jax.random.fold_in(key, 2)
    position = jnp.arange(ROWS, dtype=jnp.float32) / ROWS
    spread = jnp.exp(jax.random.uniform(key_spread, (ROWS,), jnp.float32, -1.15, 1.15))
    ramp = jnp.sqrt(1.0 + 2.0 * position)
    values = jnp.clip(jax.random.normal(key_values, (P_SIZE, ROWS), jnp.float32), -4.0, 4.0)
    return (values * (spread * ramp)[None, :]).astype(jnp.float32)


def steps_of(own_key, shape, pieces, low, top_value):
    loudness, own = 1.0, jax.random.fold_in(own_key, 6)
    for dim, parts in pieces:
        draws = jnp.exp(jax.random.uniform(jax.random.fold_in(own, dim), (parts,), jnp.float32, low / len(pieces), top_value / len(pieces)))
        loudness = loudness * jnp.repeat(draws, shape[dim] // parts).reshape([-1 if axis == dim else 1 for axis in range(len(shape))])
    return loudness


def setup_inputs(seed: int = 0, part: int = 0) -> dict:
    arg_keys = jax.random.split(jax.random.key(seed), 5)
    own_keys = jax.random.split(jax.random.fold_in(arg_keys[4], part), 5)
    features = draw_features(jax.random.fold_in(jax.random.fold_in(arg_keys[4], part), 71), part)
    lengthscale = jnp.clip(jnp.exp(jax.random.uniform(own_keys[1], (F,), jnp.float32, math.log(4.0), math.log(12.0))), 4.0, 12.0)
    noise_var = jnp.clip(jnp.exp(math.log(1.0) - 2.9957323 * jax.random.uniform(own_keys[2], (ROWS,), jnp.float32) ** steps_of(own_keys[2], (ROWS,), ((0, 16),), -0.2, 0.2)), 0.05, 1.0)
    probes = draw_probes(jax.random.fold_in(jax.random.fold_in(arg_keys[4], part), 71), part)
    return {"features": features, "lengthscale": lengthscale, "noise_var": noise_var, "probes": probes}


def kernel_rows(scaled, square_norms, probe_bf, row_scaled, row_norms):
    inner = jnp.dot(scaled.T, row_scaled, preferred_element_type=jnp.float32)
    weights = jnp.exp(-0.5 * (square_norms[:, None] + row_norms[None, :] - 2.0 * inner)).astype(jnp.bfloat16)
    return jnp.dot(probe_bf, weights, preferred_element_type=jnp.float32)


def reference(features, lengthscale, noise_var, probes):
    scaled = (features.astype(jnp.float32) / lengthscale[:, None]).astype(jnp.bfloat16)
    square_norms = jnp.sum(jnp.square(scaled.astype(jnp.float32)), axis=0)
    probe_bf = probes.astype(jnp.bfloat16)
    stride = math.gcd(ROWS, 512)
    block_count = ROWS // stride
    row_blocks = jnp.transpose(scaled.reshape(F, block_count, stride), (1, 0, 2))
    norm_blocks = square_norms.reshape(block_count, stride)

    def one_block(block_pair):
        return kernel_rows(scaled, square_norms, probe_bf, block_pair[0], block_pair[1])

    images = lax.map(one_block, (row_blocks, norm_blocks))
    kernel_part = jnp.transpose(images, (1, 0, 2)).reshape(P_SIZE, ROWS)
    image = kernel_part + noise_var[None, :] * probes
    start_norms = jnp.sum(probes * probes, axis=1)
    curvature = jnp.sum(probes * image, axis=1)
    alpha = start_norms / curvature
    solution = alpha[:, None] * probes
    residual = probes - alpha[:, None] * image
    new_norms = jnp.sum(residual * residual, axis=1)
    direction = residual + (new_norms / start_norms)[:, None] * probes
    return (solution, residual, direction)
```

```python
import jax
import jax.numpy as jnp
from jax import lax
from jax.experimental import pallas as pl
from jax.experimental.pallas import tpu as pltpu
from jax.sharding import PartitionSpec as P

AXES = ("blk", "grp", "sub")


def image_kernel(feature_count, own_ref, noise_ref, probes_ref, packed_ref, image_ref, sums_ref):
    own = own_ref[:feature_count, :]
    own_norms = jnp.sum(jnp.square(own.astype(jnp.float32)), axis=0, keepdims=True)
    probes = probes_ref[...]

    def one_block(number, total):
        block = packed_ref[number]
        columns = block[:feature_count, :]
        inner = lax.dot_general(
            columns, own, (((0,), (0,)), ((), ())), preferred_element_type=jnp.float32
        )
        norms = jnp.sum(jnp.square(columns.astype(jnp.float32)), axis=0, keepdims=True)
        weights = jnp.exp(-0.5 * (norms.T + own_norms - 2.0 * inner)).astype(jnp.bfloat16)
        return total + jnp.dot(
            block[feature_count:, :], weights, preferred_element_type=jnp.float32
        )

    total = lax.fori_loop(0, packed_ref.shape[0], one_block, jnp.zeros_like(probes))
    image = total + noise_ref[...] * probes
    image_ref[...] = image
    sums_ref[0] = jnp.sum(probes * probes, axis=1, keepdims=True)
    sums_ref[1] = jnp.sum(probes * image, axis=1, keepdims=True)
    sums_ref[2] = jnp.sum(image * image, axis=1, keepdims=True)


def local(features, lengthscale, noise_var, probes):
    scaled = (features.astype(jnp.float32) / lengthscale[:, None]).astype(jnp.bfloat16)
    packed = jnp.concatenate([scaled, probes.astype(jnp.bfloat16)], axis=0)
    gathered = lax.all_gather(packed, AXES, axis=0, tiled=False)
    image, sums = pl.pallas_call(
        lambda *refs: image_kernel(features.shape[0], *refs),
        out_shape=(
            jax.ShapeDtypeStruct(probes.shape, jnp.float32),
            jax.ShapeDtypeStruct((3, probes.shape[0], 1), jnp.float32),
        ),
        in_specs=[pl.BlockSpec(memory_space=pltpu.VMEM)] * 4,
        out_specs=(pl.BlockSpec(memory_space=pltpu.VMEM),) * 2,
        compiler_params=pltpu.CompilerParams(vmem_limit_bytes=48 * 1024 * 1024),
    )(packed, noise_var[None, :], probes, gathered)
    sums = jnp.sum(lax.all_gather(sums.reshape(3, -1), AXES, axis=0, tiled=False), axis=0)
    start_norms, curvature, image_norms = sums[0], sums[1], sums[2]
    alpha = start_norms / curvature
    new_norms = start_norms - 2.0 * alpha * curvature + alpha * alpha * image_norms
    residual = probes - alpha[:, None] * image
    solution = alpha[:, None] * probes
    direction = residual + (new_norms / start_norms)[:, None] * probes
    return (solution, residual, direction)


def solution(mesh):
    spread = P(None, ("parts", "blk", "grp", "sub"))
    return jax.shard_map(
        local,
        mesh=mesh,
        in_specs=(spread, P("parts"), P(("parts", "blk", "grp", "sub")), spread),
        out_specs=(spread, spread, spread),
        check_vma=False,
    )
```

```python
import jax
import jax.numpy as jnp
from jax import lax
from jax.experimental import pallas as pl
from jax.experimental.pallas import tpu as pltpu
from jax.sharding import PartitionSpec as P

AXES = ("blk", "grp", "sub")
DIRECT = 16
VMEM = pltpu.CompilerParams(vmem_limit_bytes=40 * 1024 * 1024)
HALF = 8


def pack_kernel(features_ref, lengthscale_ref, probes_ref, packed_ref):
    feature_count, width = features_ref.shape
    scale = jnp.broadcast_to(lengthscale_ref[...], (feature_count, feature_count)).T
    scale = jnp.concatenate([scale] * (width // feature_count), axis=1)
    scaled = (features_ref[...].astype(jnp.float32) / scale).astype(jnp.bfloat16)
    packed_ref[:feature_count, :] = scaled
    rest = -0.5 * jnp.sum(jnp.square(scaled.astype(jnp.float32)), axis=0, keepdims=True)
    row = lax.broadcasted_iota(jnp.int32, (2 * HALF, width), 0)
    rows = jnp.where((row >= HALF) & (row < HALF + 3), 1.0, 0.0)
    for piece in range(3):
        part = rest.astype(jnp.bfloat16).astype(jnp.float32)
        rows = jnp.where(row == piece, part, rows)
        rest = rest - part
    packed_ref[feature_count : feature_count + 2 * HALF, :] = rows.astype(jnp.bfloat16)
    packed_ref[feature_count + 2 * HALF :, :] = probes_ref[...].astype(jnp.bfloat16)


def image_kernel(feature_count, block_count, own_too, *refs):
    packed_ref, noise_ref, probes_ref = refs[:3]
    block_refs = refs[3 : 3 + block_count]
    image_ref, sums_ref, packed, noise, probes, *rest = refs[3 + block_count :]
    slots, semaphores = rest[:-1], rest[-1]
    first = [
        pltpu.make_async_copy(source, target, semaphores.at[number])
        for number, (source, target) in enumerate(
            ((packed_ref, packed), (noise_ref, noise), (probes_ref, probes))
        )
    ]
    copies = [
        pltpu.make_async_copy(source, slot, semaphores.at[3 + number])
        for number, (source, slot) in enumerate(zip(block_refs, slots))
    ]
    for copy in first + copies:
        copy.start()
    depth = feature_count + 2 * HALF
    first[0].wait()
    norm_rows = packed[feature_count:depth, :].astype(jnp.float32)
    own = jnp.concatenate(
        [packed[:feature_count, :].astype(jnp.float32), norm_rows[HALF:], norm_rows[:HALF]], axis=0
    )
    own = own.T.astype(jnp.bfloat16)

    def add_block(block, total):
        exponent = jnp.dot(own, block[:depth, :], preferred_element_type=jnp.float32)
        weights = jnp.exp(exponent).astype(jnp.bfloat16)
        return total + lax.dot_general(
            weights,
            block[depth:, :],
            (((1,), (1,)), ((), ())),
            preferred_element_type=jnp.float32,
        )

    total = jnp.zeros((own.shape[0], probes.shape[0]), jnp.float32)
    if own_too:
        total = add_block(packed, total)
    for copy, slot in zip(copies, slots):
        copy.wait()
        if len(slot.shape) == 2:
            total = add_block(slot, total)
        else:
            total = lax.fori_loop(
                0, slot.shape[0], lambda number, value: add_block(slot.at[number], value), total
            )
    first[1].wait()
    first[2].wait()
    own_probes = probes[...]
    image = total.T + noise[...] * own_probes
    image_ref[...] = image
    lane = lax.broadcasted_iota(jnp.int32, sums_ref.shape, 1)
    sums = jnp.where(lane == 0, jnp.sum(own_probes * own_probes, axis=1, keepdims=True), 0.0)
    sums = jnp.where(lane == 1, jnp.sum(own_probes * image, axis=1, keepdims=True), sums)
    sums_ref[...] = jnp.where(lane == 2, jnp.sum(image * image, axis=1, keepdims=True), sums)


def finish_kernel(image_ref, probes_ref, *refs):
    *sums_refs, solution_ref, residual_ref, direction_ref = refs
    sums = jnp.zeros(sums_refs[0].shape[-2:], jnp.float32)
    for ref in sums_refs:
        value = ref[...]
        sums = sums + (value if value.ndim == 2 else jnp.sum(value, axis=0))
    start_norms, curvature, image_norms = sums[:, 0:1], sums[:, 1:2], sums[:, 2:3]
    alpha = start_norms / curvature
    new_norms = start_norms - 2.0 * alpha * curvature + alpha * alpha * image_norms
    probes = probes_ref[...]
    residual = probes - alpha * image_ref[...]
    solution_ref[...] = alpha * probes
    residual_ref[...] = residual
    direction_ref[...] = residual + (new_norms / start_norms) * probes


def others(value, count):
    if count > DIRECT:
        return [lax.all_gather(value, AXES, axis=0, tiled=False)], False
    return [
        lax.ppermute(value, AXES, [(i, (i + step) % count) for i in range(count)])
        for step in range(1, count)
    ], True


def make_local(count):
    def local(features, lengthscale, noise_var, probes):
        feature_count, width = features.shape
        packed = pl.pallas_call(
            pack_kernel,
            out_shape=jax.ShapeDtypeStruct(
                (feature_count + 2 * HALF + probes.shape[0], width), jnp.bfloat16
            ),
            compiler_params=VMEM,
        )(features, lengthscale[None, :], probes)
        blocks, direct = others(packed, count)
        image, sums = pl.pallas_call(
            lambda *refs: image_kernel(feature_count, len(blocks), direct, *refs),
            out_shape=(
                jax.ShapeDtypeStruct(probes.shape, jnp.float32),
                jax.ShapeDtypeStruct((probes.shape[0], 128), jnp.float32),
            ),
            in_specs=[pl.BlockSpec(memory_space=pl.ANY)] * (3 + len(blocks)),
            scratch_shapes=[
                pltpu.VMEM(packed.shape, packed.dtype),
                pltpu.VMEM((1, width), jnp.float32),
                pltpu.VMEM(probes.shape, jnp.float32),
                *[pltpu.VMEM(block.shape, block.dtype) for block in blocks],
                pltpu.SemaphoreType.DMA((3 + len(blocks),)),
            ],
            compiler_params=VMEM,
        )(packed, noise_var[None, :], probes, *blocks)
        more, direct = others(sums, count)
        outs = (jax.ShapeDtypeStruct(probes.shape, jnp.float32),) * 3
        return pl.pallas_call(finish_kernel, out_shape=outs, compiler_params=VMEM)(
            image, probes, *(([sums] if direct else []) + more)
        )

    return local


def solution(mesh):
    count = 1
    for axis in AXES:
        count *= mesh.shape[axis]
    spread = P(None, ("parts", "blk", "grp", "sub"))
    return jax.shard_map(
        make_local(count),
        mesh=mesh,
        in_specs=(spread, P("parts"), P(("parts", "blk", "grp", "sub")), spread),
        out_specs=(spread, spread, spread),
        check_vma=False,
    )
```

```python
import jax
import jax.numpy as jnp
from jax import lax
from jax.experimental import pallas as pl
from jax.experimental.pallas import tpu as pltpu
from jax.sharding import PartitionSpec as P

PLANE = ("grp", "sub")
LINE = ("blk",)
DIRECT = 8
VMEM = pltpu.CompilerParams(vmem_limit_bytes=40 * 1024 * 1024)
HALF = 8


def pieces_of(value):
    pieces = []
    for _ in range(3):
        piece = value.astype(jnp.bfloat16).astype(jnp.float32)
        pieces.append(piece)
        value = value - piece
    return pieces


def pack_kernel(features_hbm, lengthscale_hbm, probes_hbm, line_ref, plane_ref, *scratch):
    features_ref, lengthscale_ref, probes_ref, semaphores = scratch
    copies = [
        pltpu.make_async_copy(source, target, semaphores.at[number])
        for number, (source, target) in enumerate(
            (
                (features_hbm, features_ref),
                (lengthscale_hbm, lengthscale_ref),
                (probes_hbm, probes_ref),
            )
        )
    ]
    for copy in copies:
        copy.start()
    for copy in copies:
        copy.wait()
    feature_count, width = features_ref.shape
    scale = jnp.broadcast_to(lengthscale_ref[...], (feature_count, feature_count)).T
    scale = jnp.concatenate([scale] * (width // feature_count), axis=1)
    scaled = (features_ref[...].astype(jnp.float32) / scale).astype(jnp.bfloat16)
    norms = -0.5 * jnp.sum(jnp.square(scaled.astype(jnp.float32)), axis=0, keepdims=True)
    row = lax.broadcasted_iota(jnp.int32, (2 * HALF, width), 0)
    rows = jnp.where((row >= HALF) & (row < HALF + 3), 1.0, 0.0)
    for number, piece in enumerate(pieces_of(norms)):
        rows = jnp.where(row == number, piece, rows)
    probes = jnp.concatenate(pieces_of(probes_ref[...]), axis=0)
    packed = jnp.concatenate([scaled, rows.astype(jnp.bfloat16), probes.astype(jnp.bfloat16)], axis=0)
    plane_ref[...] = packed
    line_ref[...] = packed[: line_ref.shape[0], :]


def image_kernel(depth, plane_count, *refs):
    plane_refs = refs[:plane_count]
    line_refs = refs[plane_count:-2]
    noise_ref, partial_ref = refs[-2:]
    rows = [ref[:depth, :] for ref in plane_refs]
    probe_count = partial_ref.shape[1]

    def add_block(block_ref, totals):
        block = block_ref[:depth, :].astype(jnp.float32)
        first, last = depth - 2 * HALF, depth - HALF
        columns = jnp.concatenate([block[:first], block[last:], block[first:last]], axis=0)
        columns = columns.T.astype(jnp.bfloat16)
        probes = block_ref[depth : depth + probe_count, :]
        result = []
        for own, total in zip(rows, totals):
            exponent = jnp.dot(columns, own, preferred_element_type=jnp.float32)
            weights = jnp.exp(exponent).astype(jnp.bfloat16)
            result.append(total + jnp.dot(probes, weights, preferred_element_type=jnp.float32))
        return result

    own_probes = probes_of(plane_refs[0], depth, probe_count)
    totals = [noise_ref[...] * own_probes]
    totals += [jnp.zeros(own_probes.shape, jnp.float32)] * (plane_count - 1)
    for ref in line_refs:
        if len(ref.shape) == 2:
            totals = add_block(ref, totals)
        else:
            totals = lax.fori_loop(
                0, ref.shape[0], lambda number, value: add_block(ref.at[number], value), totals
            )
    for number, total in enumerate(totals):
        partial_ref[number] = total


def probes_of(ref, depth, probe_count):
    parts = [
        ref[depth + number * probe_count : depth + (number + 1) * probe_count, :].astype(jnp.float32)
        for number in range(3)
    ]
    return parts[0] + (parts[1] + parts[2])


def combine_kernel(depth, plane_count, *refs):
    plane_refs = refs[:plane_count]
    partial_refs = refs[plane_count:-2]
    image_ref, sums_ref = refs[-2:]
    probe_count = image_ref.shape[0]
    lane = lax.broadcasted_iota(jnp.int32, sums_ref.shape, 1)
    products = [0.0, 0.0, 0.0]
    for number, plane_ref in enumerate(plane_refs):
        probes = probes_of(plane_ref, depth, probe_count)
        image = sum(
            ref[place_of(step, number, plane_count)] for step, ref in enumerate(partial_refs)
        )
        if number == 0:
            image_ref[...] = image
        products[0] += probes * probes
        products[1] += probes * image
        products[2] += image * image
    sums = jnp.zeros(sums_ref.shape, jnp.float32)
    for number, product in enumerate(products):
        sums = jnp.where(lane == number, jnp.sum(product, axis=1, keepdims=True), sums)
    sums_ref[...] = sums


def finish_kernel(image_ref, probes_ref, *refs):
    *sums_refs, solution_ref, residual_ref, direction_ref = refs
    sums = jnp.zeros(sums_refs[0].shape[-2:], jnp.float32)
    for ref in sums_refs:
        value = ref[...]
        sums = sums + (value if value.ndim == 2 else jnp.sum(value, axis=0))
    start_norms, curvature, image_norms = sums[:, 0:1], sums[:, 1:2], sums[:, 2:3]
    alpha = start_norms / curvature
    new_norms = start_norms - 2.0 * alpha * curvature + alpha * alpha * image_norms
    probes = probes_ref[...]
    residual = probes - alpha * image_ref[...]
    solution_ref[...] = alpha * probes
    residual_ref[...] = residual
    direction_ref[...] = residual + (new_norms / start_norms) * probes


def paired(count):
    return count & (count - 1) == 0


def source_of(device, step, count):
    return device ^ step if paired(count) else (device - step) % count


def place_of(step, number, count):
    return step ^ number if paired(count) else (number - step) % count


def everywhere(value, axes, count):
    if count > DIRECT:
        return [lax.all_gather(value, axes, axis=0, tiled=False)]
    return [value] + [
        lax.ppermute(value, axes, [(source_of(i, step, count), i) for i in range(count)])
        for step in range(1, count)
    ]


def make_local(plane_count, line_count):
    def local(features, lengthscale, noise_var, probes):
        feature_count, width = features.shape
        probe_count = probes.shape[0]
        depth = feature_count + 2 * HALF
        line, plane = pl.pallas_call(
            pack_kernel,
            out_shape=(
                jax.ShapeDtypeStruct((depth + probe_count, width), jnp.bfloat16),
                jax.ShapeDtypeStruct((depth + 3 * probe_count, width), jnp.bfloat16),
            ),
            in_specs=[pl.BlockSpec(memory_space=pl.ANY)] * 3,
            scratch_shapes=[
                pltpu.VMEM(features.shape, features.dtype),
                pltpu.VMEM((1, feature_count), jnp.float32),
                pltpu.VMEM(probes.shape, jnp.float32),
                pltpu.SemaphoreType.DMA((3,)),
            ],
            compiler_params=VMEM,
        )(features, lengthscale[None, :], probes)
        lines = everywhere(line, LINE, line_count)
        planes = everywhere(plane, PLANE, plane_count)
        partial = pl.pallas_call(
            lambda *refs: image_kernel(depth, plane_count, *refs),
            out_shape=jax.ShapeDtypeStruct((plane_count, probe_count, width), jnp.float32),
            compiler_params=VMEM,
        )(*planes, *lines, noise_var[None, :])
        image, sums = pl.pallas_call(
            lambda *refs: combine_kernel(depth, plane_count, *refs),
            out_shape=(
                jax.ShapeDtypeStruct(probes.shape, jnp.float32),
                jax.ShapeDtypeStruct((probe_count, 128), jnp.float32),
            ),
            compiler_params=VMEM,
        )(*planes, *everywhere(partial, PLANE, plane_count))
        outs = (jax.ShapeDtypeStruct(probes.shape, jnp.float32),) * 3
        return pl.pallas_call(finish_kernel, out_shape=outs, compiler_params=VMEM)(
            image, probes, *everywhere(sums, LINE, line_count)
        )

    return local


def solution(mesh):
    plane_count = mesh.shape["grp"] * mesh.shape["sub"]
    spread = P(None, ("parts", "blk", "grp", "sub"))
    return jax.shard_map(
        make_local(plane_count, mesh.shape["blk"]),
        mesh=mesh,
        in_specs=(spread, P("parts"), P(("parts", "blk", "grp", "sub")), spread),
        out_specs=(spread, spread, spread),
        check_vma=False,
    )
```

```python
import jax
import jax.numpy as jnp
from jax import lax
from jax.experimental import pallas as pl
from jax.experimental.pallas import tpu as pltpu
from jax.sharding import PartitionSpec as P

PLANE = ("grp", "sub")
LINE = ("blk",)
DIRECT = 8
VMEM = pltpu.CompilerParams(vmem_limit_bytes=40 * 1024 * 1024)
HALF = 8


def pieces_of(value):
    pieces = []
    for _ in range(3):
        piece = value.astype(jnp.bfloat16).astype(jnp.float32)
        pieces.append(piece)
        value = value - piece
    return pieces


def pack_kernel(features_hbm, lengthscale_hbm, probes_hbm, line_ref, plane_ref, *scratch):
    features_ref, lengthscale_ref, probes_ref, semaphores = scratch
    copies = [
        pltpu.make_async_copy(source, target, semaphores.at[number])
        for number, (source, target) in enumerate(
            (
                (features_hbm, features_ref),
                (lengthscale_hbm, lengthscale_ref),
                (probes_hbm, probes_ref),
            )
        )
    ]
    for copy in copies:
        copy.start()
    for copy in copies:
        copy.wait()
    feature_count, width = features_ref.shape
    scale = jnp.broadcast_to(lengthscale_ref[...], (feature_count, feature_count)).T
    scale = jnp.concatenate([scale] * (width // feature_count), axis=1)
    scaled = (features_ref[...].astype(jnp.float32) / scale).astype(jnp.bfloat16)
    norms = -0.5 * jnp.sum(jnp.square(scaled.astype(jnp.float32)), axis=0, keepdims=True)
    row = lax.broadcasted_iota(jnp.int32, (2 * HALF, width), 0)
    rows = jnp.where((row >= HALF) & (row < HALF + 3), 1.0, 0.0)
    for number, piece in enumerate(pieces_of(norms)):
        rows = jnp.where(row == number, piece, rows)
    probes = jnp.concatenate(pieces_of(probes_ref[...]), axis=0)
    packed = jnp.concatenate([scaled, rows.astype(jnp.bfloat16), probes.astype(jnp.bfloat16)], axis=0)
    plane_ref[...] = packed
    line_ref[...] = packed[: line_ref.shape[0], :]


def image_kernel(depth, plane_count, *refs):
    plane_refs = refs[:plane_count]
    line_refs = refs[plane_count:-2]
    noise_ref, partial_ref = refs[-2:]
    rows = [ref[:depth, :] for ref in plane_refs]
    probe_count = partial_ref.shape[1]

    def add_block(block_ref, totals):
        block = block_ref[:depth, :].astype(jnp.float32)
        first, last = depth - 2 * HALF, depth - HALF
        columns = jnp.concatenate([block[:first], block[last:], block[first:last]], axis=0)
        columns = columns.T.astype(jnp.bfloat16)
        probes = block_ref[depth : depth + probe_count, :]
        result = []
        for own, total in zip(rows, totals):
            exponent = jnp.dot(columns, own, preferred_element_type=jnp.float32)
            weights = jnp.exp(exponent).astype(jnp.bfloat16)
            result.append(total + jnp.dot(probes, weights, preferred_element_type=jnp.float32))
        return result

    own_probes = probes_of(plane_refs[0], depth, probe_count)
    totals = [noise_ref[...] * own_probes]
    totals += [jnp.zeros(own_probes.shape, jnp.float32)] * (plane_count - 1)
    for ref in line_refs:
        if len(ref.shape) == 2:
            totals = add_block(ref, totals)
        else:
            totals = lax.fori_loop(
                0, ref.shape[0], lambda number, value: add_block(ref.at[number], value), totals
            )
    for number, total in enumerate(totals):
        partial_ref[number] = total


def probes_of(ref, depth, probe_count):
    parts = [
        ref[depth + number * probe_count : depth + (number + 1) * probe_count, :].astype(jnp.float32)
        for number in range(3)
    ]
    return parts[0] + (parts[1] + parts[2])


def combine_kernel(depth, plane_count, *refs):
    plane_refs = refs[:plane_count]
    partial_refs = refs[plane_count:-2]
    image_ref, sums_ref = refs[-2:]
    probe_count = image_ref.shape[0]
    lane = lax.broadcasted_iota(jnp.int32, sums_ref.shape, 1)
    products = [0.0, 0.0, 0.0]
    for number, plane_ref in enumerate(plane_refs):
        probes = probes_of(plane_ref, depth, probe_count)
        image = sum(
            ref[place_of(step, number, plane_count)] for step, ref in enumerate(partial_refs)
        )
        if number == 0:
            image_ref[...] = image
        products[0] += probes * probes
        products[1] += probes * image
        products[2] += image * image
    sums = jnp.zeros(sums_ref.shape, jnp.float32)
    for number, product in enumerate(products):
        sums = jnp.where(lane == number, jnp.sum(product, axis=1, keepdims=True), sums)
    sums_ref[...] = sums


def finish_kernel(image_ref, probes_ref, *refs):
    *sums_refs, solution_ref, residual_ref, direction_ref = refs
    sums = jnp.zeros(sums_refs[0].shape[-2:], jnp.float32)
    for ref in sums_refs:
        value = ref[...]
        sums = sums + (value if value.ndim == 2 else jnp.sum(value, axis=0))
    start_norms, curvature, image_norms = sums[:, 0:1], sums[:, 1:2], sums[:, 2:3]
    alpha = start_norms / curvature
    new_norms = start_norms - 2.0 * alpha * curvature + alpha * alpha * image_norms
    probes = probes_ref[...]
    residual = probes - alpha * image_ref[...]
    solution_ref[...] = alpha * probes
    residual_ref[...] = residual
    direction_ref[...] = residual + (new_norms / start_norms) * probes


def paired(count):
    return count & (count - 1) == 0


def source_of(device, step, count):
    return device ^ step if paired(count) else (device - step) % count


def place_of(step, number, count):
    return step ^ number if paired(count) else (number - step) % count


def everywhere(value, axes, count):
    if count > DIRECT:
        return [lax.all_gather(value, axes, axis=0, tiled=False)]
    return [value] + [
        lax.ppermute(value, axes, [(source_of(i, step, count), i) for i in range(count)])
        for step in range(1, count)
    ]


def make_local(plane_count, line_count):
    def local(features, lengthscale, noise_var, probes):
        feature_count, width = features.shape
        probe_count = probes.shape[0]
        depth = feature_count + 2 * HALF
        line, plane = pl.pallas_call(
            pack_kernel,
            out_shape=(
                jax.ShapeDtypeStruct((depth + probe_count, width), jnp.bfloat16),
                jax.ShapeDtypeStruct((depth + 3 * probe_count, width), jnp.bfloat16),
            ),
            in_specs=[pl.BlockSpec(memory_space=pltpu.HBM)] * 3,
            scratch_shapes=[
                pltpu.VMEM(features.shape, features.dtype),
                pltpu.VMEM((1, feature_count), jnp.float32),
                pltpu.VMEM(probes.shape, jnp.float32),
                pltpu.SemaphoreType.DMA((3,)),
            ],
            compiler_params=VMEM,
        )(features, lengthscale[None, :], probes)
        lines = everywhere(line, LINE, line_count)
        planes = everywhere(plane, PLANE, plane_count)
        partial = pl.pallas_call(
            lambda *refs: image_kernel(depth, plane_count, *refs),
            out_shape=jax.ShapeDtypeStruct((plane_count, probe_count, width), jnp.float32),
            compiler_params=VMEM,
        )(*planes, *lines, noise_var[None, :])
        image, sums = pl.pallas_call(
            lambda *refs: combine_kernel(depth, plane_count, *refs),
            out_shape=(
                jax.ShapeDtypeStruct(probes.shape, jnp.float32),
                jax.ShapeDtypeStruct((probe_count, 128), jnp.float32),
            ),
            compiler_params=VMEM,
        )(*planes, *everywhere(partial, PLANE, plane_count))
        outs = (jax.ShapeDtypeStruct(probes.shape, jnp.float32),) * 3
        return pl.pallas_call(finish_kernel, out_shape=outs, compiler_params=VMEM)(
            image,
            probes,
            lax.all_to_all(
                jnp.broadcast_to(sums, (line_count, *sums.shape)), LINE, split_axis=0, concat_axis=0
            ),
        )

    return local


def solution(mesh):
    plane_count = mesh.shape["grp"] * mesh.shape["sub"]
    spread = P(None, ("parts", "blk", "grp", "sub"))
    return jax.shard_map(
        make_local(plane_count, mesh.shape["blk"]),
        mesh=mesh,
        in_specs=(spread, P("parts"), P(("parts", "blk", "grp", "sub")), spread),
        out_specs=(spread, spread, spread),
        check_vma=False,
    )
```

```python
import jax
import jax.numpy as jnp
from jax import lax
from jax.experimental import pallas as pl
from jax.experimental.pallas import tpu as pltpu
from jax.sharding import PartitionSpec as P

PLANE = ("grp", "sub")
LINE = ("blk",)
DIRECT = 8
VMEM = pltpu.CompilerParams(vmem_limit_bytes=40 * 1024 * 1024)
HALF = 8


def pieces_of(value):
    pieces = []
    for _ in range(3):
        piece = value.astype(jnp.bfloat16).astype(jnp.float32)
        pieces.append(piece)
        value = value - piece
    return pieces


def norm_rows(scaled, place):
    norms = -0.5 * jnp.sum(jnp.square(scaled.astype(jnp.float32)), axis=0, keepdims=True)
    row = lax.broadcasted_iota(jnp.int32, (2 * HALF, scaled.shape[1]), 0)
    here, there = place * HALF, (1 - place) * HALF
    rows = jnp.where((row >= there) & (row < there + 3), 1.0, 0.0)
    for number, piece in enumerate(pieces_of(norms)):
        rows = jnp.where(row == here + number, piece, rows)
    return rows.astype(jnp.bfloat16)


def pack_kernel(scaled_ref, probes_ref, line_ref, plane_ref):
    scaled = scaled_ref[...]
    rows = norm_rows(scaled, 0)
    high, low, _ = pieces_of(probes_ref[...])
    high, low = high.astype(jnp.bfloat16), low.astype(jnp.bfloat16)
    line_ref[...] = jnp.concatenate([scaled, rows.astype(jnp.bfloat16), high], axis=0)
    plane_ref[...] = jnp.concatenate([scaled, high, low], axis=0)


def image_kernel(feature_count, plane_count, *refs):
    plane_refs = refs[:plane_count]
    line_refs = refs[plane_count:-3]
    noise_ref, probes_ref, partial_ref = refs[-3:]
    depth = feature_count + 2 * HALF
    rows = []
    for ref in plane_refs:
        scaled = ref[:feature_count, :]
        rows.append(jnp.concatenate([scaled, norm_rows(scaled, 1)], axis=0))

    def add_block(block_ref, totals):
        columns = block_ref[:depth, :].astype(jnp.float32).T.astype(jnp.bfloat16)
        probes = block_ref[depth:, :]
        result = []
        for own, total in zip(rows, totals):
            exponent = jnp.dot(columns, own, preferred_element_type=jnp.float32)
            weights = jnp.exp(exponent).astype(jnp.bfloat16)
            result.append(total + jnp.dot(probes, weights, preferred_element_type=jnp.float32))
        return result

    totals = [noise_ref[...] * probes_ref[...]]
    totals += [jnp.zeros(probes_ref.shape, jnp.float32)] * (plane_count - 1)
    for ref in line_refs:
        if len(ref.shape) == 2:
            totals = add_block(ref, totals)
        else:
            totals = lax.fori_loop(
                0, ref.shape[0], lambda number, value: add_block(ref.at[number], value), totals
            )
    for number, total in enumerate(totals):
        partial_ref[number] = total


def combine_kernel(feature_count, plane_count, *refs):
    plane_refs = refs[:plane_count]
    probes_ref = refs[plane_count]
    partial_refs = refs[plane_count + 1 : -2]
    image_ref, sums_ref = refs[-2:]
    probe_count = image_ref.shape[0]
    lane = lax.broadcasted_iota(jnp.int32, sums_ref.shape, 1)
    products = [0.0, 0.0, 0.0]
    for number, plane_ref in enumerate(plane_refs):
        image = sum(
            ref[place_of(step, number, plane_count)] for step, ref in enumerate(partial_refs)
        )
        if number == 0:
            image_ref[...] = image
            probes = probes_ref[...]
        else:
            middle = feature_count + probe_count
            probes = plane_ref[feature_count:middle, :].astype(jnp.float32)
            probes = probes + plane_ref[middle:, :].astype(jnp.float32)
        products[0] += probes * probes
        products[1] += probes * image
        products[2] += image * image
    sums = jnp.zeros(sums_ref.shape, jnp.float32)
    for number, product in enumerate(products):
        sums = jnp.where(lane == number, jnp.sum(product, axis=1, keepdims=True), sums)
    sums_ref[...] = sums


def finish_kernel(image_ref, probes_ref, *refs):
    *sums_refs, solution_ref, residual_ref, direction_ref = refs
    sums = jnp.zeros(sums_refs[0].shape[-2:], jnp.float32)
    for ref in sums_refs:
        value = ref[...]
        sums = sums + (value if value.ndim == 2 else jnp.sum(value, axis=0))
    start_norms, curvature, image_norms = sums[:, 0:1], sums[:, 1:2], sums[:, 2:3]
    alpha = start_norms / curvature
    new_norms = start_norms - 2.0 * alpha * curvature + alpha * alpha * image_norms
    probes = probes_ref[...]
    residual = probes - alpha * image_ref[...]
    solution_ref[...] = alpha * probes
    residual_ref[...] = residual
    direction_ref[...] = residual + (new_norms / start_norms) * probes


def paired(count):
    return count & (count - 1) == 0


def source_of(device, step, count):
    return device ^ step if paired(count) else (device - step) % count


def place_of(step, number, count):
    return step ^ number if paired(count) else (number - step) % count


def everywhere(value, axes, count):
    if count > DIRECT:
        return [lax.all_gather(value, axes, axis=0, tiled=False)]
    return [value] + [
        lax.ppermute(value, axes, [(source_of(i, step, count), i) for i in range(count)])
        for step in range(1, count)
    ]


def plane_blocks(value, shape):
    grp_count, sub_count = shape
    if sub_count != 2 or not paired(grp_count):
        return everywhere(value, PLANE, grp_count * sub_count)
    blocks = everywhere(value, ("sub",), sub_count)
    moved = [everywhere(block, ("grp",), grp_count) for block in blocks]
    return [moved[sub][grp] for grp in range(grp_count) for sub in range(sub_count)]


def make_local(plane_shape, line_count):
    plane_count = plane_shape[0] * plane_shape[1]

    def local(features, lengthscale, noise_var, probes):
        feature_count, width = features.shape
        probe_count = probes.shape[0]
        scaled = (features.astype(jnp.float32) / lengthscale[:, None]).astype(jnp.bfloat16)
        line, plane = pl.pallas_call(
            pack_kernel,
            out_shape=(
                jax.ShapeDtypeStruct((feature_count + 2 * HALF + probe_count, width), jnp.bfloat16),
                jax.ShapeDtypeStruct((feature_count + 2 * probe_count, width), jnp.bfloat16),
            ),
            compiler_params=VMEM,
        )(scaled, probes)
        lines = everywhere(line, LINE, line_count)
        planes = plane_blocks(plane, plane_shape)
        partial = pl.pallas_call(
            lambda *refs: image_kernel(feature_count, plane_count, *refs),
            out_shape=jax.ShapeDtypeStruct((plane_count, probe_count, width), jnp.float32),
            compiler_params=VMEM,
        )(*planes, *lines, noise_var[None, :], probes)
        image, sums = pl.pallas_call(
            lambda *refs: combine_kernel(feature_count, plane_count, *refs),
            out_shape=(
                jax.ShapeDtypeStruct(probes.shape, jnp.float32),
                jax.ShapeDtypeStruct((probe_count, 128), jnp.float32),
            ),
            compiler_params=VMEM,
        )(*planes, probes, *everywhere(partial, PLANE, plane_count))
        outs = (jax.ShapeDtypeStruct(probes.shape, jnp.float32),) * 3
        return pl.pallas_call(finish_kernel, out_shape=outs, compiler_params=VMEM)(
            image, probes, *everywhere(sums, LINE, line_count)
        )

    return local


def solution(mesh):
    plane_shape = (mesh.shape["grp"], mesh.shape["sub"])
    spread = P(None, ("parts", "blk", "grp", "sub"))
    return jax.shard_map(
        make_local(plane_shape, mesh.shape["blk"]),
        mesh=mesh,
        in_specs=(spread, P("parts"), P(("parts", "blk", "grp", "sub")), spread),
        out_specs=(spread, spread, spread),
        check_vma=False,
    )
```

```python
import jax
import jax.numpy as jnp
from jax import lax
from jax.experimental import pallas as pl
from jax.experimental.pallas import tpu as pltpu
from jax.sharding import PartitionSpec as P

PLANE = ("grp", "sub")
LINE = ("blk",)
DIRECT = 8
VMEM = pltpu.CompilerParams(vmem_limit_bytes=40 * 1024 * 1024)
HALF = 8


def pieces_of(value):
    pieces = []
    for _ in range(3):
        piece = value.astype(jnp.bfloat16).astype(jnp.float32)
        pieces.append(piece)
        value = value - piece
    return pieces


def norm_rows(scaled, place):
    norms = -0.5 * jnp.sum(jnp.square(scaled.astype(jnp.float32)), axis=0, keepdims=True)
    row = lax.broadcasted_iota(jnp.int32, (2 * HALF, scaled.shape[1]), 0)
    here, there = place * HALF, (1 - place) * HALF
    rows = jnp.where((row >= there) & (row < there + 3), 1.0, 0.0)
    for number, piece in enumerate(pieces_of(norms)):
        rows = jnp.where(row == here + number, piece, rows)
    return rows.astype(jnp.bfloat16)


def pack_kernel(scaled_ref, probes_ref, line_ref):
    line_ref[...] = jnp.concatenate(
        [scaled_ref[...], probes_ref[...].astype(jnp.bfloat16)], axis=0
    )


def image_kernel(feature_count, plane_count, *refs):
    plane_refs = refs[:plane_count]
    line_refs = refs[plane_count:-3]
    noise_ref, probes_ref, partial_ref = refs[-3:]
    rows = [jnp.concatenate([ref[...], norm_rows(ref[...], 1)], axis=0) for ref in plane_refs]

    def add_block(block_ref, totals):
        scaled = block_ref[:feature_count, :]
        columns = jnp.concatenate([scaled, norm_rows(scaled, 0)], axis=0)
        columns = columns.astype(jnp.float32).T.astype(jnp.bfloat16)
        probes = block_ref[feature_count:, :]
        result = []
        for own, total in zip(rows, totals):
            exponent = jnp.dot(columns, own, preferred_element_type=jnp.float32)
            weights = jnp.exp(exponent).astype(jnp.bfloat16)
            result.append(total + jnp.dot(probes, weights, preferred_element_type=jnp.float32))
        return result

    totals = [noise_ref[...] * probes_ref[...]]
    totals += [jnp.zeros(probes_ref.shape, jnp.float32)] * (plane_count - 1)
    for ref in line_refs:
        if len(ref.shape) == 2:
            totals = add_block(ref, totals)
        else:
            totals = lax.fori_loop(
                0, ref.shape[0], lambda number, value: add_block(ref.at[number], value), totals
            )
    for number, total in enumerate(totals):
        partial_ref[number] = total
    partial_ref[plane_count] = probes_ref[...]


def combine_kernel(plane_count, *refs):
    partial_refs = refs[:-2]
    image_ref, sums_ref = refs[-2:]
    lane = lax.broadcasted_iota(jnp.int32, sums_ref.shape, 1)
    products = [0.0, 0.0, 0.0]
    for number, own_ref in enumerate(partial_refs):
        image = sum(
            ref[place_of(step, number, plane_count)] for step, ref in enumerate(partial_refs)
        )
        if number == 0:
            image_ref[...] = image
        probes = own_ref[plane_count]
        products[0] += probes * probes
        products[1] += probes * image
        products[2] += image * image
    sums = jnp.zeros(sums_ref.shape, jnp.float32)
    for number, product in enumerate(products):
        sums = jnp.where(lane == number, jnp.sum(product, axis=1, keepdims=True), sums)
    sums_ref[...] = sums


def finish_kernel(image_ref, probes_ref, *refs):
    *sums_refs, solution_ref, residual_ref, direction_ref = refs
    sums = jnp.zeros(sums_refs[0].shape[-2:], jnp.float32)
    for ref in sums_refs:
        value = ref[...]
        sums = sums + (value if value.ndim == 2 else jnp.sum(value, axis=0))
    start_norms, curvature, image_norms = sums[:, 0:1], sums[:, 1:2], sums[:, 2:3]
    alpha = start_norms / curvature
    new_norms = start_norms - 2.0 * alpha * curvature + alpha * alpha * image_norms
    probes = probes_ref[...]
    residual = probes - alpha * image_ref[...]
    solution_ref[...] = alpha * probes
    residual_ref[...] = residual
    direction_ref[...] = residual + (new_norms / start_norms) * probes


def paired(count):
    return count & (count - 1) == 0


def source_of(device, step, count):
    return device ^ step if paired(count) else (device - step) % count


def place_of(step, number, count):
    return step ^ number if paired(count) else (number - step) % count


def everywhere(value, axes, count):
    if count > DIRECT:
        return [lax.all_gather(value, axes, axis=0, tiled=False)]
    return [value] + [
        lax.ppermute(value, axes, [(source_of(i, step, count), i) for i in range(count)])
        for step in range(1, count)
    ]


def plane_blocks(value, shape):
    grp_count, sub_count = shape
    if sub_count != 2 or not paired(grp_count):
        return everywhere(value, PLANE, grp_count * sub_count)
    blocks = everywhere(value, ("sub",), sub_count)
    moved = [everywhere(block, ("grp",), grp_count) for block in blocks]
    return [moved[sub][grp] for grp in range(grp_count) for sub in range(sub_count)]


def make_local(plane_shape, line_count):
    plane_count = plane_shape[0] * plane_shape[1]

    def local(features, lengthscale, noise_var, probes):
        feature_count, width = features.shape
        probe_count = probes.shape[0]
        scaled = (features.astype(jnp.float32) / lengthscale[:, None]).astype(jnp.bfloat16)
        line = pl.pallas_call(
            pack_kernel,
            out_shape=jax.ShapeDtypeStruct((feature_count + probe_count, width), jnp.bfloat16),
            compiler_params=VMEM,
        )(scaled, probes)
        lines = everywhere(line, LINE, line_count)
        planes = plane_blocks(scaled, plane_shape)
        partial = pl.pallas_call(
            lambda *refs: image_kernel(feature_count, plane_count, *refs),
            out_shape=jax.ShapeDtypeStruct((plane_count + 1, probe_count, width), jnp.float32),
            compiler_params=VMEM,
        )(*planes, *lines, noise_var[None, :], probes)
        image, sums = pl.pallas_call(
            lambda *refs: combine_kernel(plane_count, *refs),
            out_shape=(
                jax.ShapeDtypeStruct(probes.shape, jnp.float32),
                jax.ShapeDtypeStruct((probe_count, 128), jnp.float32),
            ),
            compiler_params=VMEM,
        )(*everywhere(partial, PLANE, plane_count))
        outs = (jax.ShapeDtypeStruct(probes.shape, jnp.float32),) * 3
        return pl.pallas_call(finish_kernel, out_shape=outs, compiler_params=VMEM)(
            image, probes, *everywhere(sums, LINE, line_count)
        )

    return local


def solution(mesh):
    plane_shape = (mesh.shape["grp"], mesh.shape["sub"])
    spread = P(None, ("parts", "blk", "grp", "sub"))
    return jax.shard_map(
        make_local(plane_shape, mesh.shape["blk"]),
        mesh=mesh,
        in_specs=(spread, P("parts"), P(("parts", "blk", "grp", "sub")), spread),
        out_specs=(spread, spread, spread),
        check_vma=False,
    )
```

```python
import jax
import jax.numpy as jnp
from jax import lax
from jax.experimental import pallas as pl
from jax.experimental.pallas import tpu as pltpu
from jax.sharding import PartitionSpec as P

PLANE = ("grp", "sub")
LINE = ("blk",)
DIRECT = 8
VMEM = pltpu.CompilerParams(vmem_limit_bytes=40 * 1024 * 1024)
HALF = 8


def pieces_of(value):
    pieces = []
    for _ in range(3):
        piece = value.astype(jnp.bfloat16).astype(jnp.float32)
        pieces.append(piece)
        value = value - piece
    return pieces


def norm_rows(scaled, place):
    norms = -0.5 * jnp.sum(jnp.square(scaled.astype(jnp.float32)), axis=0, keepdims=True)
    row = lax.broadcasted_iota(jnp.int32, (2 * HALF, scaled.shape[1]), 0)
    here, there = place * HALF, (1 - place) * HALF
    rows = jnp.where((row >= there) & (row < there + 3), 1.0, 0.0)
    for number, piece in enumerate(pieces_of(norms)):
        rows = jnp.where(row == here + number, piece, rows)
    return rows.astype(jnp.bfloat16)


def pack_kernel(scaled_ref, probes_ref, line_ref):
    line_ref[...] = jnp.concatenate(
        [scaled_ref[...], probes_ref[...].astype(jnp.bfloat16)], axis=0
    )


def image_kernel(feature_count, plane_count, *refs):
    plane_refs = refs[:plane_count]
    line_refs = refs[plane_count:-3]
    noise_ref, probes_ref, partial_ref = refs[-3:]
    rows = [jnp.concatenate([ref[...], norm_rows(ref[...], 1)], axis=0) for ref in plane_refs]

    def add_blocks(blocks, totals):
        columns = []
        for block in blocks:
            scaled = block[:feature_count, :]
            block_columns = jnp.concatenate([scaled, norm_rows(scaled, 0)], axis=0)
            columns.append(block_columns.astype(jnp.float32).T.astype(jnp.bfloat16))
        columns = jnp.concatenate(columns, axis=0)
        probes = jnp.concatenate([block[feature_count:, :] for block in blocks], axis=1)
        result = []
        for own, total in zip(rows, totals):
            exponent = jnp.dot(columns, own, preferred_element_type=jnp.float32)
            weights = jnp.exp(exponent).astype(jnp.bfloat16)
            result.append(total + jnp.dot(probes, weights, preferred_element_type=jnp.float32))
        return result

    totals = [noise_ref[...] * probes_ref[...]]
    totals += [jnp.zeros(probes_ref.shape, jnp.float32)] * (plane_count - 1)
    if len(line_refs[0].shape) == 2:
        totals = add_blocks([ref[...] for ref in line_refs], totals)
    else:
        totals = lax.fori_loop(
            0,
            line_refs[0].shape[0],
            lambda number, value: add_blocks([line_refs[0][number]], value),
            totals,
        )
    for number, total in enumerate(totals):
        partial_ref[number] = total
    partial_ref[plane_count] = probes_ref[...]


def combine_kernel(plane_count, *refs):
    partial_refs = refs[:-2]
    image_ref, sums_ref = refs[-2:]
    lane = lax.broadcasted_iota(jnp.int32, sums_ref.shape, 1)
    products = [0.0, 0.0, 0.0]
    for number, own_ref in enumerate(partial_refs):
        image = sum(
            ref[place_of(step, number, plane_count)] for step, ref in enumerate(partial_refs)
        )
        if number == 0:
            image_ref[...] = image
        probes = own_ref[plane_count]
        products[0] += probes * probes
        products[1] += probes * image
        products[2] += image * image
    sums = jnp.zeros(sums_ref.shape, jnp.float32)
    for number, product in enumerate(products):
        sums = jnp.where(lane == number, jnp.sum(product, axis=1, keepdims=True), sums)
    sums_ref[...] = sums


def finish_kernel(image_ref, probes_ref, *refs):
    *sums_refs, solution_ref, residual_ref, direction_ref = refs
    sums = jnp.zeros(sums_refs[0].shape[-2:], jnp.float32)
    for ref in sums_refs:
        value = ref[...]
        sums = sums + (value if value.ndim == 2 else jnp.sum(value, axis=0))
    start_norms, curvature, image_norms = sums[:, 0:1], sums[:, 1:2], sums[:, 2:3]
    alpha = start_norms / curvature
    new_norms = start_norms - 2.0 * alpha * curvature + alpha * alpha * image_norms
    probes = probes_ref[...]
    residual = probes - alpha * image_ref[...]
    solution_ref[...] = alpha * probes
    residual_ref[...] = residual
    direction_ref[...] = residual + (new_norms / start_norms) * probes


def paired(count):
    return count & (count - 1) == 0


def source_of(device, step, count):
    return device ^ step if paired(count) else (device - step) % count


def place_of(step, number, count):
    return step ^ number if paired(count) else (number - step) % count


def everywhere(value, axes, count):
    if count > DIRECT:
        return [lax.all_gather(value, axes, axis=0, tiled=False)]
    return [value] + [
        lax.ppermute(value, axes, [(source_of(i, step, count), i) for i in range(count)])
        for step in range(1, count)
    ]


def plane_blocks(value, shape):
    grp_count, sub_count = shape
    if sub_count != 2 or not paired(grp_count):
        return everywhere(value, PLANE, grp_count * sub_count)
    blocks = everywhere(value, ("sub",), sub_count)
    moved = [everywhere(block, ("grp",), grp_count) for block in blocks]
    return [moved[sub][grp] for grp in range(grp_count) for sub in range(sub_count)]


def make_local(plane_shape, line_count):
    plane_count = plane_shape[0] * plane_shape[1]

    def local(features, lengthscale, noise_var, probes):
        feature_count, width = features.shape
        probe_count = probes.shape[0]
        scaled = (features.astype(jnp.float32) / lengthscale[:, None]).astype(jnp.bfloat16)
        line = pl.pallas_call(
            pack_kernel,
            out_shape=jax.ShapeDtypeStruct((feature_count + probe_count, width), jnp.bfloat16),
            compiler_params=VMEM,
        )(scaled, probes)
        lines = everywhere(line, LINE, line_count)
        planes = plane_blocks(scaled, plane_shape)
        partial = pl.pallas_call(
            lambda *refs: image_kernel(feature_count, plane_count, *refs),
            out_shape=jax.ShapeDtypeStruct((plane_count + 1, probe_count, width), jnp.float32),
            compiler_params=VMEM,
        )(*planes, *lines, noise_var[None, :], probes)
        image, sums = pl.pallas_call(
            lambda *refs: combine_kernel(plane_count, *refs),
            out_shape=(
                jax.ShapeDtypeStruct(probes.shape, jnp.float32),
                jax.ShapeDtypeStruct((probe_count, 128), jnp.float32),
            ),
            compiler_params=VMEM,
        )(*everywhere(partial, PLANE, plane_count))
        outs = (jax.ShapeDtypeStruct(probes.shape, jnp.float32),) * 3
        return pl.pallas_call(finish_kernel, out_shape=outs, compiler_params=VMEM)(
            image, probes, *everywhere(sums, LINE, line_count)
        )

    return local


def solution(mesh):
    plane_shape = (mesh.shape["grp"], mesh.shape["sub"])
    spread = P(None, ("parts", "blk", "grp", "sub"))
    return jax.shard_map(
        make_local(plane_shape, mesh.shape["blk"]),
        mesh=mesh,
        in_specs=(spread, P("parts"), P(("parts", "blk", "grp", "sub")), spread),
        out_specs=(spread, spread, spread),
        check_vma=False,
    )
```

```python
import jax
import jax.numpy as jnp
from jax import lax
from jax.experimental import pallas as pl
from jax.experimental.pallas import tpu as pltpu
from jax.sharding import PartitionSpec as P

PLANE = ("grp", "sub")
LINE = ("blk",)
DIRECT = 8
VMEM = pltpu.CompilerParams(vmem_limit_bytes=40 * 1024 * 1024)
HALF = 8


def pieces_of(value):
    pieces = []
    for _ in range(3):
        piece = value.astype(jnp.bfloat16).astype(jnp.float32)
        pieces.append(piece)
        value = value - piece
    return pieces


def norm_rows(scaled, place):
    norms = -0.5 * jnp.sum(jnp.square(scaled.astype(jnp.float32)), axis=0, keepdims=True)
    row = lax.broadcasted_iota(jnp.int32, (2 * HALF, scaled.shape[1]), 0)
    here, there = place * HALF, (1 - place) * HALF
    rows = jnp.where((row >= there) & (row < there + 3), 1.0, 0.0)
    for number, piece in enumerate(pieces_of(norms)):
        rows = jnp.where(row == here + number, piece, rows)
    return rows.astype(jnp.bfloat16)


def pack_kernel(scaled_ref, probes_ref, line_ref):
    line_ref[...] = jnp.concatenate(
        [scaled_ref[...], probes_ref[...].astype(jnp.bfloat16)], axis=0
    )


def image_kernel(feature_count, plane_count, first, *refs):
    plane_refs = refs[:plane_count]
    line_refs = refs[plane_count:-3]
    start_ref, probes_ref, partial_ref = refs[-3:]
    rows = [jnp.concatenate([ref[...], norm_rows(ref[...], 1)], axis=0) for ref in plane_refs]

    def add_blocks(blocks, totals):
        columns = []
        for block in blocks:
            scaled = block[:feature_count, :]
            block_columns = jnp.concatenate([scaled, norm_rows(scaled, 0)], axis=0)
            columns.append(block_columns.astype(jnp.float32).T.astype(jnp.bfloat16))
        columns = jnp.concatenate(columns, axis=0)
        probes = jnp.concatenate([block[feature_count:, :] for block in blocks], axis=1)
        result = []
        for own, total in zip(rows, totals):
            exponent = jnp.dot(columns, own, preferred_element_type=jnp.float32)
            weights = jnp.exp(exponent).astype(jnp.bfloat16)
            result.append(total + jnp.dot(probes, weights, preferred_element_type=jnp.float32))
        return result

    if first:
        totals = [start_ref[...] * probes_ref[...]]
        totals += [jnp.zeros(probes_ref.shape, jnp.float32)] * (plane_count - 1)
    else:
        totals = [start_ref[number] for number in range(plane_count)]
    if len(line_refs[0].shape) == 2:
        totals = add_blocks([ref[...] for ref in line_refs], totals)
    else:
        totals = lax.fori_loop(
            0,
            line_refs[0].shape[0],
            lambda number, value: add_blocks([line_refs[0][number]], value),
            totals,
        )
    for number, total in enumerate(totals):
        partial_ref[number] = total
    partial_ref[plane_count] = probes_ref[...]


def combine_kernel(plane_count, *refs):
    partial_refs = refs[:-2]
    image_ref, sums_ref = refs[-2:]
    lane = lax.broadcasted_iota(jnp.int32, sums_ref.shape, 1)
    products = [0.0, 0.0, 0.0]
    for number, own_ref in enumerate(partial_refs):
        image = sum(
            ref[place_of(step, number, plane_count)] for step, ref in enumerate(partial_refs)
        )
        if number == 0:
            image_ref[...] = image
        probes = own_ref[plane_count]
        products[0] += probes * probes
        products[1] += probes * image
        products[2] += image * image
    sums = jnp.zeros(sums_ref.shape, jnp.float32)
    for number, product in enumerate(products):
        sums = jnp.where(lane == number, jnp.sum(product, axis=1, keepdims=True), sums)
    sums_ref[...] = sums


def finish_kernel(image_ref, probes_ref, *refs):
    *sums_refs, solution_ref, residual_ref, direction_ref = refs
    sums = jnp.zeros(sums_refs[0].shape[-2:], jnp.float32)
    for ref in sums_refs:
        value = ref[...]
        sums = sums + (value if value.ndim == 2 else jnp.sum(value, axis=0))
    start_norms, curvature, image_norms = sums[:, 0:1], sums[:, 1:2], sums[:, 2:3]
    alpha = start_norms / curvature
    new_norms = start_norms - 2.0 * alpha * curvature + alpha * alpha * image_norms
    probes = probes_ref[...]
    residual = probes - alpha * image_ref[...]
    solution_ref[...] = alpha * probes
    residual_ref[...] = residual
    direction_ref[...] = residual + (new_norms / start_norms) * probes


def paired(count):
    return count & (count - 1) == 0


def source_of(device, step, count):
    return device ^ step if paired(count) else (device - step) % count


def place_of(step, number, count):
    return step ^ number if paired(count) else (number - step) % count


def everywhere(value, axes, count):
    if count > DIRECT:
        return [lax.all_gather(value, axes, axis=0, tiled=False)]
    return [value] + [
        lax.ppermute(value, axes, [(source_of(i, step, count), i) for i in range(count)])
        for step in range(1, count)
    ]


def plane_blocks(value, shape):
    grp_count, sub_count = shape
    if sub_count != 2 or not paired(grp_count):
        return everywhere(value, PLANE, grp_count * sub_count)
    blocks = everywhere(value, ("sub",), sub_count)
    moved = [everywhere(block, ("grp",), grp_count) for block in blocks]
    return [moved[sub][grp] for grp in range(grp_count) for sub in range(sub_count)]


def make_local(plane_shape, line_count):
    plane_count = plane_shape[0] * plane_shape[1]

    def local(features, lengthscale, noise_var, probes):
        feature_count, width = features.shape
        probe_count = probes.shape[0]
        scaled = (features.astype(jnp.float32) / lengthscale[:, None]).astype(jnp.bfloat16)
        line = pl.pallas_call(
            pack_kernel,
            out_shape=jax.ShapeDtypeStruct((feature_count + probe_count, width), jnp.bfloat16),
            compiler_params=VMEM,
        )(scaled, probes)
        lines = everywhere(line, LINE, line_count)
        planes = plane_blocks(scaled, plane_shape)

        def partial_of(blocks, start, first):
            work = plane_count * len(blocks) * width * width
            return pl.pallas_call(
                lambda *refs: image_kernel(feature_count, plane_count, first, *refs),
                out_shape=jax.ShapeDtypeStruct((plane_count + 1, probe_count, width), jnp.float32),
                compiler_params=VMEM,
                cost_estimate=pl.CostEstimate(
                    flops=2 * work * (feature_count + probe_count),
                    bytes_accessed=4 * width * plane_count * feature_count,
                    transcendentals=work,
                ),
            )(*planes, *blocks, start, probes)

        partial = partial_of(lines[:3], noise_var[None, :], True)
        if len(lines) > 3:
            partial = partial_of(lines[3:], partial, False)
        image, sums = pl.pallas_call(
            lambda *refs: combine_kernel(plane_count, *refs),
            out_shape=(
                jax.ShapeDtypeStruct(probes.shape, jnp.float32),
                jax.ShapeDtypeStruct((probe_count, 128), jnp.float32),
            ),
            compiler_params=VMEM,
        )(*everywhere(partial, PLANE, plane_count))
        outs = (jax.ShapeDtypeStruct(probes.shape, jnp.float32),) * 3
        return pl.pallas_call(finish_kernel, out_shape=outs, compiler_params=VMEM)(
            image, probes, *everywhere(sums, LINE, line_count)
        )

    return local


def solution(mesh):
    plane_shape = (mesh.shape["grp"], mesh.shape["sub"])
    spread = P(None, ("parts", "blk", "grp", "sub"))
    return jax.shard_map(
        make_local(plane_shape, mesh.shape["blk"]),
        mesh=mesh,
        in_specs=(spread, P("parts"), P(("parts", "blk", "grp", "sub")), spread),
        out_specs=(spread, spread, spread),
        check_vma=False,
    )
```

```python
import jax
import jax.numpy as jnp
from jax import lax
from jax.experimental import pallas as pl
from jax.experimental.pallas import tpu as pltpu
from jax.sharding import PartitionSpec as P

PLANE = ("grp", "sub")
LINE = ("blk",)
DIRECT = 8
VMEM = pltpu.CompilerParams(vmem_limit_bytes=40 * 1024 * 1024)
HALF = 8


def pieces_of(value):
    pieces = []
    for _ in range(3):
        piece = value.astype(jnp.bfloat16).astype(jnp.float32)
        pieces.append(piece)
        value = value - piece
    return pieces


def norm_rows(scaled, place):
    norms = -0.5 * jnp.sum(jnp.square(scaled.astype(jnp.float32)), axis=0, keepdims=True)
    row = lax.broadcasted_iota(jnp.int32, (2 * HALF, scaled.shape[1]), 0)
    here, there = place * HALF, (1 - place) * HALF
    rows = jnp.where((row >= there) & (row < there + 3), 1.0, 0.0)
    for number, piece in enumerate(pieces_of(norms)):
        rows = jnp.where(row == here + number, piece, rows)
    return rows.astype(jnp.bfloat16)


def pack_kernel(scaled_ref, probes_ref, line_ref):
    line_ref[...] = jnp.concatenate(
        [scaled_ref[...], probes_ref[...].astype(jnp.bfloat16)], axis=0
    )


def image_kernel(feature_count, plane_count, *refs):
    plane_refs = refs[:plane_count]
    line_refs = refs[plane_count:-3]
    noise_ref, probes_ref, partial_ref = refs[-3:]
    rows = [jnp.concatenate([ref[...], norm_rows(ref[...], 1)], axis=0) for ref in plane_refs]

    def add_blocks(blocks, totals):
        columns = []
        for block in blocks:
            scaled = block[:feature_count, :]
            block_columns = jnp.concatenate([scaled, norm_rows(scaled, 0)], axis=0)
            columns.append(block_columns.astype(jnp.float32).T.astype(jnp.bfloat16))
        columns = jnp.concatenate(columns, axis=0)
        probes = jnp.concatenate([block[feature_count:, :] for block in blocks], axis=1)
        result = []
        for own, total in zip(rows, totals):
            exponent = jnp.dot(columns, own, preferred_element_type=jnp.float32)
            weights = jnp.exp(exponent).astype(jnp.bfloat16)
            result.append(total + jnp.dot(probes, weights, preferred_element_type=jnp.float32))
        return result

    totals = [noise_ref[...] * probes_ref[...]]
    totals += [jnp.zeros(probes_ref.shape, jnp.float32)] * (plane_count - 1)
    if len(line_refs[0].shape) == 2:
        totals = add_blocks([ref[...] for ref in line_refs], totals)
    else:
        totals = lax.fori_loop(
            0,
            line_refs[0].shape[0],
            lambda number, value: add_blocks([line_refs[0][number]], value),
            totals,
        )
    for number, total in enumerate(totals):
        partial_ref[number] = total
    partial_ref[plane_count] = probes_ref[...]


def combine_kernel(plane_count, *refs):
    partial_refs = [refs[number] for number in exchange_order(plane_count)]
    image_ref, sums_ref = refs[-2:]
    lane = lax.broadcasted_iota(jnp.int32, sums_ref.shape, 1)
    products = [0.0, 0.0, 0.0]
    for number, own_ref in enumerate(partial_refs):
        image = sum(
            ref[place_of(step, number, plane_count)] for step, ref in enumerate(partial_refs)
        )
        if number == 0:
            image_ref[...] = image
        probes = own_ref[plane_count]
        products[0] += probes * probes
        products[1] += probes * image
        products[2] += image * image
    sums = jnp.zeros(sums_ref.shape, jnp.float32)
    for number, product in enumerate(products):
        sums = jnp.where(lane == number, jnp.sum(product, axis=1, keepdims=True), sums)
    sums_ref[...] = sums


def finish_kernel(image_ref, probes_ref, *refs):
    *sums_refs, solution_ref, residual_ref, direction_ref = refs
    sums = jnp.zeros(sums_refs[0].shape[-2:], jnp.float32)
    for ref in sums_refs:
        value = ref[...]
        sums = sums + (value if value.ndim == 2 else jnp.sum(value, axis=0))
    start_norms, curvature, image_norms = sums[:, 0:1], sums[:, 1:2], sums[:, 2:3]
    alpha = start_norms / curvature
    new_norms = start_norms - 2.0 * alpha * curvature + alpha * alpha * image_norms
    probes = probes_ref[...]
    residual = probes - alpha * image_ref[...]
    solution_ref[...] = alpha * probes
    residual_ref[...] = residual
    direction_ref[...] = residual + (new_norms / start_norms) * probes


def paired(count):
    return count & (count - 1) == 0


def source_of(device, step, count):
    return device ^ step if paired(count) else (device - step) % count


def place_of(step, number, count):
    return step ^ number if paired(count) else (number - step) % count


def exchange_order(count):
    return (0, 1, 3, 2) if count == 4 else tuple(range(count))


def everywhere(value, axes, count):
    if count > DIRECT:
        return [lax.all_gather(value, axes, axis=0, tiled=False)]
    return [value] + [
        lax.ppermute(value, axes, [(source_of(i, step, count), i) for i in range(count)])
        for step in range(1, count)
    ]


def plane_blocks(value, shape):
    grp_count, sub_count = shape
    if sub_count != 2 or not paired(grp_count):
        return everywhere(value, PLANE, grp_count * sub_count)
    blocks = everywhere(value, ("sub",), sub_count)
    moved = [everywhere(block, ("grp",), grp_count) for block in blocks]
    return [moved[sub][grp] for grp in range(grp_count) for sub in range(sub_count)]


def make_local(plane_shape, line_count):
    plane_count = plane_shape[0] * plane_shape[1]

    def local(features, lengthscale, noise_var, probes):
        feature_count, width = features.shape
        probe_count = probes.shape[0]
        scaled = (features.astype(jnp.float32) / lengthscale[:, None]).astype(jnp.bfloat16)
        line = pl.pallas_call(
            pack_kernel,
            out_shape=jax.ShapeDtypeStruct((feature_count + probe_count, width), jnp.bfloat16),
            compiler_params=VMEM,
        )(scaled, probes)
        lines = everywhere(line, LINE, line_count)
        planes = plane_blocks(scaled, plane_shape)
        partial = pl.pallas_call(
            lambda *refs: image_kernel(feature_count, plane_count, *refs),
            out_shape=jax.ShapeDtypeStruct((plane_count + 1, probe_count, width), jnp.float32),
            compiler_params=VMEM,
        )(*planes, *lines, noise_var[None, :], probes)
        partials = everywhere(partial, PLANE, plane_count)
        image, sums = pl.pallas_call(
            lambda *refs: combine_kernel(plane_count, *refs),
            out_shape=(
                jax.ShapeDtypeStruct(probes.shape, jnp.float32),
                jax.ShapeDtypeStruct((probe_count, 128), jnp.float32),
            ),
            compiler_params=VMEM,
        )(*[partials[number] for number in exchange_order(plane_count)])
        outs = (jax.ShapeDtypeStruct(probes.shape, jnp.float32),) * 3
        return pl.pallas_call(finish_kernel, out_shape=outs, compiler_params=VMEM)(
            image, probes, *everywhere(sums, LINE, line_count)
        )

    return local


def solution(mesh):
    plane_shape = (mesh.shape["grp"], mesh.shape["sub"])
    spread = P(None, ("parts", "blk", "grp", "sub"))
    return jax.shard_map(
        make_local(plane_shape, mesh.shape["blk"]),
        mesh=mesh,
        in_specs=(spread, P("parts"), P(("parts", "blk", "grp", "sub")), spread),
        out_specs=(spread, spread, spread),
        check_vma=False,
    )
```

```python
import jax
import jax.numpy as jnp
from jax import lax
from jax.experimental import pallas as pl
from jax.experimental.pallas import tpu as pltpu
from jax.sharding import PartitionSpec as P

PLANE = ("grp", "sub")
LINE = ("blk",)
DIRECT = 8
VMEM = pltpu.CompilerParams(vmem_limit_bytes=40 * 1024 * 1024)
FORTH = (0, 4, 1, 3, 5, 6, 7, 2)
BACK = (0, 2, 7, 3, 1, 4, 5, 6)
EXCHANGE = {count: tuple(range(count)) for count in range(1, DIRECT + 1)} | {4: (0, 1, 3, 2)}


def pieces_of(value):
    pieces = []
    for _ in range(3):
        piece = value.astype(jnp.bfloat16).astype(jnp.float32)
        pieces.append(piece)
        value = value - piece
    return pieces


def half_norms(scaled, axis):
    return 0.5 * jnp.sum(jnp.square(scaled), axis=axis, keepdims=True)


def arranged(blocks, places):
    return [blocks[place] for place in places] if len(blocks) == len(places) else list(blocks)


def pack_kernel(scaled_ref, probes_ref, line_ref, plane_ref):
    high, low, _ = pieces_of(probes_ref[...])
    high, low = high.astype(jnp.bfloat16), low.astype(jnp.bfloat16)
    line_ref[...] = jnp.concatenate([scaled_ref[...], high], axis=0)
    plane_ref[...] = jnp.concatenate([scaled_ref[...], high, low], axis=0)


def image_kernel(feature_count, plane_count, *refs):
    noise_ref, probes_ref, partial_ref = refs[-3:]
    block_refs = arranged(refs[:-3], BACK)
    plane_refs = block_refs[:plane_count]
    line_refs = block_refs[plane_count:]
    rows = []
    for ref in plane_refs:
        scaled = ref[:feature_count, :]
        rows.append((scaled, half_norms(scaled.astype(jnp.float32), 0)))

    def add_blocks(blocks, totals):
        columns, column_norms = [], []
        for block in blocks:
            scaled = block[:feature_count, :].astype(jnp.float32).T
            columns.append(scaled.astype(jnp.bfloat16))
            column_norms.append(half_norms(scaled, 1))
        columns = jnp.concatenate(columns, axis=0)
        column_norms = jnp.concatenate(column_norms, axis=0)
        probes = jnp.concatenate([block[feature_count:, :] for block in blocks], axis=1)
        result = []
        for (own, own_norms), total in zip(rows, totals):
            inner = jnp.dot(columns, own, preferred_element_type=jnp.float32)
            weights = jnp.exp(inner - (column_norms + own_norms)).astype(jnp.bfloat16)
            result.append(total + jnp.dot(probes, weights, preferred_element_type=jnp.float32))
        return result

    totals = [noise_ref[...] * probes_ref[...]]
    totals += [jnp.zeros(probes_ref.shape, jnp.float32)] * (plane_count - 1)
    if len(line_refs[0].shape) == 2:
        totals = add_blocks([ref[...] for ref in line_refs], totals)
    else:
        totals = lax.fori_loop(
            0,
            line_refs[0].shape[0],
            lambda number, value: add_blocks([line_refs[0][number]], value),
            totals,
        )
    for number, total in enumerate(totals):
        partial_ref[number] = total


def combine_kernel(feature_count, plane_count, *refs):
    plane_refs = refs[:plane_count]
    probes_ref = refs[plane_count]
    partial_refs = refs[plane_count + 1 : -2]
    partial_refs = [partial_refs[number] for number in EXCHANGE[plane_count]]
    image_ref, sums_ref = refs[-2:]
    probe_count = image_ref.shape[0]
    lane = lax.broadcasted_iota(jnp.int32, sums_ref.shape, 1)
    products = [0.0, 0.0, 0.0]
    for number, plane_ref in enumerate(plane_refs):
        image = sum(
            ref[place_of(step, number, plane_count)] for step, ref in enumerate(partial_refs)
        )
        if number == 0:
            image_ref[...] = image
            probes = probes_ref[...]
        else:
            middle = feature_count + probe_count
            probes = plane_ref[feature_count:middle, :].astype(jnp.float32)
            probes = probes + plane_ref[middle:, :].astype(jnp.float32)
        products[0] += probes * probes
        products[1] += probes * image
        products[2] += image * image
    sums = jnp.zeros(sums_ref.shape, jnp.float32)
    for number, product in enumerate(products):
        sums = jnp.where(lane == number, jnp.sum(product, axis=1, keepdims=True), sums)
    sums_ref[...] = sums


def finish_kernel(image_ref, probes_ref, *refs):
    *sums_refs, solution_ref, residual_ref, direction_ref = refs
    sums = jnp.zeros(sums_refs[0].shape[-2:], jnp.float32)
    for ref in sums_refs:
        value = ref[...]
        sums = sums + (value if value.ndim == 2 else jnp.sum(value, axis=0))
    start_norms, curvature, image_norms = sums[:, 0:1], sums[:, 1:2], sums[:, 2:3]
    alpha = start_norms / curvature
    new_norms = start_norms - 2.0 * alpha * curvature + alpha * alpha * image_norms
    probes = probes_ref[...]
    residual = probes - alpha * image_ref[...]
    solution_ref[...] = alpha * probes
    residual_ref[...] = residual
    direction_ref[...] = residual + (new_norms / start_norms) * probes


def paired(count):
    return count & (count - 1) == 0


def source_of(device, step, count):
    return device ^ step if paired(count) else (device - step) % count


def place_of(step, number, count):
    return step ^ number if paired(count) else (number - step) % count


def everywhere(value, axes, count):
    if count > DIRECT:
        return [lax.all_gather(value, axes, axis=0, tiled=False)]
    blocks = {0: value}
    for step in range(1, count):
        pairs = [(source_of(i, step, count), i) for i in range(count)]
        blocks[step] = lax.ppermute(value, axes, pairs)
    return [blocks[step] for step in range(count)]


def plane_blocks(value, shape):
    grp_count, sub_count = shape
    if sub_count != 2 or not paired(grp_count):
        return everywhere(value, PLANE, grp_count * sub_count)
    blocks = everywhere(value, ("sub",), sub_count)
    moved = [everywhere(block, ("grp",), grp_count) for block in blocks]
    return [moved[sub][grp] for grp in range(grp_count) for sub in range(sub_count)]


def make_local(plane_shape, line_count):
    plane_count = plane_shape[0] * plane_shape[1]

    def local(features, lengthscale, noise_var, probes):
        feature_count, width = features.shape
        probe_count = probes.shape[0]
        scaled = (features.astype(jnp.float32) / lengthscale[:, None]).astype(jnp.bfloat16)
        line, plane = pl.pallas_call(
            pack_kernel,
            out_shape=(
                jax.ShapeDtypeStruct((feature_count + probe_count, width), jnp.bfloat16),
                jax.ShapeDtypeStruct((feature_count + 2 * probe_count, width), jnp.bfloat16),
            ),
            compiler_params=VMEM,
        )(scaled, probes)
        lines = everywhere(line, LINE, line_count)
        planes = everywhere(plane, PLANE, plane_count)
        partial = pl.pallas_call(
            lambda *refs: image_kernel(feature_count, plane_count, *refs),
            out_shape=jax.ShapeDtypeStruct((plane_count, probe_count, width), jnp.float32),
            compiler_params=VMEM,
        )(*arranged(planes + lines, FORTH), noise_var[None, :], probes)
        partials = everywhere(partial, PLANE, plane_count)
        image, sums = pl.pallas_call(
            lambda *refs: combine_kernel(feature_count, plane_count, *refs),
            out_shape=(
                jax.ShapeDtypeStruct(probes.shape, jnp.float32),
                jax.ShapeDtypeStruct((probe_count, 128), jnp.float32),
            ),
            compiler_params=VMEM,
        )(*planes, probes, *[partials[number] for number in EXCHANGE[plane_count]])
        outs = (jax.ShapeDtypeStruct(probes.shape, jnp.float32),) * 3
        return pl.pallas_call(finish_kernel, out_shape=outs, compiler_params=VMEM)(
            image, probes, *everywhere(sums, LINE, line_count)
        )

    return local


def solution(mesh):
    plane_shape = (mesh.shape["grp"], mesh.shape["sub"])
    spread = P(None, ("parts", "blk", "grp", "sub"))
    return jax.shard_map(
        make_local(plane_shape, mesh.shape["blk"]),
        mesh=mesh,
        in_specs=(spread, P("parts"), P(("parts", "blk", "grp", "sub")), spread),
        out_specs=(spread, spread, spread),
        check_vma=False,
    )
```

```python
import jax
import jax.numpy as jnp
from jax import lax
from jax.experimental import pallas as pl
from jax.experimental.pallas import tpu as pltpu
from jax.sharding import PartitionSpec as P

PLANE = ("grp", "sub")
LINE = ("blk",)
DIRECT = 8
VMEM = pltpu.CompilerParams(vmem_limit_bytes=40 * 1024 * 1024)
LOG2_E = 1.4426950408889634
HALF = 8


def pieces_of(value):
    pieces = []
    for _ in range(3):
        piece = value.astype(jnp.bfloat16).astype(jnp.float32)
        pieces.append(piece)
        value = value - piece
    return pieces


def norm_rows(scaled, place):
    norms = -0.5 * jnp.sum(jnp.square(scaled.astype(jnp.float32)), axis=0, keepdims=True)
    row = lax.broadcasted_iota(jnp.int32, (2 * HALF, scaled.shape[1]), 0)
    here, there = place * HALF, (1 - place) * HALF
    rows = jnp.where((row >= there) & (row < there + 3), 1.0, 0.0)
    for number, piece in enumerate(pieces_of(norms)):
        rows = jnp.where(row == here + number, piece, rows)
    return rows.astype(jnp.bfloat16)


def pack_kernel(scaled_ref, probes_ref, line_ref):
    line_ref[...] = jnp.concatenate(
        [scaled_ref[...], probes_ref[...].astype(jnp.bfloat16)], axis=0
    )


def image_kernel(feature_count, plane_count, *refs):
    plane_refs = refs[:plane_count]
    line_refs = refs[plane_count:-3]
    noise_ref, probes_ref, partial_ref = refs[-3:]
    rows = [jnp.concatenate([ref[...], norm_rows(ref[...], 1)], axis=0) for ref in plane_refs]

    def add_blocks(blocks, totals):
        columns = []
        for block in blocks:
            scaled = block[:feature_count, :]
            block_columns = jnp.concatenate([scaled, norm_rows(scaled, 0)], axis=0)
            columns.append(block_columns.astype(jnp.float32).T.astype(jnp.bfloat16))
        columns = jnp.concatenate(columns, axis=0)
        probes = jnp.concatenate([block[feature_count:, :] for block in blocks], axis=1)
        result = []
        for own, total in zip(rows, totals):
            exponent = jnp.dot(columns, own, preferred_element_type=jnp.float32)
            weights = jnp.exp2(exponent * LOG2_E).astype(jnp.bfloat16)
            result.append(total + jnp.dot(probes, weights, preferred_element_type=jnp.float32))
        return result

    totals = [noise_ref[...] * probes_ref[...]]
    totals += [jnp.zeros(probes_ref.shape, jnp.float32)] * (plane_count - 1)
    if len(line_refs[0].shape) == 2:
        totals = add_blocks([ref[...] for ref in line_refs], totals)
    else:
        totals = lax.fori_loop(
            0,
            line_refs[0].shape[0],
            lambda number, value: add_blocks([line_refs[0][number]], value),
            totals,
        )
    for number, total in enumerate(totals):
        partial_ref[number] = total
    partial_ref[plane_count] = probes_ref[...]


def combine_kernel(plane_count, *refs):
    partial_refs = [refs[number] for number in exchange_order(plane_count)]
    image_ref, sums_ref = refs[-2:]
    lane = lax.broadcasted_iota(jnp.int32, sums_ref.shape, 1)
    products = [0.0, 0.0, 0.0]
    for number, own_ref in enumerate(partial_refs):
        image = sum(
            ref[place_of(step, number, plane_count)] for step, ref in enumerate(partial_refs)
        )
        if number == 0:
            image_ref[...] = image
        probes = own_ref[plane_count]
        products[0] += probes * probes
        products[1] += probes * image
        products[2] += image * image
    sums = jnp.zeros(sums_ref.shape, jnp.float32)
    for number, product in enumerate(products):
        sums = jnp.where(lane == number, jnp.sum(product, axis=1, keepdims=True), sums)
    sums_ref[...] = sums


def finish_kernel(image_ref, probes_ref, *refs):
    *sums_refs, solution_ref, residual_ref, direction_ref = refs
    sums = jnp.zeros(sums_refs[0].shape[-2:], jnp.float32)
    for ref in sums_refs:
        value = ref[...]
        sums = sums + (value if value.ndim == 2 else jnp.sum(value, axis=0))
    start_norms, curvature, image_norms = sums[:, 0:1], sums[:, 1:2], sums[:, 2:3]
    alpha = start_norms / curvature
    new_norms = start_norms - 2.0 * alpha * curvature + alpha * alpha * image_norms
    probes = probes_ref[...]
    residual = probes - alpha * image_ref[...]
    solution_ref[...] = alpha * probes
    residual_ref[...] = residual
    direction_ref[...] = residual + (new_norms / start_norms) * probes


def paired(count):
    return count & (count - 1) == 0


def source_of(device, step, count):
    return device ^ step if paired(count) else (device - step) % count


def place_of(step, number, count):
    return step ^ number if paired(count) else (number - step) % count


def exchange_order(count):
    return (0, 1, 3, 2) if count == 4 else tuple(range(count))


def everywhere(value, axes, count):
    if count > DIRECT:
        return [lax.all_gather(value, axes, axis=0, tiled=False)]
    return [value] + [
        lax.ppermute(value, axes, [(source_of(i, step, count), i) for i in range(count)])
        for step in range(1, count)
    ]


def plane_blocks(value, shape):
    grp_count, sub_count = shape
    if sub_count != 2 or not paired(grp_count):
        return everywhere(value, PLANE, grp_count * sub_count)
    blocks = everywhere(value, ("sub",), sub_count)
    moved = [everywhere(block, ("grp",), grp_count) for block in blocks]
    return [moved[sub][grp] for grp in range(grp_count) for sub in range(sub_count)]


def make_local(plane_shape, line_count):
    plane_count = plane_shape[0] * plane_shape[1]

    def local(features, lengthscale, noise_var, probes):
        feature_count, width = features.shape
        probe_count = probes.shape[0]
        scaled = (features.astype(jnp.float32) / lengthscale[:, None]).astype(jnp.bfloat16)
        line = pl.pallas_call(
            pack_kernel,
            out_shape=jax.ShapeDtypeStruct((feature_count + probe_count, width), jnp.bfloat16),
            compiler_params=VMEM,
        )(scaled, probes)
        lines = everywhere(line, LINE, line_count)
        planes = plane_blocks(scaled, plane_shape)
        partial = pl.pallas_call(
            lambda *refs: image_kernel(feature_count, plane_count, *refs),
            out_shape=jax.ShapeDtypeStruct((plane_count + 1, probe_count, width), jnp.float32),
            compiler_params=VMEM,
        )(*planes, *lines, noise_var[None, :], probes)
        partials = everywhere(partial, PLANE, plane_count)
        image, sums = pl.pallas_call(
            lambda *refs: combine_kernel(plane_count, *refs),
            out_shape=(
                jax.ShapeDtypeStruct(probes.shape, jnp.float32),
                jax.ShapeDtypeStruct((probe_count, 128), jnp.float32),
            ),
            compiler_params=VMEM,
        )(*[partials[number] for number in exchange_order(plane_count)])
        outs = (jax.ShapeDtypeStruct(probes.shape, jnp.float32),) * 3
        return pl.pallas_call(finish_kernel, out_shape=outs, compiler_params=VMEM)(
            image, probes, *everywhere(sums, LINE, line_count)
        )

    return local


def solution(mesh):
    plane_shape = (mesh.shape["grp"], mesh.shape["sub"])
    spread = P(None, ("parts", "blk", "grp", "sub"))
    return jax.shard_map(
        make_local(plane_shape, mesh.shape["blk"]),
        mesh=mesh,
        in_specs=(spread, P("parts"), P(("parts", "blk", "grp", "sub")), spread),
        out_specs=(spread, spread, spread),
        check_vma=False,
    )
```

```python
import jax
import jax.numpy as jnp
from jax import lax
from jax.experimental import pallas as pl
from jax.experimental.pallas import tpu as pltpu
from jax.sharding import PartitionSpec as P

PLANE = ("grp", "sub")
LINE = ("blk",)
DIRECT = 8
VMEM = pltpu.CompilerParams(vmem_limit_bytes=40 * 1024 * 1024)
LOG2_E = 1.4426950408889634
HALF = 8


def pieces_of(value):
    pieces = []
    for _ in range(3):
        piece = value.astype(jnp.bfloat16).astype(jnp.float32)
        pieces.append(piece)
        value = value - piece
    return pieces


def norm_rows(scaled, place):
    norms = -0.5 * jnp.sum(jnp.square(scaled.astype(jnp.float32)), axis=0, keepdims=True)
    row = lax.broadcasted_iota(jnp.int32, (2 * HALF, scaled.shape[1]), 0)
    here, there = place * HALF, (1 - place) * HALF
    rows = jnp.where((row >= there) & (row < there + 3), 1.0, 0.0)
    for number, piece in enumerate(pieces_of(norms)):
        rows = jnp.where(row == here + number, piece, rows)
    return rows.astype(jnp.bfloat16)


def pack_kernel(scaled_ref, probes_ref, line_ref):
    line_ref[...] = jnp.concatenate(
        [scaled_ref[...], probes_ref[...].astype(jnp.bfloat16)], axis=0
    )


def image_kernel(feature_count, plane_count, *refs):
    plane_refs = refs[:plane_count]
    line_refs = refs[plane_count:-3]
    noise_ref, probes_ref, partial_ref = refs[-3:]
    width = partial_ref.shape[2]
    rows = []
    for ref in plane_refs:
        own = jnp.concatenate([ref[...], norm_rows(ref[...], 1)], axis=0)
        rows.append(own.astype(jnp.float32).T.astype(jnp.bfloat16))
    rows = jnp.concatenate(rows, axis=0)

    def add_block(block, total):
        scaled = block[:feature_count, :]
        columns = jnp.concatenate([scaled, norm_rows(scaled, 0)], axis=0)
        exponent = jnp.dot(rows, columns, preferred_element_type=jnp.float32)
        weights = jnp.exp2(exponent * LOG2_E).astype(jnp.bfloat16)
        return total + lax.dot_general(
            weights,
            block[feature_count:, :],
            (((1,), (1,)), ((), ())),
            preferred_element_type=jnp.float32,
        )

    total = jnp.zeros((plane_count * width, probes_ref.shape[0]), jnp.float32)
    if len(line_refs[0].shape) == 2:
        for ref in line_refs:
            total = add_block(ref[...], total)
    else:
        total = lax.fori_loop(
            0,
            line_refs[0].shape[0],
            lambda number, value: add_block(line_refs[0][number], value),
            total,
        )
    for number in range(plane_count):
        partial_ref[number] = total[number * width : (number + 1) * width, :].T
    partial_ref[0] += noise_ref[...] * probes_ref[...]
    partial_ref[plane_count] = probes_ref[...]


def combine_kernel(plane_count, *refs):
    partial_refs = [refs[number] for number in exchange_order(plane_count)]
    image_ref, sums_ref = refs[-2:]
    lane = lax.broadcasted_iota(jnp.int32, sums_ref.shape, 1)
    products = [0.0, 0.0, 0.0]
    for number, own_ref in enumerate(partial_refs):
        image = sum(
            ref[place_of(step, number, plane_count)] for step, ref in enumerate(partial_refs)
        )
        if number == 0:
            image_ref[...] = image
        probes = own_ref[plane_count]
        products[0] += probes * probes
        products[1] += probes * image
        products[2] += image * image
    sums = jnp.zeros(sums_ref.shape, jnp.float32)
    for number, product in enumerate(products):
        sums = jnp.where(lane == number, jnp.sum(product, axis=1, keepdims=True), sums)
    sums_ref[...] = sums


def finish_kernel(image_ref, probes_ref, *refs):
    *sums_refs, solution_ref, residual_ref, direction_ref = refs
    sums = jnp.zeros(sums_refs[0].shape[-2:], jnp.float32)
    for ref in sums_refs:
        value = ref[...]
        sums = sums + (value if value.ndim == 2 else jnp.sum(value, axis=0))
    start_norms, curvature, image_norms = sums[:, 0:1], sums[:, 1:2], sums[:, 2:3]
    alpha = start_norms / curvature
    new_norms = start_norms - 2.0 * alpha * curvature + alpha * alpha * image_norms
    probes = probes_ref[...]
    residual = probes - alpha * image_ref[...]
    solution_ref[...] = alpha * probes
    residual_ref[...] = residual
    direction_ref[...] = residual + (new_norms / start_norms) * probes


def paired(count):
    return count & (count - 1) == 0


def source_of(device, step, count):
    return device ^ step if paired(count) else (device - step) % count


def place_of(step, number, count):
    return step ^ number if paired(count) else (number - step) % count


def exchange_order(count):
    return (0, 1, 3, 2) if count == 4 else tuple(range(count))


def everywhere(value, axes, count):
    if count > DIRECT:
        return [lax.all_gather(value, axes, axis=0, tiled=False)]
    return [value] + [
        lax.ppermute(value, axes, [(source_of(i, step, count), i) for i in range(count)])
        for step in range(1, count)
    ]


def plane_blocks(value, shape):
    grp_count, sub_count = shape
    if sub_count != 2 or not paired(grp_count):
        return everywhere(value, PLANE, grp_count * sub_count)
    blocks = everywhere(value, ("sub",), sub_count)
    moved = [everywhere(block, ("grp",), grp_count) for block in blocks]
    return [moved[sub][grp] for grp in range(grp_count) for sub in range(sub_count)]


def make_local(plane_shape, line_count):
    plane_count = plane_shape[0] * plane_shape[1]

    def local(features, lengthscale, noise_var, probes):
        feature_count, width = features.shape
        probe_count = probes.shape[0]
        scaled = (features.astype(jnp.float32) / lengthscale[:, None]).astype(jnp.bfloat16)
        line = pl.pallas_call(
            pack_kernel,
            out_shape=jax.ShapeDtypeStruct((feature_count + probe_count, width), jnp.bfloat16),
            compiler_params=VMEM,
        )(scaled, probes)
        lines = everywhere(line, LINE, line_count)
        planes = plane_blocks(scaled, plane_shape)
        partial = pl.pallas_call(
            lambda *refs: image_kernel(feature_count, plane_count, *refs),
            out_shape=jax.ShapeDtypeStruct((plane_count + 1, probe_count, width), jnp.float32),
            compiler_params=VMEM,
        )(*planes, *lines, noise_var[None, :], probes)
        partials = everywhere(partial, PLANE, plane_count)
        image, sums = pl.pallas_call(
            lambda *refs: combine_kernel(plane_count, *refs),
            out_shape=(
                jax.ShapeDtypeStruct(probes.shape, jnp.float32),
                jax.ShapeDtypeStruct((probe_count, 128), jnp.float32),
            ),
            compiler_params=VMEM,
        )(*[partials[number] for number in exchange_order(plane_count)])
        outs = (jax.ShapeDtypeStruct(probes.shape, jnp.float32),) * 3
        return pl.pallas_call(finish_kernel, out_shape=outs, compiler_params=VMEM)(
            image, probes, *everywhere(sums, LINE, line_count)
        )

    return local


def solution(mesh):
    plane_shape = (mesh.shape["grp"], mesh.shape["sub"])
    spread = P(None, ("parts", "blk", "grp", "sub"))
    return jax.shard_map(
        make_local(plane_shape, mesh.shape["blk"]),
        mesh=mesh,
        in_specs=(spread, P("parts"), P(("parts", "blk", "grp", "sub")), spread),
        out_specs=(spread, spread, spread),
        check_vma=False,
    )
```

```python
import jax
import jax.numpy as jnp
from jax import lax
from jax.experimental import pallas as pl
from jax.experimental.pallas import tpu as pltpu
from jax.sharding import PartitionSpec as P

PLANE = ("grp", "sub")
LINE = ("blk",)
DIRECT = 8
VMEM = pltpu.CompilerParams(vmem_limit_bytes=40 * 1024 * 1024)
HALF = 8


def pieces_of(value):
    pieces = []
    for _ in range(3):
        piece = value.astype(jnp.bfloat16).astype(jnp.float32)
        pieces.append(piece)
        value = value - piece
    return pieces


def norm_rows(scaled, place):
    norms = -0.5 * jnp.sum(jnp.square(scaled.astype(jnp.float32)), axis=0, keepdims=True)
    row = lax.broadcasted_iota(jnp.int32, (2 * HALF, scaled.shape[1]), 0)
    here, there = place * HALF, (1 - place) * HALF
    rows = jnp.where((row >= there) & (row < there + 3), 1.0, 0.0)
    for number, piece in enumerate(pieces_of(norms)):
        rows = jnp.where(row == here + number, piece, rows)
    return rows.astype(jnp.bfloat16)


def pack_kernel(scaled_ref, probes_ref, line_ref):
    line_ref[...] = jnp.concatenate(
        [scaled_ref[...], probes_ref[...].astype(jnp.bfloat16)], axis=0
    )


def image_kernel(feature_count, plane_count, *refs):
    plane_refs = refs[:plane_count]
    line_refs = refs[plane_count:-3]
    noise_ref, probes_ref, partial_ref = refs[-3:]
    rows = [jnp.concatenate([ref[...], norm_rows(ref[...], 1)], axis=0) for ref in plane_refs]

    def add_blocks(blocks, totals):
        columns = []
        for block in blocks:
            scaled = block[:feature_count, :]
            block_columns = jnp.concatenate([scaled, norm_rows(scaled, 0)], axis=0)
            columns.append(block_columns.astype(jnp.float32).T.astype(jnp.bfloat16))
        columns = jnp.concatenate(columns, axis=0)
        probes = jnp.concatenate([block[feature_count:, :] for block in blocks], axis=1)
        result = []
        for own, total in zip(rows, totals):
            exponent = jnp.dot(columns, own, preferred_element_type=jnp.float32)
            weights = jnp.exp(exponent).astype(jnp.bfloat16)
            result.append(total + jnp.dot(probes, weights, preferred_element_type=jnp.float32))
        return result

    totals = [noise_ref[...] * probes_ref[...]]
    totals += [jnp.zeros(probes_ref.shape, jnp.float32)] * (plane_count - 1)
    if len(line_refs[0].shape) == 2:
        totals = add_blocks([ref[...] for ref in line_refs], totals)
    else:
        totals = lax.fori_loop(
            0,
            line_refs[0].shape[0],
            lambda number, value: add_blocks([line_refs[0][number]], value),
            totals,
        )
    for number, total in enumerate(totals):
        partial_ref[number] = total
    partial_ref[plane_count] = probes_ref[...]


def combine_kernel(plane_count, *refs):
    partial_refs = [refs[number] for number in exchange_order(plane_count)]
    image_ref, sums_ref = refs[-2:]
    lane = lax.broadcasted_iota(jnp.int32, sums_ref.shape, 1)
    products = [0.0, 0.0, 0.0]
    for number, own_ref in enumerate(partial_refs):
        image = sum(
            ref[place_of(step, number, plane_count)] for step, ref in enumerate(partial_refs)
        )
        if number == 0:
            image_ref[...] = image
        probes = own_ref[plane_count]
        products[0] += probes * probes
        products[1] += probes * image
        products[2] += image * image
    sums = jnp.zeros(sums_ref.shape, jnp.float32)
    for number, product in enumerate(products):
        sums = jnp.where(lane == number, jnp.sum(product, axis=1, keepdims=True), sums)
    sums_ref[...] = sums


def finish_kernel(image_ref, probes_ref, *refs):
    *sums_refs, solution_ref, residual_ref, direction_ref = refs
    sums = jnp.zeros(sums_refs[0].shape[-2:], jnp.float32)
    for ref in sums_refs:
        value = ref[...]
        sums = sums + (value if value.ndim == 2 else jnp.sum(value, axis=0))
    start_norms, curvature, image_norms = sums[:, 0:1], sums[:, 1:2], sums[:, 2:3]
    alpha = start_norms / curvature
    new_norms = start_norms - 2.0 * alpha * curvature + alpha * alpha * image_norms
    probes = probes_ref[...]
    residual = probes - alpha * image_ref[...]
    solution_ref[...] = alpha * probes
    residual_ref[...] = residual
    direction_ref[...] = residual + (new_norms / start_norms) * probes


def paired(count):
    return count & (count - 1) == 0


def source_of(device, step, count):
    return device ^ step if paired(count) else (device - step) % count


def place_of(step, number, count):
    return step ^ number if paired(count) else (number - step) % count


def exchange_order(count):
    return (0, 1, 3, 2) if count == 4 else tuple(range(count))


def everywhere(value, axes, count):
    if count > DIRECT:
        return [lax.all_gather(value, axes, axis=0, tiled=False)]
    return [value] + [
        lax.ppermute(value, axes, [(source_of(i, step, count), i) for i in range(count)])
        for step in range(1, count)
    ]


def along_line(value, line_count, sub_count):
    if line_count > DIRECT or sub_count != 2:
        return everywhere(value, LINE, line_count)
    blocks = [value]
    for step in range(1, line_count):
        pairs = [
            (2 * source_of(place, step, line_count) + 1 - core, 2 * place + core)
            for place in range(line_count)
            for core in range(2)
        ]
        blocks.append(lax.ppermute(value, LINE + ("sub",), pairs))
    return blocks


def plane_blocks(value, shape):
    grp_count, sub_count = shape
    if sub_count != 2 or not paired(grp_count):
        return everywhere(value, PLANE, grp_count * sub_count)
    blocks = everywhere(value, ("sub",), sub_count)
    moved = [everywhere(block, ("grp",), grp_count) for block in blocks]
    return [moved[sub][grp] for grp in range(grp_count) for sub in range(sub_count)]


def make_local(plane_shape, line_count):
    plane_count = plane_shape[0] * plane_shape[1]

    def local(features, lengthscale, noise_var, probes):
        feature_count, width = features.shape
        probe_count = probes.shape[0]
        scaled = (features.astype(jnp.float32) / lengthscale[:, None]).astype(jnp.bfloat16)
        line = pl.pallas_call(
            pack_kernel,
            out_shape=jax.ShapeDtypeStruct((feature_count + probe_count, width), jnp.bfloat16),
            compiler_params=VMEM,
        )(scaled, probes)
        lines = along_line(line, line_count, plane_shape[1])
        planes = plane_blocks(scaled, plane_shape)
        partial = pl.pallas_call(
            lambda *refs: image_kernel(feature_count, plane_count, *refs),
            out_shape=jax.ShapeDtypeStruct((plane_count + 1, probe_count, width), jnp.float32),
            compiler_params=VMEM,
        )(*planes, *lines, noise_var[None, :], probes)
        partials = everywhere(partial, PLANE, plane_count)
        image, sums = pl.pallas_call(
            lambda *refs: combine_kernel(plane_count, *refs),
            out_shape=(
                jax.ShapeDtypeStruct(probes.shape, jnp.float32),
                jax.ShapeDtypeStruct((probe_count, 128), jnp.float32),
            ),
            compiler_params=VMEM,
        )(*[partials[number] for number in exchange_order(plane_count)])
        outs = (jax.ShapeDtypeStruct(probes.shape, jnp.float32),) * 3
        return pl.pallas_call(finish_kernel, out_shape=outs, compiler_params=VMEM)(
            image, probes, *along_line(sums, line_count, plane_shape[1])
        )

    return local


def solution(mesh):
    plane_shape = (mesh.shape["grp"], mesh.shape["sub"])
    spread = P(None, ("parts", "blk", "grp", "sub"))
    return jax.shard_map(
        make_local(plane_shape, mesh.shape["blk"]),
        mesh=mesh,
        in_specs=(spread, P("parts"), P(("parts", "blk", "grp", "sub")), spread),
        out_specs=(spread, spread, spread),
        check_vma=False,
    )
```

```python
import jax
import jax.numpy as jnp
from jax import lax
from jax.experimental import pallas as pl
from jax.experimental.pallas import tpu as pltpu
from jax.sharding import PartitionSpec as P

PLANE = ("grp", "sub")
LINE = ("blk",)
DIRECT = 8
VMEM = pltpu.CompilerParams(vmem_limit_bytes=40 * 1024 * 1024)
HALF = 8


def pieces_of(value):
    pieces = []
    for _ in range(3):
        piece = value.astype(jnp.bfloat16).astype(jnp.float32)
        pieces.append(piece)
        value = value - piece
    return pieces


def norm_rows(scaled, place):
    norms = -0.5 * jnp.sum(jnp.square(scaled.astype(jnp.float32)), axis=0, keepdims=True)
    row = lax.broadcasted_iota(jnp.int32, (2 * HALF, scaled.shape[1]), 0)
    here, there = place * HALF, (1 - place) * HALF
    rows = jnp.where((row >= there) & (row < there + 3), 1.0, 0.0)
    for number, piece in enumerate(pieces_of(norms)):
        rows = jnp.where(row == here + number, piece, rows)
    return rows.astype(jnp.bfloat16)


def pack_kernel(scaled_ref, probes_ref, line_ref):
    line_ref[...] = jnp.concatenate(
        [scaled_ref[...], probes_ref[...].astype(jnp.bfloat16)], axis=0
    )


def apply_blocks(feature_count, rows, blocks, totals):
    columns = []
    for block in blocks:
        scaled = block[:feature_count, :]
        block_columns = jnp.concatenate([scaled, norm_rows(scaled, 0)], axis=0)
        columns.append(block_columns.astype(jnp.float32).T.astype(jnp.bfloat16))
    columns = jnp.concatenate(columns, axis=0)
    probes = jnp.concatenate([block[feature_count:, :] for block in blocks], axis=1)
    result = []
    for own, total in zip(rows, totals):
        exponent = jnp.dot(columns, own, preferred_element_type=jnp.float32)
        weights = jnp.exp(exponent).astype(jnp.bfloat16)
        result.append(total + jnp.dot(probes, weights, preferred_element_type=jnp.float32))
    return result


def image_kernel(feature_count, plane_count, *refs):
    plane_refs = refs[:plane_count]
    line_refs = refs[plane_count:-4]
    noise_ref, probes_ref, partial_ref, rows_ref = refs[-4:]
    rows = [jnp.concatenate([ref[...], norm_rows(ref[...], 1)], axis=0) for ref in plane_refs]
    for number, own in enumerate(rows):
        rows_ref[number] = own
    totals = [noise_ref[...] * probes_ref[...]]
    totals += [jnp.zeros(probes_ref.shape, jnp.float32)] * (plane_count - 1)
    if len(line_refs[0].shape) == 2:
        totals = apply_blocks(feature_count, rows, [ref[...] for ref in line_refs], totals)
    else:
        totals = lax.fori_loop(
            0,
            line_refs[0].shape[0],
            lambda number, value: apply_blocks(
                feature_count, rows, [line_refs[0][number]], value
            ),
            totals,
        )
    for number, total in enumerate(totals):
        partial_ref[number] = total
    partial_ref[plane_count] = probes_ref[...]


def add_kernel(feature_count, plane_count, rows_ref, start_ref, line_ref, partial_ref):
    rows = [rows_ref[number] for number in range(plane_count)]
    totals = [start_ref[number] for number in range(plane_count)]
    totals = apply_blocks(feature_count, rows, [line_ref[...]], totals)
    for number, total in enumerate(totals):
        partial_ref[number] = total
    partial_ref[plane_count] = start_ref[plane_count]


def combine_kernel(plane_count, *refs):
    partial_refs = [refs[number] for number in exchange_order(plane_count)]
    image_ref, sums_ref = refs[-2:]
    lane = lax.broadcasted_iota(jnp.int32, sums_ref.shape, 1)
    products = [0.0, 0.0, 0.0]
    for number, own_ref in enumerate(partial_refs):
        image = sum(
            ref[place_of(step, number, plane_count)] for step, ref in enumerate(partial_refs)
        )
        if number == 0:
            image_ref[...] = image
        probes = own_ref[plane_count]
        products[0] += probes * probes
        products[1] += probes * image
        products[2] += image * image
    sums = jnp.zeros(sums_ref.shape, jnp.float32)
    for number, product in enumerate(products):
        sums = jnp.where(lane == number, jnp.sum(product, axis=1, keepdims=True), sums)
    sums_ref[...] = sums


def finish_kernel(image_ref, probes_ref, *refs):
    *sums_refs, solution_ref, residual_ref, direction_ref = refs
    sums = jnp.zeros(sums_refs[0].shape[-2:], jnp.float32)
    for ref in sums_refs:
        value = ref[...]
        sums = sums + (value if value.ndim == 2 else jnp.sum(value, axis=0))
    start_norms, curvature, image_norms = sums[:, 0:1], sums[:, 1:2], sums[:, 2:3]
    alpha = start_norms / curvature
    new_norms = start_norms - 2.0 * alpha * curvature + alpha * alpha * image_norms
    probes = probes_ref[...]
    residual = probes - alpha * image_ref[...]
    solution_ref[...] = alpha * probes
    residual_ref[...] = residual
    direction_ref[...] = residual + (new_norms / start_norms) * probes


def paired(count):
    return count & (count - 1) == 0


def source_of(device, step, count):
    return device ^ step if paired(count) else (device - step) % count


def place_of(step, number, count):
    return step ^ number if paired(count) else (number - step) % count


def exchange_order(count):
    return (0, 1, 3, 2) if count == 4 else tuple(range(count))


def everywhere(value, axes, count):
    if count > DIRECT:
        return [lax.all_gather(value, axes, axis=0, tiled=False)]
    return [value] + [
        lax.ppermute(value, axes, [(source_of(i, step, count), i) for i in range(count)])
        for step in range(1, count)
    ]


def along_line(value, line_count, sub_count):
    if line_count > DIRECT or sub_count != 2:
        return everywhere(value, LINE, line_count)
    blocks = [value]
    for step in range(1, line_count):
        pairs = [
            (2 * source_of(place, step, line_count) + 1 - core, 2 * place + core)
            for place in range(line_count)
            for core in range(2)
        ]
        blocks.append(lax.ppermute(value, LINE + ("sub",), pairs))
    return blocks


def plane_blocks(value, shape):
    grp_count, sub_count = shape
    if sub_count != 2 or not paired(grp_count):
        return everywhere(value, PLANE, grp_count * sub_count)
    blocks = everywhere(value, ("sub",), sub_count)
    moved = [everywhere(block, ("grp",), grp_count) for block in blocks]
    return [moved[sub][grp] for grp in range(grp_count) for sub in range(sub_count)]


def make_local(plane_shape, line_count):
    plane_count = plane_shape[0] * plane_shape[1]

    def local(features, lengthscale, noise_var, probes):
        feature_count, width = features.shape
        probe_count = probes.shape[0]
        scaled = (features.astype(jnp.float32) / lengthscale[:, None]).astype(jnp.bfloat16)
        line = pl.pallas_call(
            pack_kernel,
            out_shape=jax.ShapeDtypeStruct((feature_count + probe_count, width), jnp.bfloat16),
            compiler_params=VMEM,
        )(scaled, probes)
        lines = along_line(line, line_count, plane_shape[1])
        planes = plane_blocks(scaled, plane_shape)
        early, late = lines[:1] + lines[2:], lines[1:2]
        partial_shape = jax.ShapeDtypeStruct((plane_count + 1, probe_count, width), jnp.float32)
        partial, rows = pl.pallas_call(
            lambda *refs: image_kernel(feature_count, plane_count, *refs),
            out_shape=(
                partial_shape,
                jax.ShapeDtypeStruct((plane_count, feature_count + 2 * HALF, width), jnp.bfloat16),
            ),
            compiler_params=VMEM,
        )(*planes, *early, noise_var[None, :], probes)
        for block in late:
            partial = pl.pallas_call(
                lambda *refs: add_kernel(feature_count, plane_count, *refs),
                out_shape=partial_shape,
                compiler_params=VMEM,
            )(rows, partial, block)
        partials = everywhere(partial, PLANE, plane_count)
        image, sums = pl.pallas_call(
            lambda *refs: combine_kernel(plane_count, *refs),
            out_shape=(
                jax.ShapeDtypeStruct(probes.shape, jnp.float32),
                jax.ShapeDtypeStruct((probe_count, 128), jnp.float32),
            ),
            compiler_params=VMEM,
        )(*[partials[number] for number in exchange_order(plane_count)])
        outs = (jax.ShapeDtypeStruct(probes.shape, jnp.float32),) * 3
        return pl.pallas_call(finish_kernel, out_shape=outs, compiler_params=VMEM)(
            image, probes, *along_line(sums, line_count, plane_shape[1])
        )

    return local


def solution(mesh):
    plane_shape = (mesh.shape["grp"], mesh.shape["sub"])
    spread = P(None, ("parts", "blk", "grp", "sub"))
    return jax.shard_map(
        make_local(plane_shape, mesh.shape["blk"]),
        mesh=mesh,
        in_specs=(spread, P("parts"), P(("parts", "blk", "grp", "sub")), spread),
        out_specs=(spread, spread, spread),
        check_vma=False,
    )
```

```python
import jax
import jax.numpy as jnp
from jax import lax
from jax.experimental import pallas as pl
from jax.experimental.pallas import tpu as pltpu
from jax.sharding import PartitionSpec as P

PLANE = ("grp", "sub")
LINE = ("blk",)
DIRECT = 8
VMEM = pltpu.CompilerParams(vmem_limit_bytes=40 * 1024 * 1024)
HALF = 8


def pieces_of(value):
    pieces = []
    for _ in range(3):
        piece = value.astype(jnp.bfloat16).astype(jnp.float32)
        pieces.append(piece)
        value = value - piece
    return pieces


def norm_rows(scaled, place):
    norms = -0.5 * jnp.sum(jnp.square(scaled.astype(jnp.float32)), axis=0, keepdims=True)
    row = lax.broadcasted_iota(jnp.int32, (2 * HALF, scaled.shape[1]), 0)
    here, there = place * HALF, (1 - place) * HALF
    rows = jnp.where((row >= there) & (row < there + 3), 1.0, 0.0)
    for number, piece in enumerate(pieces_of(norms)):
        rows = jnp.where(row == here + number, piece, rows)
    return rows.astype(jnp.bfloat16)


def pack_kernel(scaled_ref, probes_ref, line_ref):
    line_ref[...] = jnp.concatenate(
        [scaled_ref[...], probes_ref[...].astype(jnp.bfloat16)], axis=0
    )


def apply_blocks(feature_count, rows, blocks, totals):
    columns = []
    for block in blocks:
        scaled = block[:feature_count, :]
        block_columns = jnp.concatenate([scaled, norm_rows(scaled, 0)], axis=0)
        columns.append(block_columns.astype(jnp.float32).T.astype(jnp.bfloat16))
    columns = jnp.concatenate(columns, axis=0)
    probes = jnp.concatenate([block[feature_count:, :] for block in blocks], axis=1)
    result = []
    for own, total in zip(rows, totals):
        exponent = jnp.dot(columns, own, preferred_element_type=jnp.float32)
        weights = jnp.exp(exponent).astype(jnp.bfloat16)
        result.append(total + jnp.dot(probes, weights, preferred_element_type=jnp.float32))
    return result


def image_kernel(feature_count, plane_count, *refs):
    plane_refs = refs[:plane_count]
    line_refs = refs[plane_count:-3]
    noise_ref, probes_ref, partial_ref = refs[-3:]
    rows = [jnp.concatenate([ref[...], norm_rows(ref[...], 1)], axis=0) for ref in plane_refs]
    totals = [noise_ref[...] * probes_ref[...]]
    totals += [jnp.zeros(probes_ref.shape, jnp.float32)] * (plane_count - 1)
    if len(line_refs[0].shape) == 2:
        totals = apply_blocks(feature_count, rows, [ref[...] for ref in line_refs], totals)
    else:
        totals = lax.fori_loop(
            0,
            line_refs[0].shape[0],
            lambda number, value: apply_blocks(
                feature_count, rows, [line_refs[0][number]], value
            ),
            totals,
        )
    for number, total in enumerate(totals):
        partial_ref[number] = total
    partial_ref[plane_count] = probes_ref[...]


def add_kernel(feature_count, plane_count, *refs):
    plane_refs = refs[:plane_count]
    line_ref, start_ref, partial_ref = refs[plane_count:]
    rows = [jnp.concatenate([ref[...], norm_rows(ref[...], 1)], axis=0) for ref in plane_refs]
    totals = [start_ref[number] for number in range(plane_count)]
    totals = apply_blocks(feature_count, rows, [line_ref[...]], totals)
    for number, total in enumerate(totals):
        partial_ref[number] = total
    partial_ref[plane_count] = start_ref[plane_count]


def combine_kernel(plane_count, *refs):
    partial_refs = [refs[number] for number in exchange_order(plane_count)]
    image_ref, sums_ref = refs[-2:]
    lane = lax.broadcasted_iota(jnp.int32, sums_ref.shape, 1)
    products = [0.0, 0.0, 0.0]
    for number, own_ref in enumerate(partial_refs):
        image = sum(
            ref[place_of(step, number, plane_count)] for step, ref in enumerate(partial_refs)
        )
        if number == 0:
            image_ref[...] = image
        probes = own_ref[plane_count]
        products[0] += probes * probes
        products[1] += probes * image
        products[2] += image * image
    sums = jnp.zeros(sums_ref.shape, jnp.float32)
    for number, product in enumerate(products):
        sums = jnp.where(lane == number, jnp.sum(product, axis=1, keepdims=True), sums)
    sums_ref[...] = sums


def finish_kernel(image_ref, probes_ref, *refs):
    *sums_refs, solution_ref, residual_ref, direction_ref = refs
    sums = jnp.zeros(sums_refs[0].shape[-2:], jnp.float32)
    for ref in sums_refs:
        value = ref[...]
        sums = sums + (value if value.ndim == 2 else jnp.sum(value, axis=0))
    start_norms, curvature, image_norms = sums[:, 0:1], sums[:, 1:2], sums[:, 2:3]
    alpha = start_norms / curvature
    new_norms = start_norms - 2.0 * alpha * curvature + alpha * alpha * image_norms
    probes = probes_ref[...]
    residual = probes - alpha * image_ref[...]
    solution_ref[...] = alpha * probes
    residual_ref[...] = residual
    direction_ref[...] = residual + (new_norms / start_norms) * probes


def paired(count):
    return count & (count - 1) == 0


def source_of(device, step, count):
    return device ^ step if paired(count) else (device - step) % count


def place_of(step, number, count):
    return step ^ number if paired(count) else (number - step) % count


def exchange_order(count):
    return (0, 1, 3, 2) if count == 4 else tuple(range(count))


def everywhere(value, axes, count):
    if count > DIRECT:
        return [lax.all_gather(value, axes, axis=0, tiled=False)]
    return [value] + [
        lax.ppermute(value, axes, [(source_of(i, step, count), i) for i in range(count)])
        for step in range(1, count)
    ]


def along_line(value, line_count, sub_count):
    if line_count > DIRECT or sub_count != 2:
        return everywhere(value, LINE, line_count)
    blocks = [value]
    for step in range(1, line_count):
        pairs = [
            (2 * source_of(place, step, line_count) + 1 - core, 2 * place + core)
            for place in range(line_count)
            for core in range(2)
        ]
        blocks.append(lax.ppermute(value, LINE + ("sub",), pairs))
    return blocks


def plane_blocks(value, shape):
    grp_count, sub_count = shape
    if sub_count != 2 or not paired(grp_count):
        return everywhere(value, PLANE, grp_count * sub_count)
    blocks = everywhere(value, ("sub",), sub_count)
    moved = [everywhere(block, ("grp",), grp_count) for block in blocks]
    return [moved[sub][grp] for grp in range(grp_count) for sub in range(sub_count)]


def make_local(plane_shape, line_count):
    plane_count = plane_shape[0] * plane_shape[1]

    def local(features, lengthscale, noise_var, probes):
        feature_count, width = features.shape
        probe_count = probes.shape[0]
        scaled = (features.astype(jnp.float32) / lengthscale[:, None]).astype(jnp.bfloat16)
        line = pl.pallas_call(
            pack_kernel,
            out_shape=jax.ShapeDtypeStruct((feature_count + probe_count, width), jnp.bfloat16),
            compiler_params=VMEM,
        )(scaled, probes)
        lines = along_line(line, line_count, plane_shape[1])
        planes = plane_blocks(scaled, plane_shape)
        early, late = lines[:1] + lines[2:], lines[1:2]
        partial_shape = jax.ShapeDtypeStruct((plane_count + 1, probe_count, width), jnp.float32)
        partial = pl.pallas_call(
            lambda *refs: image_kernel(feature_count, plane_count, *refs),
            out_shape=partial_shape,
            compiler_params=VMEM,
            cost_estimate=pl.CostEstimate(
                flops=2 * plane_count * len(early) * width * width * (feature_count + probe_count),
                bytes_accessed=4 * width * plane_count * feature_count,
                transcendentals=plane_count * len(early) * width * width,
            ),
        )(*planes, *early, noise_var[None, :], probes)
        for block in late:
            partial = pl.pallas_call(
                lambda *refs: add_kernel(feature_count, plane_count, *refs),
                out_shape=partial_shape,
                compiler_params=VMEM,
            )(*planes, block, partial)
        partials = everywhere(partial, PLANE, plane_count)
        image, sums = pl.pallas_call(
            lambda *refs: combine_kernel(plane_count, *refs),
            out_shape=(
                jax.ShapeDtypeStruct(probes.shape, jnp.float32),
                jax.ShapeDtypeStruct((probe_count, 128), jnp.float32),
            ),
            compiler_params=VMEM,
        )(*[partials[number] for number in exchange_order(plane_count)])
        outs = (jax.ShapeDtypeStruct(probes.shape, jnp.float32),) * 3
        return pl.pallas_call(finish_kernel, out_shape=outs, compiler_params=VMEM)(
            image, probes, *along_line(sums, line_count, plane_shape[1])
        )

    return local


def solution(mesh):
    plane_shape = (mesh.shape["grp"], mesh.shape["sub"])
    spread = P(None, ("parts", "blk", "grp", "sub"))
    return jax.shard_map(
        make_local(plane_shape, mesh.shape["blk"]),
        mesh=mesh,
        in_specs=(spread, P("parts"), P(("parts", "blk", "grp", "sub")), spread),
        out_specs=(spread, spread, spread),
        check_vma=False,
    )
```

```python
import jax
import jax.numpy as jnp
from jax import lax
from jax.experimental import pallas as pl
from jax.experimental.pallas import tpu as pltpu
from jax.sharding import PartitionSpec as P

PLANE = ("grp", "sub")
LINE = ("blk",)
DIRECT = 8
VMEM = pltpu.CompilerParams(vmem_limit_bytes=40 * 1024 * 1024)
PARTIALS, PARTIALS_BACK = (0, 2, 3, 1), (0, 3, 1, 2)
SUMS = (0, 1, 3, 2)
HALF = 8


def pieces_of(value):
    pieces = []
    for _ in range(3):
        piece = value.astype(jnp.bfloat16).astype(jnp.float32)
        pieces.append(piece)
        value = value - piece
    return pieces


def norm_rows(scaled, place):
    norms = -0.5 * jnp.sum(jnp.square(scaled.astype(jnp.float32)), axis=0, keepdims=True)
    row = lax.broadcasted_iota(jnp.int32, (2 * HALF, scaled.shape[1]), 0)
    here, there = place * HALF, (1 - place) * HALF
    rows = jnp.where((row >= there) & (row < there + 3), 1.0, 0.0)
    for number, piece in enumerate(pieces_of(norms)):
        rows = jnp.where(row == here + number, piece, rows)
    return rows.astype(jnp.bfloat16)


def pack_kernel(scaled_ref, probes_ref, line_ref):
    line_ref[...] = jnp.concatenate(
        [scaled_ref[...], probes_ref[...].astype(jnp.bfloat16)], axis=0
    )


def columns_of(block, feature_count):
    scaled = block[:feature_count, :]
    columns = jnp.concatenate([scaled, norm_rows(scaled, 0)], axis=0)
    return columns.astype(jnp.float32).T.astype(jnp.bfloat16)


def prepare_kernel(feature_count, plane_count, *refs):
    plane_refs, line_refs = refs[:plane_count], refs[plane_count:-2]
    rows_ref, columns_ref = refs[-2:]
    for number, ref in enumerate(plane_refs):
        rows_ref[number] = jnp.concatenate([ref[...], norm_rows(ref[...], 1)], axis=0)
    for number, ref in enumerate(line_refs):
        columns_ref[number] = columns_of(ref[...], feature_count)


def image_kernel(feature_count, plane_count, *refs):
    rows_ref, noise_ref, probes_ref = refs[:3]
    columns_ref, *line_refs = refs[3:-1]
    partial_ref = refs[-1]
    totals = [noise_ref[...] * probes_ref[...]]
    totals += [jnp.zeros(probes_ref.shape, jnp.float32)] * (plane_count - 1)

    def add_columns(columns, probes, totals):
        result = []
        for number, total in enumerate(totals):
            exponent = jnp.dot(columns, rows_ref[number], preferred_element_type=jnp.float32)
            weights = jnp.exp(exponent).astype(jnp.bfloat16)
            result.append(total + jnp.dot(probes, weights, preferred_element_type=jnp.float32))
        return result

    if len(line_refs[0].shape) == 2:
        *early, late = [ref[...] for ref in line_refs]
        columns = [columns_ref[number] for number in range(len(early))]
        columns = jnp.concatenate(columns + [columns_of(late, feature_count)], axis=0)
        probes = [block[feature_count:, :] for block in early + [late]]
        totals = add_columns(columns, jnp.concatenate(probes, axis=1), totals)
    else:

        def add_block(number, totals):
            block = line_refs[0][number]
            return add_columns(
                columns_of(block, feature_count), block[feature_count:, :], totals
            )

        totals = lax.fori_loop(0, line_refs[0].shape[0], add_block, totals)
    for number, total in enumerate(totals):
        partial_ref[number] = total
    partial_ref[plane_count] = probes_ref[...]


def combine_kernel(plane_count, *refs):
    partial_refs = in_order(refs[:-2], PARTIALS_BACK)
    image_ref, sums_ref = refs[-2:]
    lane = lax.broadcasted_iota(jnp.int32, sums_ref.shape, 1)
    products = [0.0, 0.0, 0.0]
    for number, own_ref in enumerate(partial_refs):
        image = sum(
            ref[place_of(step, number, plane_count)] for step, ref in enumerate(partial_refs)
        )
        if number == 0:
            image_ref[...] = image
        probes = own_ref[plane_count]
        products[0] += probes * probes
        products[1] += probes * image
        products[2] += image * image
    sums = jnp.zeros(sums_ref.shape, jnp.float32)
    for number, product in enumerate(products):
        sums = jnp.where(lane == number, jnp.sum(product, axis=1, keepdims=True), sums)
    sums_ref[...] = sums


def finish_kernel(image_ref, probes_ref, *refs):
    *sums_refs, solution_ref, residual_ref, direction_ref = refs
    sums = jnp.zeros(sums_refs[0].shape[-2:], jnp.float32)
    for ref in sums_refs:
        value = ref[...]
        sums = sums + (value if value.ndim == 2 else jnp.sum(value, axis=0))
    start_norms, curvature, image_norms = sums[:, 0:1], sums[:, 1:2], sums[:, 2:3]
    alpha = start_norms / curvature
    new_norms = start_norms - 2.0 * alpha * curvature + alpha * alpha * image_norms
    probes = probes_ref[...]
    residual = probes - alpha * image_ref[...]
    solution_ref[...] = alpha * probes
    residual_ref[...] = residual
    direction_ref[...] = residual + (new_norms / start_norms) * probes


def paired(count):
    return count & (count - 1) == 0


def source_of(device, step, count):
    return device ^ step if paired(count) else (device - step) % count


def place_of(step, number, count):
    return step ^ number if paired(count) else (number - step) % count


def in_order(blocks, places):
    return [blocks[place] for place in places] if len(blocks) == len(places) else blocks


def everywhere(value, axes, count):
    if count > DIRECT:
        return [lax.all_gather(value, axes, axis=0, tiled=False)]
    return [value] + [
        lax.ppermute(value, axes, [(source_of(i, step, count), i) for i in range(count)])
        for step in range(1, count)
    ]


def along_line(value, line_count, sub_count):
    if line_count > DIRECT or sub_count != 2:
        return everywhere(value, LINE, line_count)
    blocks = [value]
    for step in range(1, line_count):
        pairs = [
            (2 * source_of(place, step, line_count) + 1 - core, 2 * place + core)
            for place in range(line_count)
            for core in range(2)
        ]
        blocks.append(lax.ppermute(value, LINE + ("sub",), pairs))
    return blocks


def plane_blocks(value, shape):
    grp_count, sub_count = shape
    if sub_count != 2 or not paired(grp_count):
        return everywhere(value, PLANE, grp_count * sub_count)
    blocks = everywhere(value, ("sub",), sub_count)
    moved = [everywhere(block, ("grp",), grp_count) for block in blocks]
    return [moved[sub][grp] for grp in range(grp_count) for sub in range(sub_count)]


def make_local(plane_shape, line_count):
    plane_count = plane_shape[0] * plane_shape[1]

    def local(features, lengthscale, noise_var, probes):
        feature_count, width = features.shape
        probe_count = probes.shape[0]
        scaled = (features.astype(jnp.float32) / lengthscale[:, None]).astype(jnp.bfloat16)
        line = pl.pallas_call(
            pack_kernel,
            out_shape=jax.ShapeDtypeStruct((feature_count + probe_count, width), jnp.bfloat16),
            compiler_params=VMEM,
        )(scaled, probes)
        lines = along_line(line, line_count, plane_shape[1])
        planes = plane_blocks(scaled, plane_shape)
        if len(lines) > 1:
            early, late = lines[:1] + lines[:1:-1], lines[1]
        else:
            early, late = [], lines[0]
        depth = feature_count + 2 * HALF
        work = plane_count * width * width
        rows, columns = pl.pallas_call(
            lambda *refs: prepare_kernel(feature_count, plane_count, *refs),
            out_shape=(
                jax.ShapeDtypeStruct((plane_count, depth, width), jnp.bfloat16),
                jax.ShapeDtypeStruct((max(len(early), 1), width, depth), jnp.bfloat16),
            ),
            compiler_params=VMEM,
            cost_estimate=pl.CostEstimate(
                flops=6 * work * depth, bytes_accessed=4 * plane_count * width, transcendentals=3 * work
            ),
        )(*planes, *early)
        partial = pl.pallas_call(
            lambda *refs: image_kernel(feature_count, plane_count, *refs),
            out_shape=jax.ShapeDtypeStruct((plane_count + 1, probe_count, width), jnp.float32),
            compiler_params=VMEM,
        )(rows, noise_var[None, :], probes, columns, *early, late)
        partials = everywhere(partial, PLANE, plane_count)
        image, sums = pl.pallas_call(
            lambda *refs: combine_kernel(plane_count, *refs),
            out_shape=(
                jax.ShapeDtypeStruct(probes.shape, jnp.float32),
                jax.ShapeDtypeStruct((probe_count, 128), jnp.float32),
            ),
            compiler_params=VMEM,
        )(*in_order(partials, PARTIALS))
        outs = (jax.ShapeDtypeStruct(probes.shape, jnp.float32),) * 3
        return pl.pallas_call(finish_kernel, out_shape=outs, compiler_params=VMEM)(
            image, probes, *in_order(along_line(sums, line_count, plane_shape[1]), SUMS)
        )

    return local


def solution(mesh):
    plane_shape = (mesh.shape["grp"], mesh.shape["sub"])
    spread = P(None, ("parts", "blk", "grp", "sub"))
    return jax.shard_map(
        make_local(plane_shape, mesh.shape["blk"]),
        mesh=mesh,
        in_specs=(spread, P("parts"), P(("parts", "blk", "grp", "sub")), spread),
        out_specs=(spread, spread, spread),
        check_vma=False,
    )
```

```python
import jax
import jax.numpy as jnp
from jax import lax
from jax.experimental import pallas as pl
from jax.experimental.pallas import tpu as pltpu
from jax.sharding import PartitionSpec as P

PLANE = ("grp", "sub")
LINE = ("blk",)
DIRECT = 8
VMEM = pltpu.CompilerParams(vmem_limit_bytes=40 * 1024 * 1024)
PARTIALS, PARTIALS_BACK = (0, 2, 3, 1), (0, 3, 1, 2)
SUMS = (0, 1, 3, 2)
HALF = 8


def pieces_of(value):
    pieces = []
    for _ in range(3):
        piece = value.astype(jnp.bfloat16).astype(jnp.float32)
        pieces.append(piece)
        value = value - piece
    return pieces


def norm_rows(scaled, place):
    norms = -0.5 * jnp.sum(jnp.square(scaled.astype(jnp.float32)), axis=0, keepdims=True)
    row = lax.broadcasted_iota(jnp.int32, (2 * HALF, scaled.shape[1]), 0)
    here, there = place * HALF, (1 - place) * HALF
    rows = jnp.where((row >= there) & (row < there + 3), 1.0, 0.0)
    for number, piece in enumerate(pieces_of(norms)):
        rows = jnp.where(row == here + number, piece, rows)
    return rows.astype(jnp.bfloat16)


def pack_kernel(scaled_ref, probes_ref, line_ref):
    line_ref[...] = jnp.concatenate(
        [scaled_ref[...], probes_ref[...].astype(jnp.bfloat16)], axis=0
    )


def columns_of(block, feature_count):
    scaled = block[:feature_count, :]
    columns = jnp.concatenate([scaled, norm_rows(scaled, 0)], axis=0)
    return columns.astype(jnp.float32).T.astype(jnp.bfloat16)


def prepare_kernel(feature_count, plane_count, *refs):
    plane_refs, line_refs = refs[:plane_count], refs[plane_count:-5]
    noise_ref, probes_ref, rows_ref, columns_ref, start_ref = refs[-5:]
    start_ref[...] = noise_ref[...] * probes_ref[...]
    for number, ref in enumerate(plane_refs):
        rows_ref[number] = jnp.concatenate([ref[...], norm_rows(ref[...], 1)], axis=0)
    for number, ref in enumerate(line_refs):
        columns_ref[number] = columns_of(ref[...], feature_count)


def image_kernel(feature_count, plane_count, *refs):
    rows_ref, start_ref, probes_ref = refs[:3]
    columns_ref, *line_refs = refs[3:-1]
    partial_ref = refs[-1]
    totals = [start_ref[...]]
    totals += [jnp.zeros(probes_ref.shape, jnp.float32)] * (plane_count - 1)

    def add_columns(columns, probes, totals):
        result = []
        for number, total in enumerate(totals):
            exponent = jnp.dot(columns, rows_ref[number], preferred_element_type=jnp.float32)
            weights = jnp.exp(exponent).astype(jnp.bfloat16)
            result.append(total + jnp.dot(probes, weights, preferred_element_type=jnp.float32))
        return result

    if len(line_refs[0].shape) == 2:
        *early, late = [ref[...] for ref in line_refs]
        columns = [columns_ref[number] for number in range(len(early))]
        columns = jnp.concatenate(columns + [columns_of(late, feature_count)], axis=0)
        probes = [block[feature_count:, :] for block in early + [late]]
        totals = add_columns(columns, jnp.concatenate(probes, axis=1), totals)
    else:

        def add_block(number, totals):
            block = line_refs[0][number]
            return add_columns(
                columns_of(block, feature_count), block[feature_count:, :], totals
            )

        totals = lax.fori_loop(0, line_refs[0].shape[0], add_block, totals)
    for number, total in enumerate(totals):
        partial_ref[number] = total
    partial_ref[plane_count] = probes_ref[...]


def combine_kernel(plane_count, *refs):
    partial_refs = in_order(refs[:-2], PARTIALS_BACK)
    image_ref, sums_ref = refs[-2:]
    lane = lax.broadcasted_iota(jnp.int32, sums_ref.shape, 1)
    products = [0.0, 0.0, 0.0]
    for number, own_ref in enumerate(partial_refs):
        image = sum(
            ref[place_of(step, number, plane_count)] for step, ref in enumerate(partial_refs)
        )
        if number == 0:
            image_ref[...] = image
        probes = own_ref[plane_count]
        products[0] += probes * probes
        products[1] += probes * image
        products[2] += image * image
    sums = jnp.zeros(sums_ref.shape, jnp.float32)
    for number, product in enumerate(products):
        sums = jnp.where(lane == number, jnp.sum(product, axis=1, keepdims=True), sums)
    sums_ref[...] = sums


def finish_kernel(image_ref, probes_ref, *refs):
    *sums_refs, solution_ref, residual_ref, direction_ref = refs
    sums = jnp.zeros(sums_refs[0].shape[-2:], jnp.float32)
    for ref in sums_refs:
        value = ref[...]
        sums = sums + (value if value.ndim == 2 else jnp.sum(value, axis=0))
    start_norms, curvature, image_norms = sums[:, 0:1], sums[:, 1:2], sums[:, 2:3]
    alpha = start_norms / curvature
    new_norms = start_norms - 2.0 * alpha * curvature + alpha * alpha * image_norms
    probes = probes_ref[...]
    residual = probes - alpha * image_ref[...]
    solution_ref[...] = alpha * probes
    residual_ref[...] = residual
    direction_ref[...] = residual + (new_norms / start_norms) * probes


def paired(count):
    return count & (count - 1) == 0


def source_of(device, step, count):
    return device ^ step if paired(count) else (device - step) % count


def place_of(step, number, count):
    return step ^ number if paired(count) else (number - step) % count


def in_order(blocks, places):
    return [blocks[place] for place in places] if len(blocks) == len(places) else blocks


def everywhere(value, axes, count):
    if count > DIRECT:
        return [lax.all_gather(value, axes, axis=0, tiled=False)]
    return [value] + [
        lax.ppermute(value, axes, [(source_of(i, step, count), i) for i in range(count)])
        for step in range(1, count)
    ]


def along_line(value, line_count, sub_count):
    if line_count > DIRECT or sub_count != 2:
        return everywhere(value, LINE, line_count)
    blocks = [value]
    for step in range(1, line_count):
        pairs = [
            (2 * source_of(place, step, line_count) + 1 - core, 2 * place + core)
            for place in range(line_count)
            for core in range(2)
        ]
        blocks.append(lax.ppermute(value, LINE + ("sub",), pairs))
    return blocks


def plane_blocks(value, shape):
    grp_count, sub_count = shape
    if sub_count != 2 or not paired(grp_count):
        return everywhere(value, PLANE, grp_count * sub_count)
    blocks = everywhere(value, ("sub",), sub_count)
    moved = [everywhere(block, ("grp",), grp_count) for block in blocks]
    return [moved[sub][grp] for grp in range(grp_count) for sub in range(sub_count)]


def make_local(plane_shape, line_count):
    plane_count = plane_shape[0] * plane_shape[1]

    def local(features, lengthscale, noise_var, probes):
        feature_count, width = features.shape
        probe_count = probes.shape[0]
        scaled = (features.astype(jnp.float32) / lengthscale[:, None]).astype(jnp.bfloat16)
        line = pl.pallas_call(
            pack_kernel,
            out_shape=jax.ShapeDtypeStruct((feature_count + probe_count, width), jnp.bfloat16),
            compiler_params=VMEM,
        )(scaled, probes)
        lines = along_line(line, line_count, plane_shape[1])
        planes = plane_blocks(scaled, plane_shape)
        if len(lines) > 1:
            early, late = lines[:1] + lines[:1:-1], lines[1]
        else:
            early, late = [], lines[0]
        depth = feature_count + 2 * HALF
        work = plane_count * width * width
        rows, columns, start = pl.pallas_call(
            lambda *refs: prepare_kernel(feature_count, plane_count, *refs),
            out_shape=(
                jax.ShapeDtypeStruct((plane_count, depth, width), jnp.bfloat16),
                jax.ShapeDtypeStruct((max(len(early), 1), width, depth), jnp.bfloat16),
                jax.ShapeDtypeStruct(probes.shape, jnp.float32),
            ),
            compiler_params=VMEM,
            cost_estimate=pl.CostEstimate(
                flops=6 * work * depth, bytes_accessed=4 * plane_count * width, transcendentals=3 * work
            ),
        )(*planes, *early, noise_var[None, :], probes)
        partial = pl.pallas_call(
            lambda *refs: image_kernel(feature_count, plane_count, *refs),
            out_shape=jax.ShapeDtypeStruct((plane_count + 1, probe_count, width), jnp.float32),
            compiler_params=VMEM,
        )(rows, start, probes, columns, *early, late)
        partials = everywhere(partial, PLANE, plane_count)
        image, sums = pl.pallas_call(
            lambda *refs: combine_kernel(plane_count, *refs),
            out_shape=(
                jax.ShapeDtypeStruct(probes.shape, jnp.float32),
                jax.ShapeDtypeStruct((probe_count, 128), jnp.float32),
            ),
            compiler_params=VMEM,
        )(*in_order(partials, PARTIALS))
        outs = (jax.ShapeDtypeStruct(probes.shape, jnp.float32),) * 3
        return pl.pallas_call(finish_kernel, out_shape=outs, compiler_params=VMEM)(
            image, probes, *in_order(along_line(sums, line_count, plane_shape[1]), SUMS)
        )

    return local


def solution(mesh):
    plane_shape = (mesh.shape["grp"], mesh.shape["sub"])
    spread = P(None, ("parts", "blk", "grp", "sub"))
    return jax.shard_map(
        make_local(plane_shape, mesh.shape["blk"]),
        mesh=mesh,
        in_specs=(spread, P("parts"), P(("parts", "blk", "grp", "sub")), spread),
        out_specs=(spread, spread, spread),
        check_vma=False,
    )
```

```python
import jax
import jax.numpy as jnp
from jax import lax
from jax.experimental import pallas as pl
from jax.experimental.pallas import tpu as pltpu
from jax.sharding import PartitionSpec as P

PLANE = ("grp", "sub")
LINE = ("blk",)
DIRECT = 8
VMEM = pltpu.CompilerParams(vmem_limit_bytes=40 * 1024 * 1024)
PARTIALS, PARTIALS_BACK = (0, 2, 3, 1), (0, 3, 1, 2)
SUMS = (0, 1, 3, 2)
HALF = 8


def pieces_of(value):
    pieces = []
    for _ in range(3):
        piece = value.astype(jnp.bfloat16).astype(jnp.float32)
        pieces.append(piece)
        value = value - piece
    return pieces


def norm_rows(scaled, place):
    norms = -0.5 * jnp.sum(jnp.square(scaled.astype(jnp.float32)), axis=0, keepdims=True)
    row = lax.broadcasted_iota(jnp.int32, (2 * HALF, scaled.shape[1]), 0)
    here, there = place * HALF, (1 - place) * HALF
    rows = jnp.where((row >= there) & (row < there + 3), 1.0, 0.0)
    for number, piece in enumerate(pieces_of(norms)):
        rows = jnp.where(row == here + number, piece, rows)
    return rows.astype(jnp.bfloat16)


def pack_kernel(scaled_ref, probes_ref, line_ref):
    line_ref[...] = jnp.concatenate(
        [scaled_ref[...], probes_ref[...].astype(jnp.bfloat16)], axis=0
    )


def columns_of(block, feature_count):
    scaled = block[:feature_count, :]
    columns = jnp.concatenate([scaled, norm_rows(scaled, 0)], axis=0)
    return columns.astype(jnp.float32).T.astype(jnp.bfloat16)


def prepare_kernel(feature_count, plane_count, *refs):
    plane_refs, line_refs = refs[:plane_count], refs[plane_count:-5]
    noise_ref, probes_ref, rows_ref, columns_ref, start_ref = refs[-5:]
    start_ref[...] = noise_ref[...] * probes_ref[...]
    for number, ref in enumerate(plane_refs):
        rows_ref[number] = jnp.concatenate([ref[...], norm_rows(ref[...], 1)], axis=0)
    for number, ref in enumerate(line_refs):
        columns_ref[number] = columns_of(ref[...], feature_count)


def image_kernel(feature_count, plane_count, *refs):
    rows_ref, start_ref, probes_ref = refs[:3]
    columns_ref, *line_refs = refs[3:-1]
    partial_ref = refs[-1]
    totals = [start_ref[...]]
    totals += [jnp.zeros(probes_ref.shape, jnp.float32)] * (plane_count - 1)

    def add_columns(columns, probes, totals):
        result = []
        for number, total in enumerate(totals):
            exponent = jnp.dot(columns, rows_ref[number], preferred_element_type=jnp.float32)
            weights = jnp.exp(exponent).astype(jnp.bfloat16)
            result.append(total + jnp.dot(probes, weights, preferred_element_type=jnp.float32))
        return result

    if len(line_refs[0].shape) == 2:
        *early, late = [ref[...] for ref in line_refs]
        columns = [columns_ref[number] for number in range(len(early))]
        columns = jnp.concatenate(columns + [columns_of(late, feature_count)], axis=0)
        probes = [block[feature_count:, :] for block in early + [late]]
        totals = add_columns(columns, jnp.concatenate(probes, axis=1), totals)
    else:

        def add_block(number, totals):
            block = line_refs[0][number]
            return add_columns(
                columns_of(block, feature_count), block[feature_count:, :], totals
            )

        totals = lax.fori_loop(0, line_refs[0].shape[0], add_block, totals)
    for number, total in enumerate(totals):
        partial_ref[number] = total
    partial_ref[plane_count] = probes_ref[...]


def combine_kernel(plane_count, *refs):
    partial_refs = in_order(refs[:-2], PARTIALS_BACK)
    image_ref, sums_ref = refs[-2:]
    lane = lax.broadcasted_iota(jnp.int32, sums_ref.shape, 1)
    products = [0.0, 0.0, 0.0]
    for number, own_ref in enumerate(partial_refs):
        image = sum(
            ref[place_of(step, number, plane_count)] for step, ref in enumerate(partial_refs)
        )
        if number == 0:
            image_ref[...] = image
        probes = own_ref[plane_count]
        products[0] += probes * probes
        products[1] += probes * image
        products[2] += image * image
    sums = jnp.zeros(sums_ref.shape, jnp.float32)
    for number, product in enumerate(products):
        sums = jnp.where(lane == number, jnp.sum(product, axis=1, keepdims=True), sums)
    sums_ref[...] = sums


def finish_kernel(image_ref, probes_ref, *refs):
    *sums_refs, solution_ref, residual_ref, direction_ref = refs
    sums = jnp.zeros(sums_refs[0].shape[-2:], jnp.float32)
    for ref in sums_refs:
        value = ref[...]
        sums = sums + (value if value.ndim == 2 else jnp.sum(value, axis=0))
    start_norms, curvature, image_norms = sums[:, 0:1], sums[:, 1:2], sums[:, 2:3]
    alpha = start_norms / curvature
    new_norms = start_norms - 2.0 * alpha * curvature + alpha * alpha * image_norms
    probes = probes_ref[...]
    residual = probes - alpha * image_ref[...]
    solution_ref[...] = alpha * probes
    residual_ref[...] = residual
    direction_ref[...] = residual + (new_norms / start_norms) * probes


def paired(count):
    return count & (count - 1) == 0


def source_of(device, step, count):
    return device ^ step if paired(count) else (device - step) % count


def place_of(step, number, count):
    return step ^ number if paired(count) else (number - step) % count


def in_order(blocks, places):
    return [blocks[place] for place in places] if len(blocks) == len(places) else blocks


def everywhere(value, axes, count):
    if count > DIRECT:
        return [lax.all_gather(value, axes, axis=0, tiled=False)]
    return [value] + [
        lax.ppermute(value, axes, [(source_of(i, step, count), i) for i in range(count)])
        for step in range(1, count)
    ]


def along_line(value, line_count, sub_count):
    if line_count > DIRECT or sub_count != 2:
        return everywhere(value, LINE, line_count)
    blocks = [value]
    for step in range(1, line_count):
        pairs = [
            (2 * source_of(place, step, line_count) + 1 - core, 2 * place + core)
            for place in range(line_count)
            for core in range(2)
        ]
        blocks.append(lax.ppermute(value, LINE + ("sub",), pairs))
    return blocks


def plane_blocks(value, shape):
    grp_count, sub_count = shape
    if sub_count != 2 or not paired(grp_count) or grp_count > DIRECT:
        return everywhere(value, PLANE, grp_count * sub_count)
    own, other = everywhere(value, ("sub",), sub_count)
    blocks = [own, other]
    for step in range(1, grp_count):
        pairs = [
            (2 * (place ^ step) + 1 - core, 2 * place + core)
            for place in range(grp_count)
            for core in range(2)
        ]
        crossed = [lax.ppermute(block, PLANE, pairs) for block in (own, other)]
        blocks += [crossed[1], crossed[0]]
    return blocks


def make_local(plane_shape, line_count):
    plane_count = plane_shape[0] * plane_shape[1]

    def local(features, lengthscale, noise_var, probes):
        feature_count, width = features.shape
        probe_count = probes.shape[0]
        scaled = (features.astype(jnp.float32) / lengthscale[:, None]).astype(jnp.bfloat16)
        line = pl.pallas_call(
            pack_kernel,
            out_shape=jax.ShapeDtypeStruct((feature_count + probe_count, width), jnp.bfloat16),
            compiler_params=VMEM,
        )(scaled, probes)
        lines = along_line(line, line_count, plane_shape[1])
        planes = plane_blocks(scaled, plane_shape)
        if len(lines) > 1:
            early, late = lines[:1] + lines[:1:-1], lines[1]
        else:
            early, late = [], lines[0]
        depth = feature_count + 2 * HALF
        work = plane_count * width * width
        rows, columns, start = pl.pallas_call(
            lambda *refs: prepare_kernel(feature_count, plane_count, *refs),
            out_shape=(
                jax.ShapeDtypeStruct((plane_count, depth, width), jnp.bfloat16),
                jax.ShapeDtypeStruct((max(len(early), 1), width, depth), jnp.bfloat16),
                jax.ShapeDtypeStruct(probes.shape, jnp.float32),
            ),
            compiler_params=VMEM,
            cost_estimate=pl.CostEstimate(
                flops=6 * work * depth, bytes_accessed=4 * plane_count * width, transcendentals=3 * work
            ),
        )(*planes, *early, noise_var[None, :], probes)
        partial = pl.pallas_call(
            lambda *refs: image_kernel(feature_count, plane_count, *refs),
            out_shape=jax.ShapeDtypeStruct((plane_count + 1, probe_count, width), jnp.float32),
            compiler_params=VMEM,
        )(rows, start, probes, columns, *early, late)
        partials = everywhere(partial, PLANE, plane_count)
        image, sums = pl.pallas_call(
            lambda *refs: combine_kernel(plane_count, *refs),
            out_shape=(
                jax.ShapeDtypeStruct(probes.shape, jnp.float32),
                jax.ShapeDtypeStruct((probe_count, 128), jnp.float32),
            ),
            compiler_params=VMEM,
        )(*in_order(partials, PARTIALS))
        outs = (jax.ShapeDtypeStruct(probes.shape, jnp.float32),) * 3
        return pl.pallas_call(finish_kernel, out_shape=outs, compiler_params=VMEM)(
            image, probes, *in_order(along_line(sums, line_count, plane_shape[1]), SUMS)
        )

    return local


def solution(mesh):
    plane_shape = (mesh.shape["grp"], mesh.shape["sub"])
    spread = P(None, ("parts", "blk", "grp", "sub"))
    return jax.shard_map(
        make_local(plane_shape, mesh.shape["blk"]),
        mesh=mesh,
        in_specs=(spread, P("parts"), P(("parts", "blk", "grp", "sub")), spread),
        out_specs=(spread, spread, spread),
        check_vma=False,
    )
```

```python
import jax
import jax.numpy as jnp
from jax import lax
from jax.experimental import pallas as pl
from jax.experimental.pallas import tpu as pltpu
from jax.sharding import PartitionSpec as P

PLANE = ("grp", "sub")
LINE = ("blk",)
DIRECT = 8
VMEM = pltpu.CompilerParams(vmem_limit_bytes=40 * 1024 * 1024)
PARTIALS, PARTIALS_BACK = (0, 1, 3, 2), (0, 1, 3, 2)
SUMS = (0, 1, 2, 3)
HALF = 8


def pieces_of(value):
    pieces = []
    for _ in range(3):
        piece = value.astype(jnp.bfloat16).astype(jnp.float32)
        pieces.append(piece)
        value = value - piece
    return pieces


def norm_rows(scaled, place):
    norms = -0.5 * jnp.sum(jnp.square(scaled.astype(jnp.float32)), axis=0, keepdims=True)
    row = lax.broadcasted_iota(jnp.int32, (2 * HALF, scaled.shape[1]), 0)
    here, there = place * HALF, (1 - place) * HALF
    rows = jnp.where((row >= there) & (row < there + 3), 1.0, 0.0)
    for number, piece in enumerate(pieces_of(norms)):
        rows = jnp.where(row == here + number, piece, rows)
    return rows.astype(jnp.bfloat16)


def pack_kernel(scaled_ref, probes_ref, line_ref, plane_ref):
    high, low, _ = pieces_of(probes_ref[...])
    high, low = high.astype(jnp.bfloat16), low.astype(jnp.bfloat16)
    line_ref[...] = jnp.concatenate([scaled_ref[...], high], axis=0)
    plane_ref[...] = jnp.concatenate([scaled_ref[...], high, low], axis=0)


def columns_of(block, feature_count):
    scaled = block[:feature_count, :]
    columns = jnp.concatenate([scaled, norm_rows(scaled, 0)], axis=0)
    return columns.astype(jnp.float32).T.astype(jnp.bfloat16)


def rows_of(ref, feature_count):
    scaled = ref[:feature_count, :]
    return jnp.concatenate([scaled, norm_rows(scaled, 1)], axis=0)


def prepare_kernel(feature_count, plane_count, *refs):
    plane_refs, line_refs = refs[:plane_count], refs[plane_count:-5]
    noise_ref, probes_ref, rows_ref, columns_ref, start_ref = refs[-5:]
    start_ref[...] = noise_ref[...] * probes_ref[...]
    for number, ref in enumerate(plane_refs):
        rows_ref[number] = rows_of(ref, feature_count)
    for number, ref in enumerate(line_refs):
        columns_ref[number] = columns_of(ref[...], feature_count)


def image_kernel(feature_count, plane_count, *refs):
    rows_ref, start_ref = refs[:2]
    plane_refs = refs[2:plane_count]
    columns_ref, *line_refs = refs[plane_count:-1]
    partial_ref = refs[-1]
    rows = [rows_ref[number] for number in range(2)]
    rows += [rows_of(ref, feature_count) for ref in plane_refs]
    totals = [start_ref[...]]
    totals += [jnp.zeros(start_ref.shape, jnp.float32)] * (plane_count - 1)

    def add_columns(columns, probes, totals):
        result = []
        for own, total in zip(rows, totals):
            exponent = jnp.dot(columns, own, preferred_element_type=jnp.float32)
            weights = jnp.exp(exponent).astype(jnp.bfloat16)
            result.append(total + jnp.dot(probes, weights, preferred_element_type=jnp.float32))
        return result

    if len(line_refs[0].shape) == 2:
        *early, late = [ref[...] for ref in line_refs]
        columns = [columns_ref[number] for number in range(len(early))]
        columns = jnp.concatenate(columns + [columns_of(late, feature_count)], axis=0)
        probes = [block[feature_count:, :] for block in early + [late]]
        totals = add_columns(columns, jnp.concatenate(probes, axis=1), totals)
    else:

        def add_block(number, totals):
            block = line_refs[0][number]
            return add_columns(
                columns_of(block, feature_count), block[feature_count:, :], totals
            )

        totals = lax.fori_loop(0, line_refs[0].shape[0], add_block, totals)
    for number, total in enumerate(totals):
        partial_ref[number] = total


def combine_kernel(feature_count, plane_count, *refs):
    plane_refs, probes_ref = refs[:plane_count], refs[plane_count]
    partial_refs = in_order(refs[plane_count + 1 : -2], PARTIALS_BACK)
    image_ref, sums_ref = refs[-2:]
    probe_count = image_ref.shape[0]
    lane = lax.broadcasted_iota(jnp.int32, sums_ref.shape, 1)
    products = [0.0, 0.0, 0.0]
    for number, plane_ref in enumerate(plane_refs):
        image = sum(
            ref[place_of(step, number, plane_count)] for step, ref in enumerate(partial_refs)
        )
        if number == 0:
            image_ref[...] = image
            probes = probes_ref[...]
        else:
            middle = feature_count + probe_count
            probes = plane_ref[feature_count:middle, :].astype(jnp.float32)
            probes = probes + plane_ref[middle:, :].astype(jnp.float32)
        products[0] += probes * probes
        products[1] += probes * image
        products[2] += image * image
    sums = jnp.zeros(sums_ref.shape, jnp.float32)
    for number, product in enumerate(products):
        sums = jnp.where(lane == number, jnp.sum(product, axis=1, keepdims=True), sums)
    sums_ref[...] = sums


def finish_kernel(image_ref, probes_ref, *refs):
    *sums_refs, solution_ref, residual_ref, direction_ref = refs
    sums = jnp.zeros(sums_refs[0].shape[-2:], jnp.float32)
    for ref in sums_refs:
        value = ref[...]
        sums = sums + (value if value.ndim == 2 else jnp.sum(value, axis=0))
    start_norms, curvature, image_norms = sums[:, 0:1], sums[:, 1:2], sums[:, 2:3]
    alpha = start_norms / curvature
    new_norms = start_norms - 2.0 * alpha * curvature + alpha * alpha * image_norms
    probes = probes_ref[...]
    residual = probes - alpha * image_ref[...]
    solution_ref[...] = alpha * probes
    residual_ref[...] = residual
    direction_ref[...] = residual + (new_norms / start_norms) * probes


def paired(count):
    return count & (count - 1) == 0


def source_of(device, step, count):
    return device ^ step if paired(count) else (device - step) % count


def place_of(step, number, count):
    return step ^ number if paired(count) else (number - step) % count


def in_order(blocks, places):
    return [blocks[place] for place in places] if len(blocks) == len(places) else blocks


def everywhere(value, axes, count):
    if count > DIRECT:
        return [lax.all_gather(value, axes, axis=0, tiled=False)]
    return [value] + [
        lax.ppermute(value, axes, [(source_of(i, step, count), i) for i in range(count)])
        for step in range(1, count)
    ]


def along_line(value, line_count, sub_count):
    if line_count > DIRECT or sub_count != 2:
        return everywhere(value, LINE, line_count)
    blocks = [value]
    for step in range(1, line_count):
        pairs = [
            (2 * source_of(place, step, line_count) + 1 - core, 2 * place + core)
            for place in range(line_count)
            for core in range(2)
        ]
        blocks.append(lax.ppermute(value, LINE + ("sub",), pairs))
    return blocks


def plane_blocks(value, shape):
    grp_count, sub_count = shape
    if sub_count != 2 or not paired(grp_count):
        return everywhere(value, PLANE, grp_count * sub_count)
    blocks = everywhere(value, ("sub",), sub_count)
    moved = [everywhere(block, ("grp",), grp_count) for block in blocks]
    return [moved[sub][grp] for grp in range(grp_count) for sub in range(sub_count)]


def make_local(plane_shape, line_count):
    plane_count = plane_shape[0] * plane_shape[1]

    def local(features, lengthscale, noise_var, probes):
        feature_count, width = features.shape
        probe_count = probes.shape[0]
        scaled = (features.astype(jnp.float32) / lengthscale[:, None]).astype(jnp.bfloat16)
        line, plane = pl.pallas_call(
            pack_kernel,
            out_shape=(
                jax.ShapeDtypeStruct((feature_count + probe_count, width), jnp.bfloat16),
                jax.ShapeDtypeStruct((feature_count + 2 * probe_count, width), jnp.bfloat16),
            ),
            compiler_params=VMEM,
        )(scaled, probes)
        lines = along_line(line, line_count, plane_shape[1])
        planes = plane_blocks(plane, plane_shape)
        if len(lines) > 1:
            early, late = lines[:1] + lines[2:], lines[1]
        else:
            early, late = [], lines[0]
        depth = feature_count + 2 * HALF
        work = plane_count * width * width
        rows, columns, start = pl.pallas_call(
            lambda *refs: prepare_kernel(feature_count, 2, *refs),
            out_shape=(
                jax.ShapeDtypeStruct((2, depth, width), jnp.bfloat16),
                jax.ShapeDtypeStruct((max(len(early), 1), width, depth), jnp.bfloat16),
                jax.ShapeDtypeStruct(probes.shape, jnp.float32),
            ),
            compiler_params=VMEM,
            cost_estimate=pl.CostEstimate(
                flops=6 * work * depth, bytes_accessed=4 * plane_count * width, transcendentals=3 * work
            ),
        )(*planes[:2], *early, noise_var[None, :], probes)
        partial = pl.pallas_call(
            lambda *refs: image_kernel(feature_count, plane_count, *refs),
            out_shape=jax.ShapeDtypeStruct((plane_count, probe_count, width), jnp.float32),
            compiler_params=VMEM,
        )(rows, start, *planes[2:], columns, *early, late)
        partials = everywhere(partial, PLANE, plane_count)
        image, sums = pl.pallas_call(
            lambda *refs: combine_kernel(feature_count, plane_count, *refs),
            out_shape=(
                jax.ShapeDtypeStruct(probes.shape, jnp.float32),
                jax.ShapeDtypeStruct((probe_count, 128), jnp.float32),
            ),
            compiler_params=VMEM,
        )(*planes, probes, *in_order(partials, PARTIALS))
        outs = (jax.ShapeDtypeStruct(probes.shape, jnp.float32),) * 3
        return pl.pallas_call(finish_kernel, out_shape=outs, compiler_params=VMEM)(
            image, probes, *in_order(along_line(sums, line_count, plane_shape[1]), SUMS)
        )

    return local


def solution(mesh):
    plane_shape = (mesh.shape["grp"], mesh.shape["sub"])
    spread = P(None, ("parts", "blk", "grp", "sub"))
    return jax.shard_map(
        make_local(plane_shape, mesh.shape["blk"]),
        mesh=mesh,
        in_specs=(spread, P("parts"), P(("parts", "blk", "grp", "sub")), spread),
        out_specs=(spread, spread, spread),
        check_vma=False,
    )
```

```python
import jax
import jax.numpy as jnp
from jax import lax
from jax.experimental import pallas as pl
from jax.experimental.pallas import tpu as pltpu
from jax.sharding import PartitionSpec as P

PLANE = ("grp", "sub")
LINE = ("blk",)
DIRECT = 8
VMEM = pltpu.CompilerParams(vmem_limit_bytes=40 * 1024 * 1024)
PARTIALS, PARTIALS_BACK = (0, 1, 3, 2), (0, 1, 3, 2)
SUMS = (0, 1, 2, 3)
HALF = 8


def pieces_of(value):
    pieces = []
    for _ in range(3):
        piece = value.astype(jnp.bfloat16).astype(jnp.float32)
        pieces.append(piece)
        value = value - piece
    return pieces


def norm_rows(scaled, place):
    norms = -0.5 * jnp.sum(jnp.square(scaled.astype(jnp.float32)), axis=0, keepdims=True)
    row = lax.broadcasted_iota(jnp.int32, (2 * HALF, scaled.shape[1]), 0)
    here, there = place * HALF, (1 - place) * HALF
    rows = jnp.where((row >= there) & (row < there + 3), 1.0, 0.0)
    for number, piece in enumerate(pieces_of(norms)):
        rows = jnp.where(row == here + number, piece, rows)
    return rows.astype(jnp.bfloat16)


def pack_kernel(scaled_ref, probes_ref, line_ref, plane_ref):
    high, low, _ = pieces_of(probes_ref[...])
    high, low = high.astype(jnp.bfloat16), low.astype(jnp.bfloat16)
    line_ref[...] = jnp.concatenate([scaled_ref[...], high], axis=0)
    plane_ref[...] = jnp.concatenate([scaled_ref[...], high, low], axis=0)


def columns_of(block, feature_count):
    scaled = block[:feature_count, :]
    columns = jnp.concatenate([scaled, norm_rows(scaled, 0)], axis=0)
    return columns.astype(jnp.float32).T.astype(jnp.bfloat16)


def rows_of(ref, feature_count):
    scaled = ref[:feature_count, :]
    return jnp.concatenate([scaled, norm_rows(scaled, 1)], axis=0)


def prepare_kernel(feature_count, plane_count, *refs):
    plane_refs, line_refs = refs[:plane_count], refs[plane_count:-5]
    noise_ref, probes_ref, rows_ref, columns_ref, start_ref = refs[-5:]
    start_ref[...] = noise_ref[...] * probes_ref[...]
    for number, ref in enumerate(plane_refs):
        rows_ref[number] = rows_of(ref, feature_count)
    for number, ref in enumerate(line_refs):
        columns_ref[number] = columns_of(ref[...], feature_count)


def image_kernel(feature_count, plane_count, *refs):
    rows_ref, start_ref = refs[:2]
    plane_refs = refs[2:plane_count]
    columns_ref, *line_refs = refs[plane_count:-1]
    partial_ref = refs[-1]
    rows = [rows_ref[number] for number in range(2)]
    rows += [rows_of(ref, feature_count) for ref in plane_refs]
    start = start_ref[...]
    width = start.shape[1]
    rows = [
        jnp.concatenate(rows[number : number + 2], axis=1) for number in range(0, plane_count, 2)
    ]
    totals = [jnp.zeros((start.shape[0], own.shape[1]), jnp.float32) for own in rows]

    def add_columns(columns, probes, totals):
        exponent = [jnp.dot(columns, own, preferred_element_type=jnp.float32) for own in rows]
        weights = [jnp.exp(value).astype(jnp.bfloat16) for value in exponent]
        return [
            total + jnp.dot(probes, value, preferred_element_type=jnp.float32)
            for total, value in zip(totals, weights)
        ]

    if len(line_refs[0].shape) == 2:
        *early, late = [ref[...] for ref in line_refs]
        columns = [columns_ref[number] for number in range(len(early))]
        columns = jnp.concatenate(columns + [columns_of(late, feature_count)], axis=0)
        probes = [block[feature_count:, :] for block in early + [late]]
        totals = add_columns(columns, jnp.concatenate(probes, axis=1), totals)
    else:

        def add_block(number, totals):
            block = line_refs[0][number]
            return add_columns(
                columns_of(block, feature_count), block[feature_count:, :], totals
            )

        totals = lax.fori_loop(0, line_refs[0].shape[0], add_block, totals)
    for number in range(plane_count):
        place = number % 2 * width
        total = totals[number // 2][:, place : place + width]
        partial_ref[number] = total + start if number == 0 else total


def combine_kernel(feature_count, plane_count, *refs):
    plane_refs, probes_ref = refs[:plane_count], refs[plane_count]
    partial_refs = in_order(refs[plane_count + 1 : -2], PARTIALS_BACK)
    image_ref, sums_ref = refs[-2:]
    probe_count = image_ref.shape[0]
    lane = lax.broadcasted_iota(jnp.int32, sums_ref.shape, 1)
    products = [0.0, 0.0, 0.0]
    for number, plane_ref in enumerate(plane_refs):
        image = sum(
            ref[place_of(step, number, plane_count)] for step, ref in enumerate(partial_refs)
        )
        if number == 0:
            image_ref[...] = image
            probes = probes_ref[...]
        else:
            middle = feature_count + probe_count
            probes = plane_ref[feature_count:middle, :].astype(jnp.float32)
            probes = probes + plane_ref[middle:, :].astype(jnp.float32)
        products[0] += probes * probes
        products[1] += probes * image
        products[2] += image * image
    sums = jnp.zeros(sums_ref.shape, jnp.float32)
    for number, product in enumerate(products):
        sums = jnp.where(lane == number, jnp.sum(product, axis=1, keepdims=True), sums)
    sums_ref[...] = sums


def finish_kernel(image_ref, probes_ref, *refs):
    *sums_refs, solution_ref, residual_ref, direction_ref = refs
    sums = jnp.zeros(sums_refs[0].shape[-2:], jnp.float32)
    for ref in sums_refs:
        value = ref[...]
        sums = sums + (value if value.ndim == 2 else jnp.sum(value, axis=0))
    start_norms, curvature, image_norms = sums[:, 0:1], sums[:, 1:2], sums[:, 2:3]
    alpha = start_norms / curvature
    new_norms = start_norms - 2.0 * alpha * curvature + alpha * alpha * image_norms
    probes = probes_ref[...]
    residual = probes - alpha * image_ref[...]
    solution_ref[...] = alpha * probes
    residual_ref[...] = residual
    direction_ref[...] = residual + (new_norms / start_norms) * probes


def paired(count):
    return count & (count - 1) == 0


def source_of(device, step, count):
    return device ^ step if paired(count) else (device - step) % count


def place_of(step, number, count):
    return step ^ number if paired(count) else (number - step) % count


def in_order(blocks, places):
    return [blocks[place] for place in places] if len(blocks) == len(places) else blocks


def everywhere(value, axes, count):
    if count > DIRECT:
        return [lax.all_gather(value, axes, axis=0, tiled=False)]
    return [value] + [
        lax.ppermute(value, axes, [(source_of(i, step, count), i) for i in range(count)])
        for step in range(1, count)
    ]


def along_line(value, line_count, sub_count):
    if line_count > DIRECT or sub_count != 2:
        return everywhere(value, LINE, line_count)
    blocks = [value]
    for step in range(1, line_count):
        pairs = [
            (2 * source_of(place, step, line_count) + 1 - core, 2 * place + core)
            for place in range(line_count)
            for core in range(2)
        ]
        blocks.append(lax.ppermute(value, LINE + ("sub",), pairs))
    return blocks


def plane_blocks(value, shape):
    grp_count, sub_count = shape
    if sub_count != 2 or not paired(grp_count):
        return everywhere(value, PLANE, grp_count * sub_count)
    blocks = everywhere(value, ("sub",), sub_count)
    moved = [everywhere(block, ("grp",), grp_count) for block in blocks]
    return [moved[sub][grp] for grp in range(grp_count) for sub in range(sub_count)]


def make_local(plane_shape, line_count):
    plane_count = plane_shape[0] * plane_shape[1]

    def local(features, lengthscale, noise_var, probes):
        feature_count, width = features.shape
        probe_count = probes.shape[0]
        scaled = (features.astype(jnp.float32) / lengthscale[:, None]).astype(jnp.bfloat16)
        line, plane = pl.pallas_call(
            pack_kernel,
            out_shape=(
                jax.ShapeDtypeStruct((feature_count + probe_count, width), jnp.bfloat16),
                jax.ShapeDtypeStruct((feature_count + 2 * probe_count, width), jnp.bfloat16),
            ),
            compiler_params=VMEM,
        )(scaled, probes)
        lines = along_line(line, line_count, plane_shape[1])
        planes = plane_blocks(plane, plane_shape)
        if len(lines) > 1:
            early, late = lines[:1] + lines[2:], lines[1]
        else:
            early, late = [], lines[0]
        depth = feature_count + 2 * HALF
        work = plane_count * width * width
        rows, columns, start = pl.pallas_call(
            lambda *refs: prepare_kernel(feature_count, 2, *refs),
            out_shape=(
                jax.ShapeDtypeStruct((2, depth, width), jnp.bfloat16),
                jax.ShapeDtypeStruct((max(len(early), 1), width, depth), jnp.bfloat16),
                jax.ShapeDtypeStruct(probes.shape, jnp.float32),
            ),
            compiler_params=VMEM,
            cost_estimate=pl.CostEstimate(
                flops=6 * work * depth, bytes_accessed=4 * plane_count * width, transcendentals=3 * work
            ),
        )(*planes[:2], *early, noise_var[None, :], probes)
        partial = pl.pallas_call(
            lambda *refs: image_kernel(feature_count, plane_count, *refs),
            out_shape=jax.ShapeDtypeStruct((plane_count, probe_count, width), jnp.float32),
            compiler_params=VMEM,
        )(rows, start, *planes[2:], columns, *early, late)
        partials = everywhere(partial, PLANE, plane_count)
        image, sums = pl.pallas_call(
            lambda *refs: combine_kernel(feature_count, plane_count, *refs),
            out_shape=(
                jax.ShapeDtypeStruct(probes.shape, jnp.float32),
                jax.ShapeDtypeStruct((probe_count, 128), jnp.float32),
            ),
            compiler_params=VMEM,
        )(*planes, probes, *in_order(partials, PARTIALS))
        outs = (jax.ShapeDtypeStruct(probes.shape, jnp.float32),) * 3
        return pl.pallas_call(finish_kernel, out_shape=outs, compiler_params=VMEM)(
            image, probes, *in_order(along_line(sums, line_count, plane_shape[1]), SUMS)
        )

    return local


def solution(mesh):
    plane_shape = (mesh.shape["grp"], mesh.shape["sub"])
    spread = P(None, ("parts", "blk", "grp", "sub"))
    return jax.shard_map(
        make_local(plane_shape, mesh.shape["blk"]),
        mesh=mesh,
        in_specs=(spread, P("parts"), P(("parts", "blk", "grp", "sub")), spread),
        out_specs=(spread, spread, spread),
        check_vma=False,
    )
```

```python
import jax
import jax.numpy as jnp
from jax import lax
from jax.experimental import pallas as pl
from jax.experimental.pallas import tpu as pltpu
from jax.sharding import PartitionSpec as P

PLANE = ("grp", "sub")
LINE = ("blk",)
DIRECT = 8
VMEM = pltpu.CompilerParams(vmem_limit_bytes=40 * 1024 * 1024)
PARTIALS, PARTIALS_BACK = (0, 1, 3, 2), (0, 1, 3, 2)
SUMS = (0, 1, 2, 3)
ABREAST = 4
HALF = 8


def pieces_of(value):
    pieces = []
    for _ in range(3):
        piece = value.astype(jnp.bfloat16).astype(jnp.float32)
        pieces.append(piece)
        value = value - piece
    return pieces


def norm_rows(scaled, place):
    norms = -0.5 * jnp.sum(jnp.square(scaled.astype(jnp.float32)), axis=0, keepdims=True)
    row = lax.broadcasted_iota(jnp.int32, (2 * HALF, scaled.shape[1]), 0)
    here, there = place * HALF, (1 - place) * HALF
    rows = jnp.where((row >= there) & (row < there + 3), 1.0, 0.0)
    for number, piece in enumerate(pieces_of(norms)):
        rows = jnp.where(row == here + number, piece, rows)
    return rows.astype(jnp.bfloat16)


def pack_kernel(scaled_ref, probes_ref, line_ref, plane_ref):
    high, low, _ = pieces_of(probes_ref[...])
    high, low = high.astype(jnp.bfloat16), low.astype(jnp.bfloat16)
    line_ref[...] = jnp.concatenate([scaled_ref[...], high], axis=0)
    plane_ref[...] = jnp.concatenate([scaled_ref[...], high, low], axis=0)


def columns_of(block, feature_count):
    scaled = block[:feature_count, :]
    columns = jnp.concatenate([scaled, norm_rows(scaled, 0)], axis=0)
    return columns.astype(jnp.float32).T.astype(jnp.bfloat16)


def rows_of(ref, feature_count):
    scaled = ref[:feature_count, :]
    return jnp.concatenate([scaled, norm_rows(scaled, 1)], axis=0)


def prepare_kernel(feature_count, plane_count, *refs):
    plane_refs, line_refs = refs[:plane_count], refs[plane_count:-5]
    noise_ref, probes_ref, rows_ref, columns_ref, start_ref = refs[-5:]
    start_ref[...] = noise_ref[...] * probes_ref[...]
    for number, ref in enumerate(plane_refs):
        rows_ref[number] = rows_of(ref, feature_count)
    for number, ref in enumerate(line_refs):
        columns_ref[number] = columns_of(ref[...], feature_count)


def image_kernel(feature_count, plane_count, *refs):
    rows_ref, start_ref = refs[:2]
    plane_refs = refs[2:plane_count]
    columns_ref, *line_refs = refs[plane_count:-1]
    partial_ref = refs[-1]
    rows = [rows_ref[number] for number in range(2)]
    rows += [rows_of(ref, feature_count) for ref in plane_refs]
    start = start_ref[...]
    width = start.shape[1]
    rows = [
        jnp.concatenate(rows[number : number + ABREAST], axis=1)
        for number in range(0, plane_count, ABREAST)
    ]
    totals = [jnp.zeros((start.shape[0], own.shape[1]), jnp.float32) for own in rows]

    def add_columns(columns, probes, totals):
        exponent = [jnp.dot(columns, own, preferred_element_type=jnp.float32) for own in rows]
        weights = [jnp.exp(value).astype(jnp.bfloat16) for value in exponent]
        return [
            total + jnp.dot(probes, value, preferred_element_type=jnp.float32)
            for total, value in zip(totals, weights)
        ]

    if len(line_refs[0].shape) == 2:
        *early, late = [ref[...] for ref in line_refs]
        columns = [columns_ref[number] for number in range(len(early))]
        columns = jnp.concatenate(columns + [columns_of(late, feature_count)], axis=0)
        probes = [block[feature_count:, :] for block in early + [late]]
        totals = add_columns(columns, jnp.concatenate(probes, axis=1), totals)
    else:

        def add_block(number, totals):
            block = line_refs[0][number]
            return add_columns(
                columns_of(block, feature_count), block[feature_count:, :], totals
            )

        totals = lax.fori_loop(0, line_refs[0].shape[0], add_block, totals)
    for number in range(plane_count):
        place = number % ABREAST * width
        total = totals[number // ABREAST][:, place : place + width]
        partial_ref[number] = total + start if number == 0 else total


def combine_kernel(feature_count, plane_count, *refs):
    plane_refs, probes_ref = refs[:plane_count], refs[plane_count]
    partial_refs = in_order(refs[plane_count + 1 : -2], PARTIALS_BACK)
    image_ref, sums_ref = refs[-2:]
    probe_count = image_ref.shape[0]
    lane = lax.broadcasted_iota(jnp.int32, sums_ref.shape, 1)
    products = [0.0, 0.0, 0.0]
    for number, plane_ref in enumerate(plane_refs):
        image = sum(
            ref[place_of(step, number, plane_count)] for step, ref in enumerate(partial_refs)
        )
        if number == 0:
            image_ref[...] = image
            probes = probes_ref[...]
        else:
            middle = feature_count + probe_count
            probes = plane_ref[feature_count:middle, :].astype(jnp.float32)
            probes = probes + plane_ref[middle:, :].astype(jnp.float32)
        products[0] += probes * probes
        products[1] += probes * image
        products[2] += image * image
    sums = jnp.zeros(sums_ref.shape, jnp.float32)
    for number, product in enumerate(products):
        sums = jnp.where(lane == number, jnp.sum(product, axis=1, keepdims=True), sums)
    sums_ref[...] = sums


def finish_kernel(image_ref, probes_ref, *refs):
    *sums_refs, solution_ref, residual_ref, direction_ref = refs
    sums = jnp.zeros(sums_refs[0].shape[-2:], jnp.float32)
    for ref in sums_refs:
        value = ref[...]
        sums = sums + (value if value.ndim == 2 else jnp.sum(value, axis=0))
    start_norms, curvature, image_norms = sums[:, 0:1], sums[:, 1:2], sums[:, 2:3]
    alpha = start_norms / curvature
    new_norms = start_norms - 2.0 * alpha * curvature + alpha * alpha * image_norms
    probes = probes_ref[...]
    residual = probes - alpha * image_ref[...]
    solution_ref[...] = alpha * probes
    residual_ref[...] = residual
    direction_ref[...] = residual + (new_norms / start_norms) * probes


def paired(count):
    return count & (count - 1) == 0


def source_of(device, step, count):
    return device ^ step if paired(count) else (device - step) % count


def place_of(step, number, count):
    return step ^ number if paired(count) else (number - step) % count


def in_order(blocks, places):
    return [blocks[place] for place in places] if len(blocks) == len(places) else blocks


def everywhere(value, axes, count):
    if count > DIRECT:
        return [lax.all_gather(value, axes, axis=0, tiled=False)]
    return [value] + [
        lax.ppermute(value, axes, [(source_of(i, step, count), i) for i in range(count)])
        for step in range(1, count)
    ]


def along_line(value, line_count, sub_count):
    if line_count > DIRECT or sub_count != 2:
        return everywhere(value, LINE, line_count)
    blocks = [value]
    for step in range(1, line_count):
        pairs = [
            (2 * source_of(place, step, line_count) + 1 - core, 2 * place + core)
            for place in range(line_count)
            for core in range(2)
        ]
        blocks.append(lax.ppermute(value, LINE + ("sub",), pairs))
    return blocks


def plane_blocks(value, shape):
    grp_count, sub_count = shape
    if sub_count != 2 or not paired(grp_count):
        return everywhere(value, PLANE, grp_count * sub_count)
    blocks = everywhere(value, ("sub",), sub_count)
    moved = [everywhere(block, ("grp",), grp_count) for block in blocks]
    return [moved[sub][grp] for grp in range(grp_count) for sub in range(sub_count)]


def make_local(plane_shape, line_count):
    plane_count = plane_shape[0] * plane_shape[1]

    def local(features, lengthscale, noise_var, probes):
        feature_count, width = features.shape
        probe_count = probes.shape[0]
        scaled = (features.astype(jnp.float32) / lengthscale[:, None]).astype(jnp.bfloat16)
        line, plane = pl.pallas_call(
            pack_kernel,
            out_shape=(
                jax.ShapeDtypeStruct((feature_count + probe_count, width), jnp.bfloat16),
                jax.ShapeDtypeStruct((feature_count + 2 * probe_count, width), jnp.bfloat16),
            ),
            compiler_params=VMEM,
        )(scaled, probes)
        lines = along_line(line, line_count, plane_shape[1])
        planes = plane_blocks(plane, plane_shape)
        if len(lines) > 1:
            early, late = lines[:1] + lines[2:], lines[1]
        else:
            early, late = [], lines[0]
        depth = feature_count + 2 * HALF
        work = plane_count * width * width
        rows, columns, start = pl.pallas_call(
            lambda *refs: prepare_kernel(feature_count, 2, *refs),
            out_shape=(
                jax.ShapeDtypeStruct((2, depth, width), jnp.bfloat16),
                jax.ShapeDtypeStruct((max(len(early), 1), width, depth), jnp.bfloat16),
                jax.ShapeDtypeStruct(probes.shape, jnp.float32),
            ),
            compiler_params=VMEM,
            cost_estimate=pl.CostEstimate(
                flops=6 * work * depth, bytes_accessed=4 * plane_count * width, transcendentals=3 * work
            ),
        )(*planes[:2], *early, noise_var[None, :], probes)
        partial = pl.pallas_call(
            lambda *refs: image_kernel(feature_count, plane_count, *refs),
            out_shape=jax.ShapeDtypeStruct((plane_count, probe_count, width), jnp.float32),
            compiler_params=VMEM,
        )(rows, start, *planes[2:], columns, *early, late)
        partials = everywhere(partial, PLANE, plane_count)
        image, sums = pl.pallas_call(
            lambda *refs: combine_kernel(feature_count, plane_count, *refs),
            out_shape=(
                jax.ShapeDtypeStruct(probes.shape, jnp.float32),
                jax.ShapeDtypeStruct((probe_count, 128), jnp.float32),
            ),
            compiler_params=VMEM,
        )(*planes, probes, *in_order(partials, PARTIALS))
        outs = (jax.ShapeDtypeStruct(probes.shape, jnp.float32),) * 3
        return pl.pallas_call(finish_kernel, out_shape=outs, compiler_params=VMEM)(
            image, probes, *in_order(along_line(sums, line_count, plane_shape[1]), SUMS)
        )

    return local


def solution(mesh):
    plane_shape = (mesh.shape["grp"], mesh.shape["sub"])
    spread = P(None, ("parts", "blk", "grp", "sub"))
    return jax.shard_map(
        make_local(plane_shape, mesh.shape["blk"]),
        mesh=mesh,
        in_specs=(spread, P("parts"), P(("parts", "blk", "grp", "sub")), spread),
        out_specs=(spread, spread, spread),
        check_vma=False,
    )
```

```python
import jax
import jax.numpy as jnp
from jax import lax
from jax.experimental import pallas as pl
from jax.experimental.pallas import tpu as pltpu
from jax.sharding import PartitionSpec as P

PLANE = ("grp", "sub")
LINE = ("blk",)
DIRECT = 8
VMEM = pltpu.CompilerParams(vmem_limit_bytes=40 * 1024 * 1024)
PARTIALS, PARTIALS_BACK = (0, 2, 3, 1), (0, 3, 1, 2)
SUMS = (0, 1, 3, 2)
HALF = 8


def pieces_of(value):
    pieces = []
    for _ in range(3):
        piece = value.astype(jnp.bfloat16).astype(jnp.float32)
        pieces.append(piece)
        value = value - piece
    return pieces


def norm_rows(scaled, place):
    norms = -0.5 * jnp.sum(jnp.square(scaled.astype(jnp.float32)), axis=0, keepdims=True)
    row = lax.broadcasted_iota(jnp.int32, (2 * HALF, scaled.shape[1]), 0)
    here, there = place * HALF, (1 - place) * HALF
    rows = jnp.where((row >= there) & (row < there + 3), 1.0, 0.0)
    for number, piece in enumerate(pieces_of(norms)):
        rows = jnp.where(row == here + number, piece, rows)
    return rows.astype(jnp.bfloat16)


def pack_kernel(scaled_ref, probes_ref, line_ref, plane_ref):
    high, low, _ = pieces_of(probes_ref[...])
    high, low = high.astype(jnp.bfloat16), low.astype(jnp.bfloat16)
    line_ref[...] = jnp.concatenate([scaled_ref[...], high], axis=0)
    plane_ref[...] = jnp.concatenate([scaled_ref[...], high, low], axis=0)


def columns_of(block, feature_count):
    scaled = block[:feature_count, :]
    columns = jnp.concatenate([scaled, norm_rows(scaled, 0)], axis=0)
    return columns.astype(jnp.float32).T.astype(jnp.bfloat16)


def rows_of(ref, feature_count):
    scaled = ref[:feature_count, :]
    return jnp.concatenate([scaled, norm_rows(scaled, 1)], axis=0)


def prepare_kernel(feature_count, plane_count, *refs):
    plane_refs, line_refs = refs[:plane_count], refs[plane_count:-5]
    noise_ref, probes_ref, rows_ref, columns_ref, start_ref = refs[-5:]
    start_ref[...] = noise_ref[...] * probes_ref[...]
    for number, ref in enumerate(plane_refs):
        rows_ref[number] = rows_of(ref, feature_count)
    for number, ref in enumerate(line_refs):
        if len(ref.shape) == 2:
            columns_ref[number] = columns_of(ref[...], feature_count)


def add_columns(columns, probes, rows, totals):
    exponents = [jnp.dot(columns, own, preferred_element_type=jnp.float32) for own in rows]
    weights = [jnp.exp(value).astype(jnp.bfloat16) for value in exponents]
    return [
        total + jnp.dot(probes, value, preferred_element_type=jnp.float32)
        for total, value in zip(totals, weights)
    ]


def paired_rows(rows_ref, plane_refs, feature_count):
    rows = [rows_ref[number] for number in range(2)]
    rows += [rows_of(ref, feature_count) for ref in plane_refs]
    return [jnp.concatenate(rows[place : place + 2], axis=1) for place in range(0, len(rows), 2)]


def paired_totals(ref):
    totals = [ref[number] for number in range(ref.shape[0])]
    return [jnp.concatenate(totals[place : place + 2], axis=1) for place in range(0, len(totals), 2)]


def store_totals(totals, ref):
    width = ref.shape[2]
    for number in range(ref.shape[0]):
        place = number % 2 * width
        ref[number] = totals[number // 2][:, place : place + width]


def image_kernel(feature_count, plane_count, *refs):
    rows_ref, start_ref = refs[:2]
    columns_ref, *line_refs = refs[plane_count:-1]
    partial_ref = refs[-1]
    rows = paired_rows(rows_ref, refs[2:plane_count], feature_count)
    start = start_ref[...]
    none = jnp.zeros_like(start)
    totals = [jnp.concatenate([start, none], axis=1)]
    totals += [jnp.concatenate([none, none], axis=1)] * (len(rows) - 1)
    if len(line_refs[0].shape) == 2:
        columns = [columns_ref[number] for number in range(len(line_refs))]
        probes = [ref[feature_count:, :] for ref in line_refs]
        totals = add_columns(
            jnp.concatenate(columns, axis=0), jnp.concatenate(probes, axis=1), rows, totals
        )
    else:

        def add_block(number, totals):
            block = line_refs[0][number]
            return add_columns(
                columns_of(block, feature_count), block[feature_count:, :], rows, totals
            )

        totals = lax.fori_loop(0, line_refs[0].shape[0], add_block, totals)
    store_totals(totals, partial_ref)


def late_kernel(feature_count, plane_count, *refs):
    rows_ref, start_ref = refs[:2]
    block_ref, partial_ref = refs[plane_count:]
    rows = paired_rows(rows_ref, refs[2:plane_count], feature_count)
    block = block_ref[...]
    totals = add_columns(
        columns_of(block, feature_count),
        block[feature_count:, :],
        rows,
        paired_totals(start_ref),
    )
    store_totals(totals, partial_ref)


def combine_kernel(feature_count, plane_count, *refs):
    plane_refs, probes_ref = refs[:plane_count], refs[plane_count]
    partial_refs = in_order(refs[plane_count + 1 : -2], PARTIALS_BACK)
    image_ref, sums_ref = refs[-2:]
    probe_count = image_ref.shape[0]
    lane = lax.broadcasted_iota(jnp.int32, sums_ref.shape, 1)
    products = [0.0, 0.0, 0.0]
    for number, plane_ref in enumerate(plane_refs):
        image = sum(
            ref[place_of(step, number, plane_count)] for step, ref in enumerate(partial_refs)
        )
        if number == 0:
            image_ref[...] = image
            probes = probes_ref[...]
        else:
            middle = feature_count + probe_count
            probes = plane_ref[feature_count:middle, :].astype(jnp.float32)
            probes = probes + plane_ref[middle:, :].astype(jnp.float32)
        products[0] += probes * probes
        products[1] += probes * image
        products[2] += image * image
    sums = jnp.zeros(sums_ref.shape, jnp.float32)
    for number, product in enumerate(products):
        sums = jnp.where(lane == number, jnp.sum(product, axis=1, keepdims=True), sums)
    sums_ref[...] = sums


def finish_kernel(image_ref, probes_ref, *refs):
    *sums_refs, solution_ref, residual_ref, direction_ref = refs
    sums = jnp.zeros(sums_refs[0].shape[-2:], jnp.float32)
    for ref in sums_refs:
        value = ref[...]
        sums = sums + (value if value.ndim == 2 else jnp.sum(value, axis=0))
    start_norms, curvature, image_norms = sums[:, 0:1], sums[:, 1:2], sums[:, 2:3]
    alpha = start_norms / curvature
    new_norms = start_norms - 2.0 * alpha * curvature + alpha * alpha * image_norms
    probes = probes_ref[...]
    residual = probes - alpha * image_ref[...]
    solution_ref[...] = alpha * probes
    residual_ref[...] = residual
    direction_ref[...] = residual + (new_norms / start_norms) * probes


def paired(count):
    return count & (count - 1) == 0


def source_of(device, step, count):
    return device ^ step if paired(count) else (device - step) % count


def place_of(step, number, count):
    return step ^ number if paired(count) else (number - step) % count


def in_order(blocks, places):
    return [blocks[place] for place in places] if len(blocks) == len(places) else blocks


def everywhere(value, axes, count):
    if count > DIRECT:
        return [lax.all_gather(value, axes, axis=0, tiled=False)]
    return [value] + [
        lax.ppermute(value, axes, [(source_of(i, step, count), i) for i in range(count)])
        for step in range(1, count)
    ]


def along_line(value, line_count, sub_count):
    if line_count > DIRECT or sub_count != 2:
        return everywhere(value, LINE, line_count)
    blocks = [value]
    for step in range(1, line_count):
        pairs = [
            (2 * source_of(place, step, line_count) + 1 - core, 2 * place + core)
            for place in range(line_count)
            for core in range(2)
        ]
        blocks.append(lax.ppermute(value, LINE + ("sub",), pairs))
    return blocks


def plane_blocks(value, shape):
    grp_count, sub_count = shape
    if sub_count != 2 or not paired(grp_count):
        return everywhere(value, PLANE, grp_count * sub_count)
    blocks = everywhere(value, ("sub",), sub_count)
    moved = [everywhere(block, ("grp",), grp_count) for block in blocks]
    return [moved[sub][grp] for grp in range(grp_count) for sub in range(sub_count)]


def make_local(plane_shape, line_count):
    plane_count = plane_shape[0] * plane_shape[1]

    def local(features, lengthscale, noise_var, probes):
        feature_count, width = features.shape
        probe_count = probes.shape[0]
        scaled = (features.astype(jnp.float32) / lengthscale[:, None]).astype(jnp.bfloat16)
        line, plane = pl.pallas_call(
            pack_kernel,
            out_shape=(
                jax.ShapeDtypeStruct((feature_count + probe_count, width), jnp.bfloat16),
                jax.ShapeDtypeStruct((feature_count + 2 * probe_count, width), jnp.bfloat16),
            ),
            compiler_params=VMEM,
        )(scaled, probes)
        lines = along_line(line, line_count, plane_shape[1])
        planes = plane_blocks(plane, plane_shape)
        if len(lines) > 1:
            early, late = lines[:1] + lines[:1:-1], lines[1:2]
        else:
            early, late = lines, []
        depth = feature_count + 2 * HALF
        work = plane_count * width * width
        rows, columns, start = pl.pallas_call(
            lambda *refs: prepare_kernel(feature_count, 2, *refs),
            out_shape=(
                jax.ShapeDtypeStruct((2, depth, width), jnp.bfloat16),
                jax.ShapeDtypeStruct((len(early), width, depth), jnp.bfloat16),
                jax.ShapeDtypeStruct(probes.shape, jnp.float32),
            ),
            compiler_params=VMEM,
            cost_estimate=pl.CostEstimate(
                flops=6 * work * depth, bytes_accessed=4 * plane_count * width, transcendentals=3 * work
            ),
        )(*planes[:2], *early, noise_var[None, :], probes)
        shape = jax.ShapeDtypeStruct((plane_count, probe_count, width), jnp.float32)
        partial = pl.pallas_call(
            lambda *refs: image_kernel(feature_count, plane_count, *refs),
            out_shape=shape,
            compiler_params=VMEM,
        )(rows, start, *planes[2:], columns, *early)
        for block in late:
            partial = pl.pallas_call(
                lambda *refs: late_kernel(feature_count, plane_count, *refs),
                out_shape=shape,
                compiler_params=VMEM,
            )(rows, partial, *planes[2:], block)
        partials = everywhere(partial, PLANE, plane_count)
        image, sums = pl.pallas_call(
            lambda *refs: combine_kernel(feature_count, plane_count, *refs),
            out_shape=(
                jax.ShapeDtypeStruct(probes.shape, jnp.float32),
                jax.ShapeDtypeStruct((probe_count, 128), jnp.float32),
            ),
            compiler_params=VMEM,
        )(*planes, probes, *in_order(partials, PARTIALS))
        outs = (jax.ShapeDtypeStruct(probes.shape, jnp.float32),) * 3
        return pl.pallas_call(finish_kernel, out_shape=outs, compiler_params=VMEM)(
            image, probes, *in_order(along_line(sums, line_count, plane_shape[1]), SUMS)
        )

    return local


def solution(mesh):
    plane_shape = (mesh.shape["grp"], mesh.shape["sub"])
    spread = P(None, ("parts", "blk", "grp", "sub"))
    return jax.shard_map(
        make_local(plane_shape, mesh.shape["blk"]),
        mesh=mesh,
        in_specs=(spread, P("parts"), P(("parts", "blk", "grp", "sub")), spread),
        out_specs=(spread, spread, spread),
        check_vma=False,
    )
```

```python
import jax
import jax.numpy as jnp
from jax import lax
from jax.experimental import pallas as pl
from jax.experimental.pallas import tpu as pltpu
from jax.sharding import PartitionSpec as P

PLANE = ("grp", "sub")
LINE = ("blk",)
DIRECT = 8
VMEM = pltpu.CompilerParams(vmem_limit_bytes=40 * 1024 * 1024)
PARTIALS, PARTIALS_BACK = (0, 1, 3, 2), (0, 1, 3, 2)
SUMS = (0, 1, 2, 3)
HALF = 8


def pieces_of(value):
    pieces = []
    for _ in range(3):
        piece = value.astype(jnp.bfloat16).astype(jnp.float32)
        pieces.append(piece)
        value = value - piece
    return pieces


def norm_rows(scaled, place):
    norms = -0.5 * jnp.sum(jnp.square(scaled.astype(jnp.float32)), axis=0, keepdims=True)
    row = lax.broadcasted_iota(jnp.int32, (2 * HALF, scaled.shape[1]), 0)
    here, there = place * HALF, (1 - place) * HALF
    rows = jnp.where((row >= there) & (row < there + 3), 1.0, 0.0)
    for number, piece in enumerate(pieces_of(norms)):
        rows = jnp.where(row == here + number, piece, rows)
    return rows.astype(jnp.bfloat16)


def pack_kernel(scaled_ref, probes_ref, line_ref, plane_ref):
    high, low, _ = pieces_of(probes_ref[...])
    high, low = high.astype(jnp.bfloat16), low.astype(jnp.bfloat16)
    line_ref[...] = jnp.concatenate([scaled_ref[...], high], axis=0)
    plane_ref[...] = jnp.concatenate([scaled_ref[...], high, low], axis=0)


def columns_of(block, feature_count):
    scaled = block[:feature_count, :]
    columns = jnp.concatenate([scaled, norm_rows(scaled, 0)], axis=0)
    return columns.astype(jnp.float32).T.astype(jnp.bfloat16)


def rows_of(ref, feature_count):
    scaled = ref[:feature_count, :]
    return jnp.concatenate([scaled, norm_rows(scaled, 1)], axis=0)


def prepare_kernel(feature_count, plane_count, *refs):
    plane_refs, line_refs = refs[:plane_count], refs[plane_count:-5]
    noise_ref, probes_ref, rows_ref, columns_ref, start_ref = refs[-5:]
    start_ref[...] = noise_ref[...] * probes_ref[...]
    for number, ref in enumerate(plane_refs):
        rows_ref[number] = rows_of(ref, feature_count)
    for number, ref in enumerate(line_refs):
        columns_ref[number] = columns_of(ref[...], feature_count)


def image_kernel(feature_count, plane_count, *refs):
    rows_ref, start_ref = refs[:2]
    plane_refs = refs[2:plane_count]
    columns_ref, *line_refs = refs[plane_count:-1]
    partial_ref = refs[-1]
    rows = [rows_ref[number] for number in range(2)]
    rows += [rows_of(ref, feature_count) for ref in plane_refs]
    start = start_ref[...]
    width = start.shape[1]
    rows = [
        jnp.concatenate(rows[number : number + 2], axis=1) for number in range(0, plane_count, 2)
    ]
    totals = [jnp.zeros((start.shape[0], own.shape[1]), jnp.float32) for own in rows]

    def add_columns(columns, probes, totals):
        height = min(512, columns.shape[0])
        for place in range(0, columns.shape[0], height):
            part = columns[place : place + height, :]
            part_probes = probes[:, place : place + height]
            exponents = [jnp.dot(part, own, preferred_element_type=jnp.float32) for own in rows]
            weights = [jnp.exp(value).astype(jnp.bfloat16) for value in exponents]
            totals = [
                total + jnp.dot(part_probes, value, preferred_element_type=jnp.float32)
                for total, value in zip(totals, weights)
            ]
        return totals

    if len(line_refs[0].shape) == 2:
        *early, late = [ref[...] for ref in line_refs]
        columns = [columns_ref[number] for number in range(len(early))]
        columns = jnp.concatenate(columns + [columns_of(late, feature_count)], axis=0)
        probes = [block[feature_count:, :] for block in early + [late]]
        totals = add_columns(columns, jnp.concatenate(probes, axis=1), totals)
    else:

        def add_block(number, totals):
            block = line_refs[0][number]
            return add_columns(
                columns_of(block, feature_count), block[feature_count:, :], totals
            )

        totals = lax.fori_loop(0, line_refs[0].shape[0], add_block, totals)
    for number in range(plane_count):
        place = number % 2 * width
        total = totals[number // 2][:, place : place + width]
        partial_ref[number] = total + start if number == 0 else total


def combine_kernel(feature_count, plane_count, *refs):
    plane_refs, probes_ref = refs[:plane_count], refs[plane_count]
    partial_refs = in_order(refs[plane_count + 1 : -2], PARTIALS_BACK)
    image_ref, sums_ref = refs[-2:]
    probe_count = image_ref.shape[0]
    lane = lax.broadcasted_iota(jnp.int32, sums_ref.shape, 1)
    products = [0.0, 0.0, 0.0]
    for number, plane_ref in enumerate(plane_refs):
        image = sum(
            ref[place_of(step, number, plane_count)] for step, ref in enumerate(partial_refs)
        )
        if number == 0:
            image_ref[...] = image
            probes = probes_ref[...]
        else:
            middle = feature_count + probe_count
            probes = plane_ref[feature_count:middle, :].astype(jnp.float32)
            probes = probes + plane_ref[middle:, :].astype(jnp.float32)
        products[0] += probes * probes
        products[1] += probes * image
        products[2] += image * image
    sums = jnp.zeros(sums_ref.shape, jnp.float32)
    for number, product in enumerate(products):
        sums = jnp.where(lane == number, jnp.sum(product, axis=1, keepdims=True), sums)
    sums_ref[...] = sums


def finish_kernel(image_ref, probes_ref, *refs):
    *sums_refs, solution_hbm, residual_hbm, direction_hbm = refs[:-4]
    solution_ref, residual_ref, direction_ref, semaphores = refs[-4:]
    sums = jnp.zeros(sums_refs[0].shape[-2:], jnp.float32)
    for ref in sums_refs:
        value = ref[...]
        sums = sums + (value if value.ndim == 2 else jnp.sum(value, axis=0))
    start_norms, curvature, image_norms = sums[:, 0:1], sums[:, 1:2], sums[:, 2:3]
    alpha = start_norms / curvature
    new_norms = start_norms - 2.0 * alpha * curvature + alpha * alpha * image_norms
    probes = probes_ref[...]
    copies = [
        pltpu.make_async_copy(source, target, semaphores.at[number])
        for number, (source, target) in enumerate(
            (
                (solution_ref, solution_hbm),
                (residual_ref, residual_hbm),
                (direction_ref, direction_hbm),
            )
        )
    ]
    solution_ref[...] = alpha * probes
    copies[0].start()
    residual = probes - alpha * image_ref[...]
    residual_ref[...] = residual
    copies[1].start()
    direction_ref[...] = residual + (new_norms / start_norms) * probes
    copies[2].start()
    for copy in copies:
        copy.wait()


def paired(count):
    return count & (count - 1) == 0


def source_of(device, step, count):
    return device ^ step if paired(count) else (device - step) % count


def place_of(step, number, count):
    return step ^ number if paired(count) else (number - step) % count


def in_order(blocks, places):
    return [blocks[place] for place in places] if len(blocks) == len(places) else blocks


def everywhere(value, axes, count):
    if count > DIRECT:
        return [lax.all_gather(value, axes, axis=0, tiled=False)]
    return [value] + [
        lax.ppermute(value, axes, [(source_of(i, step, count), i) for i in range(count)])
        for step in range(1, count)
    ]


def along_line(value, line_count, sub_count):
    if line_count > DIRECT or sub_count != 2:
        return everywhere(value, LINE, line_count)
    blocks = [value]
    for step in range(1, line_count):
        pairs = [
            (2 * source_of(place, step, line_count) + 1 - core, 2 * place + core)
            for place in range(line_count)
            for core in range(2)
        ]
        blocks.append(lax.ppermute(value, LINE + ("sub",), pairs))
    return blocks


def plane_blocks(value, shape):
    grp_count, sub_count = shape
    if sub_count != 2 or not paired(grp_count):
        return everywhere(value, PLANE, grp_count * sub_count)
    blocks = everywhere(value, ("sub",), sub_count)
    moved = [everywhere(block, ("grp",), grp_count) for block in blocks]
    return [moved[sub][grp] for grp in range(grp_count) for sub in range(sub_count)]


def make_local(plane_shape, line_count):
    plane_count = plane_shape[0] * plane_shape[1]

    def local(features, lengthscale, noise_var, probes):
        feature_count, width = features.shape
        probe_count = probes.shape[0]
        scaled = (features.astype(jnp.float32) / lengthscale[:, None]).astype(jnp.bfloat16)
        line, plane = pl.pallas_call(
            pack_kernel,
            out_shape=(
                jax.ShapeDtypeStruct((feature_count + probe_count, width), jnp.bfloat16),
                jax.ShapeDtypeStruct((feature_count + 2 * probe_count, width), jnp.bfloat16),
            ),
            compiler_params=VMEM,
        )(scaled, probes)
        lines = along_line(line, line_count, plane_shape[1])
        planes = plane_blocks(plane, plane_shape)
        if len(lines) > 1:
            early, late = lines[:1] + lines[2:], lines[1]
        else:
            early, late = [], lines[0]
        depth = feature_count + 2 * HALF
        work = plane_count * width * width
        rows, columns, start = pl.pallas_call(
            lambda *refs: prepare_kernel(feature_count, 2, *refs),
            out_shape=(
                jax.ShapeDtypeStruct((2, depth, width), jnp.bfloat16),
                jax.ShapeDtypeStruct((max(len(early), 1), width, depth), jnp.bfloat16),
                jax.ShapeDtypeStruct(probes.shape, jnp.float32),
            ),
            compiler_params=VMEM,
            cost_estimate=pl.CostEstimate(
                flops=6 * work * depth, bytes_accessed=4 * plane_count * width, transcendentals=3 * work
            ),
        )(*planes[:2], *early, noise_var[None, :], probes)
        partial = pl.pallas_call(
            lambda *refs: image_kernel(feature_count, plane_count, *refs),
            out_shape=jax.ShapeDtypeStruct((plane_count, probe_count, width), jnp.float32),
            compiler_params=VMEM,
        )(rows, start, *planes[2:], columns, *early, late)
        partials = everywhere(partial, PLANE, plane_count)
        image, sums = pl.pallas_call(
            lambda *refs: combine_kernel(feature_count, plane_count, *refs),
            out_shape=(
                jax.ShapeDtypeStruct(probes.shape, jnp.float32),
                jax.ShapeDtypeStruct((probe_count, 128), jnp.float32),
            ),
            compiler_params=VMEM,
        )(*planes, probes, *in_order(partials, PARTIALS))
        outs = (jax.ShapeDtypeStruct(probes.shape, jnp.float32),) * 3
        return pl.pallas_call(
            finish_kernel,
            out_shape=outs,
            out_specs=(pl.BlockSpec(memory_space=pl.ANY),) * 3,
            scratch_shapes=[
                *[pltpu.VMEM(probes.shape, jnp.float32)] * 3,
                pltpu.SemaphoreType.DMA((3,)),
            ],
            compiler_params=VMEM,
        )(
            image, probes, *in_order(along_line(sums, line_count, plane_shape[1]), SUMS)
        )

    return local


def solution(mesh):
    plane_shape = (mesh.shape["grp"], mesh.shape["sub"])
    spread = P(None, ("parts", "blk", "grp", "sub"))
    return jax.shard_map(
        make_local(plane_shape, mesh.shape["blk"]),
        mesh=mesh,
        in_specs=(spread, P("parts"), P(("parts", "blk", "grp", "sub")), spread),
        out_specs=(spread, spread, spread),
        check_vma=False,
    )
```

```python
import jax
import jax.numpy as jnp
from jax import lax
from jax.experimental import pallas as pl
from jax.experimental.pallas import tpu as pltpu
from jax.sharding import PartitionSpec as P

PLANE = ("grp", "sub")
LINE = ("blk",)
DIRECT = 8
VMEM = pltpu.CompilerParams(vmem_limit_bytes=40 * 1024 * 1024)
PARTIALS, PARTIALS_BACK = (0, 1, 3, 2), (0, 1, 3, 2)
SUMS = (0, 1, 2, 3)
HALF = 8


def pieces_of(value):
    pieces = []
    for _ in range(3):
        piece = value.astype(jnp.bfloat16).astype(jnp.float32)
        pieces.append(piece)
        value = value - piece
    return pieces


def norm_rows(scaled, place):
    norms = -0.5 * jnp.sum(jnp.square(scaled.astype(jnp.float32)), axis=0, keepdims=True)
    row = lax.broadcasted_iota(jnp.int32, (2 * HALF, scaled.shape[1]), 0)
    here, there = place * HALF, (1 - place) * HALF
    rows = jnp.where((row >= there) & (row < there + 3), 1.0, 0.0)
    for number, piece in enumerate(pieces_of(norms)):
        rows = jnp.where(row == here + number, piece, rows)
    return rows.astype(jnp.bfloat16)


def pack_kernel(scaled_ref, probes_ref, line_ref, plane_ref, across_ref):
    high, low, _ = pieces_of(probes_ref[...])
    high, low = high.astype(jnp.bfloat16), low.astype(jnp.bfloat16)
    line_ref[...] = jnp.concatenate([scaled_ref[...], high], axis=0)
    plane_ref[...] = jnp.concatenate([scaled_ref[...], high, low], axis=0)
    norms = norm_rows(scaled_ref[...], 1)
    across_ref[...] = jnp.concatenate([scaled_ref[...], high, low, norms], axis=0)


def columns_of(block, feature_count):
    scaled = block[:feature_count, :]
    columns = jnp.concatenate([scaled, norm_rows(scaled, 0)], axis=0)
    return columns.astype(jnp.float32).T.astype(jnp.bfloat16)


def rows_of(ref, feature_count):
    scaled = ref[:feature_count, :]
    return jnp.concatenate([scaled, norm_rows(scaled, 1)], axis=0)


def prepare_kernel(feature_count, plane_count, *refs):
    plane_refs, line_refs = refs[:plane_count], refs[plane_count:-5]
    noise_ref, probes_ref, rows_ref, columns_ref, start_ref = refs[-5:]
    start_ref[...] = noise_ref[...] * probes_ref[...]
    for number, ref in enumerate(plane_refs):
        rows_ref[number] = rows_of(ref, feature_count)
    for number, ref in enumerate(line_refs):
        columns_ref[number] = columns_of(ref[...], feature_count)


def image_kernel(feature_count, plane_count, *refs):
    rows_ref, start_ref = refs[:2]
    plane_refs = refs[2:plane_count]
    columns_ref, *line_refs = refs[plane_count:-1]
    partial_ref = refs[-1]
    rows = [rows_ref[number] for number in range(2)]
    for number, ref in enumerate(plane_refs):
        norms = ref[-2 * HALF :, :] if number % 2 == 0 else norm_rows(ref[:feature_count, :], 1)
        rows.append(jnp.concatenate([ref[:feature_count, :], norms], axis=0))
    start = start_ref[...]
    width = start.shape[1]
    rows = [
        jnp.concatenate(rows[number : number + 2], axis=1) for number in range(0, plane_count, 2)
    ]
    totals = [jnp.zeros((start.shape[0], own.shape[1]), jnp.float32) for own in rows]

    def add_columns(columns, probes, totals):
        exponent = [jnp.dot(columns, own, preferred_element_type=jnp.float32) for own in rows]
        weights = [jnp.exp(value).astype(jnp.bfloat16) for value in exponent]
        return [
            total + jnp.dot(probes, value, preferred_element_type=jnp.float32)
            for total, value in zip(totals, weights)
        ]

    if len(line_refs[0].shape) == 2:
        *early, late = [ref[...] for ref in line_refs]
        columns = [columns_ref[number] for number in range(len(early))]
        columns = jnp.concatenate(columns + [columns_of(late, feature_count)], axis=0)
        probes = [block[feature_count:, :] for block in early + [late]]
        totals = add_columns(columns, jnp.concatenate(probes, axis=1), totals)
    else:

        def add_block(number, totals):
            block = line_refs[0][number]
            return add_columns(
                columns_of(block, feature_count), block[feature_count:, :], totals
            )

        totals = lax.fori_loop(0, line_refs[0].shape[0], add_block, totals)
    for number in range(plane_count):
        place = number % 2 * width
        total = totals[number // 2][:, place : place + width]
        partial_ref[number] = total + start if number == 0 else total


def combine_kernel(feature_count, plane_count, *refs):
    plane_refs, probes_ref = refs[:plane_count], refs[plane_count]
    partial_refs = in_order(refs[plane_count + 1 : -2], PARTIALS_BACK)
    image_ref, sums_ref = refs[-2:]
    probe_count = image_ref.shape[0]
    lane = lax.broadcasted_iota(jnp.int32, sums_ref.shape, 1)
    products = [0.0, 0.0, 0.0]
    for number, plane_ref in enumerate(plane_refs):
        image = sum(
            ref[place_of(step, number, plane_count)] for step, ref in enumerate(partial_refs)
        )
        if number == 0:
            image_ref[...] = image
            probes = probes_ref[...]
        else:
            middle = feature_count + probe_count
            probes = plane_ref[feature_count:middle, :].astype(jnp.float32)
            low = plane_ref[middle : middle + probe_count, :]
            probes = probes + low.astype(jnp.float32)
        products[0] += probes * probes
        products[1] += probes * image
        products[2] += image * image
    sums = jnp.zeros(sums_ref.shape, jnp.float32)
    for number, product in enumerate(products):
        sums = jnp.where(lane == number, jnp.sum(product, axis=1, keepdims=True), sums)
    sums_ref[...] = sums


def finish_kernel(image_ref, probes_ref, *refs):
    *sums_refs, solution_ref, residual_ref, direction_ref = refs
    sums = jnp.zeros(sums_refs[0].shape[-2:], jnp.float32)
    for ref in sums_refs:
        value = ref[...]
        sums = sums + (value if value.ndim == 2 else jnp.sum(value, axis=0))
    start_norms, curvature, image_norms = sums[:, 0:1], sums[:, 1:2], sums[:, 2:3]
    alpha = start_norms / curvature
    new_norms = start_norms - 2.0 * alpha * curvature + alpha * alpha * image_norms
    probes = probes_ref[...]
    residual = probes - alpha * image_ref[...]
    solution_ref[...] = alpha * probes
    residual_ref[...] = residual
    direction_ref[...] = residual + (new_norms / start_norms) * probes


def paired(count):
    return count & (count - 1) == 0


def source_of(device, step, count):
    return device ^ step if paired(count) else (device - step) % count


def place_of(step, number, count):
    return step ^ number if paired(count) else (number - step) % count


def in_order(blocks, places):
    return [blocks[place] for place in places] if len(blocks) == len(places) else blocks


def everywhere(value, axes, count):
    if count > DIRECT:
        return [lax.all_gather(value, axes, axis=0, tiled=False)]
    return [value] + [
        lax.ppermute(value, axes, [(source_of(i, step, count), i) for i in range(count)])
        for step in range(1, count)
    ]


def along_line(value, line_count, sub_count):
    if line_count > DIRECT or sub_count != 2:
        return everywhere(value, LINE, line_count)
    blocks = [value]
    for step in range(1, line_count):
        pairs = [
            (2 * source_of(place, step, line_count) + 1 - core, 2 * place + core)
            for place in range(line_count)
            for core in range(2)
        ]
        blocks.append(lax.ppermute(value, LINE + ("sub",), pairs))
    return blocks


def plane_blocks(value, across, shape):
    grp_count, sub_count = shape
    if sub_count != 2 or not paired(grp_count):
        return everywhere(value, PLANE, grp_count * sub_count)
    own, other = everywhere(value, ("sub",), sub_count)
    near = everywhere(across, ("grp",), grp_count)
    far = everywhere(other, ("grp",), grp_count)
    blocks = [own, other]
    for grp in range(1, grp_count):
        blocks += [near[grp], far[grp]]
    return blocks


def make_local(plane_shape, line_count):
    plane_count = plane_shape[0] * plane_shape[1]

    def local(features, lengthscale, noise_var, probes):
        feature_count, width = features.shape
        probe_count = probes.shape[0]
        scaled = (features.astype(jnp.float32) / lengthscale[:, None]).astype(jnp.bfloat16)
        line, plane, across = pl.pallas_call(
            pack_kernel,
            out_shape=(
                jax.ShapeDtypeStruct((feature_count + probe_count, width), jnp.bfloat16),
                jax.ShapeDtypeStruct((feature_count + 2 * probe_count, width), jnp.bfloat16),
                jax.ShapeDtypeStruct(
                    (feature_count + 2 * probe_count + 2 * HALF, width), jnp.bfloat16
                ),
            ),
            compiler_params=VMEM,
        )(scaled, probes)
        lines = along_line(line, line_count, plane_shape[1])
        planes = plane_blocks(plane, across, plane_shape)
        if len(lines) > 1:
            early, late = lines[:1] + lines[2:], lines[1]
        else:
            early, late = [], lines[0]
        depth = feature_count + 2 * HALF
        work = plane_count * width * width
        rows, columns, start = pl.pallas_call(
            lambda *refs: prepare_kernel(feature_count, 2, *refs),
            out_shape=(
                jax.ShapeDtypeStruct((2, depth, width), jnp.bfloat16),
                jax.ShapeDtypeStruct((max(len(early), 1), width, depth), jnp.bfloat16),
                jax.ShapeDtypeStruct(probes.shape, jnp.float32),
            ),
            compiler_params=VMEM,
            cost_estimate=pl.CostEstimate(
                flops=24 * work * depth, bytes_accessed=4 * plane_count * width, transcendentals=12 * work
            ),
        )(*planes[:2], *early, noise_var[None, :], probes)
        partial = pl.pallas_call(
            lambda *refs: image_kernel(feature_count, plane_count, *refs),
            out_shape=jax.ShapeDtypeStruct((plane_count, probe_count, width), jnp.float32),
            compiler_params=VMEM,
        )(rows, start, *planes[2:], columns, *early, late)
        partials = everywhere(partial, PLANE, plane_count)
        image, sums = pl.pallas_call(
            lambda *refs: combine_kernel(feature_count, plane_count, *refs),
            out_shape=(
                jax.ShapeDtypeStruct(probes.shape, jnp.float32),
                jax.ShapeDtypeStruct((probe_count, 128), jnp.float32),
            ),
            compiler_params=VMEM,
        )(*planes, probes, *in_order(partials, PARTIALS))
        outs = (jax.ShapeDtypeStruct(probes.shape, jnp.float32),) * 3
        return pl.pallas_call(finish_kernel, out_shape=outs, compiler_params=VMEM)(
            image, probes, *in_order(along_line(sums, line_count, plane_shape[1]), SUMS)
        )

    return local


def solution(mesh):
    plane_shape = (mesh.shape["grp"], mesh.shape["sub"])
    spread = P(None, ("parts", "blk", "grp", "sub"))
    return jax.shard_map(
        make_local(plane_shape, mesh.shape["blk"]),
        mesh=mesh,
        in_specs=(spread, P("parts"), P(("parts", "blk", "grp", "sub")), spread),
        out_specs=(spread, spread, spread),
        check_vma=False,
    )
```

```python
import jax
import jax.numpy as jnp
from jax import lax
from jax.experimental import pallas as pl
from jax.experimental.pallas import tpu as pltpu
from jax.sharding import PartitionSpec as P

PLANE = ("grp", "sub")
LINE = ("blk",)
DIRECT = 8
VMEM = pltpu.CompilerParams(vmem_limit_bytes=40 * 1024 * 1024)
PARTIALS, PARTIALS_BACK = (0, 1, 3, 2), (0, 1, 3, 2)
SUMS = (0, 1, 2, 3)
HALF = 8


def pieces_of(value):
    pieces = []
    for _ in range(3):
        piece = value.astype(jnp.bfloat16).astype(jnp.float32)
        pieces.append(piece)
        value = value - piece
    return pieces


def norm_rows(scaled, place):
    norms = -0.5 * jnp.sum(jnp.square(scaled.astype(jnp.float32)), axis=0, keepdims=True)
    row = lax.broadcasted_iota(jnp.int32, (2 * HALF, scaled.shape[1]), 0)
    here, there = place * HALF, (1 - place) * HALF
    rows = jnp.where((row >= there) & (row < there + 3), 1.0, 0.0)
    for number, piece in enumerate(pieces_of(norms)):
        rows = jnp.where(row == here + number, piece, rows)
    return rows.astype(jnp.bfloat16)


def pack_kernel(scaled_ref, probes_ref, line_ref, plane_ref):
    high, low, _ = pieces_of(probes_ref[...])
    high, low = high.astype(jnp.bfloat16), low.astype(jnp.bfloat16)
    line_ref[...] = jnp.concatenate([scaled_ref[...], high], axis=0)
    plane_ref[...] = jnp.concatenate([scaled_ref[...], high, low], axis=0)


def columns_of(block, feature_count):
    scaled = block[:feature_count, :]
    columns = jnp.concatenate([scaled, norm_rows(scaled, 0)], axis=0)
    return columns.astype(jnp.float32).T.astype(jnp.bfloat16)


def rows_of(ref, feature_count):
    scaled = ref[:feature_count, :]
    return jnp.concatenate([scaled, norm_rows(scaled, 1)], axis=0)


def product(columns, probes, rows):
    exponent = jnp.dot(columns, rows, preferred_element_type=jnp.float32)
    weights = jnp.exp(exponent).astype(jnp.bfloat16)
    return jnp.dot(probes, weights, preferred_element_type=jnp.float32)


def side_by_side(refs, feature_count):
    return jnp.concatenate([rows_of(ref, feature_count) for ref in refs], axis=1)


def near_kernel(feature_count, *refs):
    plane_refs, line_refs = refs[:2], refs[2:-5]
    noise_ref, probes_ref, rows_ref, columns_ref, total_ref = refs[-5:]
    rows = side_by_side(plane_refs, feature_count)
    rows_ref[...] = rows
    start = noise_ref[...] * probes_ref[...]
    total = jnp.concatenate([start, jnp.zeros_like(start)], axis=1)
    if line_refs:
        columns = [columns_of(ref[...], feature_count) for ref in line_refs]
        for number, value in enumerate(columns):
            columns_ref[number] = value
        probes = jnp.concatenate([ref[feature_count:, :] for ref in line_refs], axis=1)
        total += product(jnp.concatenate(columns, axis=0), probes, rows)
    total_ref[...] = total


def image_kernel(feature_count, plane_count, *refs):
    rows_ref, total_ref = refs[:2]
    plane_refs = refs[2:plane_count]
    columns_ref, *line_refs = refs[plane_count:-1]
    partial_ref = refs[-1]
    width = partial_ref.shape[2]
    rows = [rows_ref[...]]
    for place in range(0, len(plane_refs), 2):
        rows.append(side_by_side(plane_refs[place : place + 2], feature_count))
    totals = [total_ref[...]] + [jnp.zeros(total_ref.shape, jnp.float32)] * (len(rows) - 1)
    if len(line_refs[0].shape) == 2:
        *early, late = [ref[...] for ref in line_refs]
        late_columns = columns_of(late, feature_count)
        columns = [columns_ref[number] for number in range(len(early))]
        columns = jnp.concatenate(columns + [late_columns], axis=0)
        probes = jnp.concatenate([block[feature_count:, :] for block in early + [late]], axis=1)
        near = totals[0] + product(late_columns, late[feature_count:, :], rows[0])
        totals = [near] + [product(columns, probes, pair) for pair in rows[1:]]
    else:

        def add_block(number, totals):
            block = line_refs[0][number]
            columns = columns_of(block, feature_count)
            return [
                total + product(columns, block[feature_count:, :], pair)
                for pair, total in zip(rows, totals)
            ]

        totals = lax.fori_loop(0, line_refs[0].shape[0], add_block, totals)
    for number in range(plane_count):
        place = number % 2 * width
        partial_ref[number] = totals[number // 2][:, place : place + width]


def combine_kernel(feature_count, plane_count, *refs):
    plane_refs, probes_ref = refs[:plane_count], refs[plane_count]
    partial_refs = in_order(refs[plane_count + 1 : -2], PARTIALS_BACK)
    image_ref, sums_ref = refs[-2:]
    probe_count = image_ref.shape[0]
    lane = lax.broadcasted_iota(jnp.int32, sums_ref.shape, 1)
    products = [0.0, 0.0, 0.0]
    for number, plane_ref in enumerate(plane_refs):
        image = sum(
            ref[place_of(step, number, plane_count)] for step, ref in enumerate(partial_refs)
        )
        if number == 0:
            image_ref[...] = image
            probes = probes_ref[...]
        else:
            middle = feature_count + probe_count
            probes = plane_ref[feature_count:middle, :].astype(jnp.float32)
            probes = probes + plane_ref[middle:, :].astype(jnp.float32)
        products[0] += probes * probes
        products[1] += probes * image
        products[2] += image * image
    sums = jnp.zeros(sums_ref.shape, jnp.float32)
    for number, product in enumerate(products):
        sums = jnp.where(lane == number, jnp.sum(product, axis=1, keepdims=True), sums)
    sums_ref[...] = sums


def finish_kernel(image_ref, probes_ref, *refs):
    *sums_refs, solution_ref, residual_ref, direction_ref = refs
    sums = jnp.zeros(sums_refs[0].shape[-2:], jnp.float32)
    for ref in sums_refs:
        value = ref[...]
        sums = sums + (value if value.ndim == 2 else jnp.sum(value, axis=0))
    start_norms, curvature, image_norms = sums[:, 0:1], sums[:, 1:2], sums[:, 2:3]
    alpha = start_norms / curvature
    new_norms = start_norms - 2.0 * alpha * curvature + alpha * alpha * image_norms
    probes = probes_ref[...]
    residual = probes - alpha * image_ref[...]
    solution_ref[...] = alpha * probes
    residual_ref[...] = residual
    direction_ref[...] = residual + (new_norms / start_norms) * probes


def paired(count):
    return count & (count - 1) == 0


def source_of(device, step, count):
    return device ^ step if paired(count) else (device - step) % count


def place_of(step, number, count):
    return step ^ number if paired(count) else (number - step) % count


def in_order(blocks, places):
    return [blocks[place] for place in places] if len(blocks) == len(places) else blocks


def everywhere(value, axes, count):
    if count > DIRECT:
        return [lax.all_gather(value, axes, axis=0, tiled=False)]
    return [value] + [
        lax.ppermute(value, axes, [(source_of(i, step, count), i) for i in range(count)])
        for step in range(1, count)
    ]


def along_line(value, line_count, sub_count):
    if line_count > DIRECT or sub_count != 2:
        return everywhere(value, LINE, line_count)
    blocks = [value]
    for step in range(1, line_count):
        pairs = [
            (2 * source_of(place, step, line_count) + 1 - core, 2 * place + core)
            for place in range(line_count)
            for core in range(2)
        ]
        blocks.append(lax.ppermute(value, LINE + ("sub",), pairs))
    return blocks


def plane_blocks(value, shape):
    grp_count, sub_count = shape
    if sub_count != 2 or not paired(grp_count):
        return everywhere(value, PLANE, grp_count * sub_count)
    blocks = everywhere(value, ("sub",), sub_count)
    moved = [everywhere(block, ("grp",), grp_count) for block in blocks]
    return [moved[sub][grp] for grp in range(grp_count) for sub in range(sub_count)]


def make_local(plane_shape, line_count):
    plane_count = plane_shape[0] * plane_shape[1]

    def local(features, lengthscale, noise_var, probes):
        feature_count, width = features.shape
        probe_count = probes.shape[0]
        scaled = (features.astype(jnp.float32) / lengthscale[:, None]).astype(jnp.bfloat16)
        line, plane = pl.pallas_call(
            pack_kernel,
            out_shape=(
                jax.ShapeDtypeStruct((feature_count + probe_count, width), jnp.bfloat16),
                jax.ShapeDtypeStruct((feature_count + 2 * probe_count, width), jnp.bfloat16),
            ),
            compiler_params=VMEM,
        )(scaled, probes)
        lines = along_line(line, line_count, plane_shape[1])
        planes = plane_blocks(plane, plane_shape)
        if len(lines) > 1:
            early, late = lines[:1] + lines[2:], lines[1]
        else:
            early, late = [], lines[0]
        depth = feature_count + 2 * HALF
        work = plane_count * width * width
        rows, columns, total = pl.pallas_call(
            lambda *refs: near_kernel(feature_count, *refs),
            out_shape=(
                jax.ShapeDtypeStruct((depth, 2 * width), jnp.bfloat16),
                jax.ShapeDtypeStruct((max(len(early), 1), width, depth), jnp.bfloat16),
                jax.ShapeDtypeStruct((probe_count, 2 * width), jnp.float32),
            ),
            compiler_params=VMEM,
            cost_estimate=pl.CostEstimate(
                flops=6 * work * depth, bytes_accessed=4 * plane_count * width, transcendentals=3 * work
            ),
        )(*planes[:2], *early, noise_var[None, :], probes)
        partial = pl.pallas_call(
            lambda *refs: image_kernel(feature_count, plane_count, *refs),
            out_shape=jax.ShapeDtypeStruct((plane_count, probe_count, width), jnp.float32),
            compiler_params=VMEM,
        )(rows, total, *planes[2:], columns, *early, late)
        partials = everywhere(partial, PLANE, plane_count)
        image, sums = pl.pallas_call(
            lambda *refs: combine_kernel(feature_count, plane_count, *refs),
            out_shape=(
                jax.ShapeDtypeStruct(probes.shape, jnp.float32),
                jax.ShapeDtypeStruct((probe_count, 128), jnp.float32),
            ),
            compiler_params=VMEM,
        )(*planes, probes, *in_order(partials, PARTIALS))
        outs = (jax.ShapeDtypeStruct(probes.shape, jnp.float32),) * 3
        return pl.pallas_call(finish_kernel, out_shape=outs, compiler_params=VMEM)(
            image, probes, *in_order(along_line(sums, line_count, plane_shape[1]), SUMS)
        )

    return local


def solution(mesh):
    plane_shape = (mesh.shape["grp"], mesh.shape["sub"])
    spread = P(None, ("parts", "blk", "grp", "sub"))
    return jax.shard_map(
        make_local(plane_shape, mesh.shape["blk"]),
        mesh=mesh,
        in_specs=(spread, P("parts"), P(("parts", "blk", "grp", "sub")), spread),
        out_specs=(spread, spread, spread),
        check_vma=False,
    )
```

```python
import jax
import jax.numpy as jnp
from jax import lax
from jax.experimental import pallas as pl
from jax.experimental.pallas import tpu as pltpu
from jax.sharding import PartitionSpec as P

PLANE = ("grp", "sub")
LINE = ("blk",)
DIRECT = 8
VMEM = pltpu.CompilerParams(vmem_limit_bytes=40 * 1024 * 1024)
PARTIALS, PARTIALS_BACK = (0, 1, 2, 3), (0, 1, 2, 3)
SUMS = (0, 1, 2, 3)
HALF = 8


def pieces_of(value):
    pieces = []
    for _ in range(3):
        piece = value.astype(jnp.bfloat16).astype(jnp.float32)
        pieces.append(piece)
        value = value - piece
    return pieces


def norm_rows(scaled, place):
    norms = -0.5 * jnp.sum(jnp.square(scaled.astype(jnp.float32)), axis=0, keepdims=True)
    row = lax.broadcasted_iota(jnp.int32, (2 * HALF, scaled.shape[1]), 0)
    here, there = place * HALF, (1 - place) * HALF
    rows = jnp.where((row >= there) & (row < there + 3), 1.0, 0.0)
    for number, piece in enumerate(pieces_of(norms)):
        rows = jnp.where(row == here + number, piece, rows)
    return rows.astype(jnp.bfloat16)


def pack_kernel(scaled_ref, probes_ref, line_ref, plane_ref):
    high, low, _ = pieces_of(probes_ref[...])
    high, low = high.astype(jnp.bfloat16), low.astype(jnp.bfloat16)
    line_ref[...] = jnp.concatenate([scaled_ref[...], high], axis=0)
    plane_ref[...] = jnp.concatenate([scaled_ref[...], high, low], axis=0)


def columns_of(block, feature_count):
    scaled = block[:feature_count, :]
    columns = jnp.concatenate([scaled, norm_rows(scaled, 0)], axis=0)
    return columns.astype(jnp.float32).T.astype(jnp.bfloat16)


def rows_of(ref, feature_count):
    scaled = ref[:feature_count, :]
    return jnp.concatenate([scaled, norm_rows(scaled, 1)], axis=0)


def prepare_kernel(feature_count, plane_count, *refs):
    plane_refs, line_refs = refs[:plane_count], refs[plane_count:-5]
    noise_ref, probes_ref, rows_ref, columns_ref, start_ref = refs[-5:]
    start_ref[...] = noise_ref[...] * probes_ref[...]
    for number, ref in enumerate(plane_refs):
        rows_ref[number] = rows_of(ref, feature_count)
    for number, ref in enumerate(line_refs):
        columns_ref[number] = columns_of(ref[...], feature_count)


def image_kernel(feature_count, plane_count, *refs):
    rows_ref, start_ref = refs[:2]
    plane_refs = refs[2:plane_count]
    columns_ref, *line_refs = refs[plane_count:-1]
    partial_ref = refs[-1]
    rows = [rows_ref[number] for number in range(2)]
    rows += [rows_of(ref, feature_count) for ref in plane_refs]
    start = start_ref[...]
    width = start.shape[1]
    rows = [
        jnp.concatenate(rows[number : number + 2], axis=1) for number in range(0, plane_count, 2)
    ]
    totals = [jnp.zeros((start.shape[0], own.shape[1]), jnp.float32) for own in rows]

    def add_columns(columns, probes, totals):
        exponent = [jnp.dot(columns, own, preferred_element_type=jnp.float32) for own in rows]
        weights = [jnp.exp(value).astype(jnp.bfloat16) for value in exponent]
        return [
            total + jnp.dot(probes, value, preferred_element_type=jnp.float32)
            for total, value in zip(totals, weights)
        ]

    if len(line_refs[0].shape) == 2:
        *early, late = [ref[...] for ref in line_refs]
        columns = [columns_ref[number] for number in range(len(early))]
        columns = jnp.concatenate(columns + [columns_of(late, feature_count)], axis=0)
        probes = [block[feature_count:, :] for block in early + [late]]
        totals = add_columns(columns, jnp.concatenate(probes, axis=1), totals)
    else:

        def add_block(number, totals):
            block = line_refs[0][number]
            return add_columns(
                columns_of(block, feature_count), block[feature_count:, :], totals
            )

        totals = lax.fori_loop(0, line_refs[0].shape[0], add_block, totals)
    for number in range(plane_count):
        place = number % 2 * width
        total = totals[number // 2][:, place : place + width]
        partial_ref[number] = total + start if number == 0 else total


def combine_kernel(feature_count, plane_count, *refs):
    plane_refs, probes_ref = refs[:plane_count], refs[plane_count]
    partial_refs = in_order(refs[plane_count + 1 : -2], PARTIALS_BACK)
    image_ref, sums_ref = refs[-2:]
    probe_count = image_ref.shape[0]
    lane = lax.broadcasted_iota(jnp.int32, sums_ref.shape, 1)
    products = [0.0, 0.0, 0.0]
    for number, plane_ref in enumerate(plane_refs):
        image = sum(
            ref[place_of(step, number, plane_count)] for step, ref in enumerate(partial_refs)
        )
        if number == 0:
            image_ref[...] = image
            probes = probes_ref[...]
        else:
            middle = feature_count + probe_count
            probes = plane_ref[feature_count:middle, :].astype(jnp.float32)
            probes = probes + plane_ref[middle:, :].astype(jnp.float32)
        products[0] += probes * probes
        products[1] += probes * image
        products[2] += image * image
    sums = jnp.zeros(sums_ref.shape, jnp.float32)
    for number, product in enumerate(products):
        sums = jnp.where(lane == number, jnp.sum(product, axis=1, keepdims=True), sums)
    sums_ref[...] = sums


def finish_kernel(image_ref, probes_ref, *refs):
    *sums_refs, solution_ref, residual_ref, direction_ref = refs
    sums = jnp.zeros(sums_refs[0].shape[-2:], jnp.float32)
    for ref in sums_refs:
        value = ref[...]
        sums = sums + (value if value.ndim == 2 else jnp.sum(value, axis=0))
    start_norms, curvature, image_norms = sums[:, 0:1], sums[:, 1:2], sums[:, 2:3]
    alpha = start_norms / curvature
    new_norms = start_norms - 2.0 * alpha * curvature + alpha * alpha * image_norms
    probes = probes_ref[...]
    residual = probes - alpha * image_ref[...]
    solution_ref[...] = alpha * probes
    residual_ref[...] = residual
    direction_ref[...] = residual + (new_norms / start_norms) * probes


def paired(count):
    return count & (count - 1) == 0


def source_of(device, step, count):
    return device ^ step if paired(count) else (device - step) % count


def place_of(step, number, count):
    return step ^ number if paired(count) else (number - step) % count


def in_order(blocks, places):
    return [blocks[place] for place in places] if len(blocks) == len(places) else blocks


def everywhere(value, axes, count):
    if count > DIRECT:
        return [lax.all_gather(value, axes, axis=0, tiled=False)]
    return [value] + [
        lax.ppermute(value, axes, [(source_of(i, step, count), i) for i in range(count)])
        for step in range(1, count)
    ]


def along_line(value, line_count, sub_count):
    if line_count > DIRECT or sub_count != 2:
        return everywhere(value, LINE, line_count)
    blocks = [value]
    for step in range(1, line_count):
        pairs = [
            (2 * source_of(place, step, line_count) + 1 - core, 2 * place + core)
            for place in range(line_count)
            for core in range(2)
        ]
        blocks.append(lax.ppermute(value, LINE + ("sub",), pairs))
    return blocks


def plane_blocks(value, shape):
    grp_count, sub_count = shape
    if sub_count != 2 or not paired(grp_count):
        return everywhere(value, PLANE, grp_count * sub_count)
    blocks = everywhere(value, ("sub",), sub_count)
    moved = [everywhere(block, ("grp",), grp_count) for block in blocks]
    return [moved[sub][grp] for grp in range(grp_count) for sub in range(sub_count)]


def make_local(plane_shape, line_count):
    plane_count = plane_shape[0] * plane_shape[1]

    def local(features, lengthscale, noise_var, probes):
        feature_count, width = features.shape
        probe_count = probes.shape[0]
        scaled = (features.astype(jnp.float32) / lengthscale[:, None]).astype(jnp.bfloat16)
        line, plane = pl.pallas_call(
            pack_kernel,
            out_shape=(
                jax.ShapeDtypeStruct((feature_count + probe_count, width), jnp.bfloat16),
                jax.ShapeDtypeStruct((feature_count + 2 * probe_count, width), jnp.bfloat16),
            ),
            compiler_params=VMEM,
        )(scaled, probes)
        lines = along_line(line, line_count, plane_shape[1])
        planes = plane_blocks(plane, plane_shape)
        if len(lines) > 1:
            early, late = lines[:1] + lines[2:], lines[1]
        else:
            early, late = [], lines[0]
        depth = feature_count + 2 * HALF
        work = plane_count * width * width
        rows, columns, start = pl.pallas_call(
            lambda *refs: prepare_kernel(feature_count, 2, *refs),
            out_shape=(
                jax.ShapeDtypeStruct((2, depth, width), jnp.bfloat16),
                jax.ShapeDtypeStruct((max(len(early), 1), width, depth), jnp.bfloat16),
                jax.ShapeDtypeStruct(probes.shape, jnp.float32),
            ),
            compiler_params=VMEM,
            cost_estimate=pl.CostEstimate(
                flops=6 * work * depth, bytes_accessed=4 * plane_count * width, transcendentals=3 * work
            ),
        )(*planes[:2], *early, noise_var[None, :], probes)
        partial = pl.pallas_call(
            lambda *refs: image_kernel(feature_count, plane_count, *refs),
            out_shape=jax.ShapeDtypeStruct((plane_count, probe_count, width), jnp.float32),
            compiler_params=VMEM,
        )(rows, start, *planes[2:], columns, *early, late)
        partials = everywhere(partial, PLANE, plane_count)
        image, sums = pl.pallas_call(
            lambda *refs: combine_kernel(feature_count, plane_count, *refs),
            out_shape=(
                jax.ShapeDtypeStruct(probes.shape, jnp.float32),
                jax.ShapeDtypeStruct((probe_count, 128), jnp.float32),
            ),
            compiler_params=VMEM,
        )(*planes, probes, *in_order(partials, PARTIALS))
        outs = (jax.ShapeDtypeStruct(probes.shape, jnp.float32),) * 3
        return pl.pallas_call(finish_kernel, out_shape=outs, compiler_params=VMEM)(
            image, probes, *in_order(along_line(sums, line_count, plane_shape[1]), SUMS)
        )

    return local


def solution(mesh):
    plane_shape = (mesh.shape["grp"], mesh.shape["sub"])
    spread = P(None, ("parts", "blk", "grp", "sub"))
    return jax.shard_map(
        make_local(plane_shape, mesh.shape["blk"]),
        mesh=mesh,
        in_specs=(spread, P("parts"), P(("parts", "blk", "grp", "sub")), spread),
        out_specs=(spread, spread, spread),
        check_vma=False,
    )
```

```python
import jax
import jax.numpy as jnp
from jax import lax
from jax.experimental import pallas as pl
from jax.experimental.pallas import tpu as pltpu
from jax.sharding import PartitionSpec as P

PLANE = ("grp", "sub")
LINE = ("blk",)
DIRECT = 8
VMEM = pltpu.CompilerParams(vmem_limit_bytes=40 * 1024 * 1024)
PARTIALS, PARTIALS_BACK = (0, 1, 2, 3), (0, 1, 2, 3)
SUMS = (0, 1, 2, 3)
HALF = 8


def pieces_of(value):
    pieces = []
    for _ in range(3):
        piece = value.astype(jnp.bfloat16).astype(jnp.float32)
        pieces.append(piece)
        value = value - piece
    return pieces


def norm_rows(scaled, place):
    norms = -0.5 * jnp.sum(jnp.square(scaled.astype(jnp.float32)), axis=0, keepdims=True)
    row = lax.broadcasted_iota(jnp.int32, (2 * HALF, scaled.shape[1]), 0)
    here, there = place * HALF, (1 - place) * HALF
    rows = jnp.where((row >= there) & (row < there + 3), 1.0, 0.0)
    for number, piece in enumerate(pieces_of(norms)):
        rows = jnp.where(row == here + number, piece, rows)
    return rows.astype(jnp.bfloat16)


def pack_kernel(scaled_ref, probes_ref, line_ref, plane_ref):
    high, low, _ = pieces_of(probes_ref[...])
    high, low = high.astype(jnp.bfloat16), low.astype(jnp.bfloat16)
    line_ref[...] = jnp.concatenate([scaled_ref[...], high], axis=0)
    plane_ref[...] = jnp.concatenate([scaled_ref[...], high, low], axis=0)


def columns_of(block, feature_count):
    scaled = block[:feature_count, :]
    columns = jnp.concatenate([scaled, norm_rows(scaled, 0)], axis=0)
    return columns.astype(jnp.float32).T.astype(jnp.bfloat16)


def rows_of(ref, feature_count):
    scaled = ref[:feature_count, :]
    return jnp.concatenate([scaled, norm_rows(scaled, 1)], axis=0)


def product(columns, probes, rows):
    exponent = jnp.dot(columns, rows, preferred_element_type=jnp.float32)
    weights = jnp.exp(exponent).astype(jnp.bfloat16)
    return jnp.dot(probes, weights, preferred_element_type=jnp.float32)


def side_by_side(refs, feature_count):
    return jnp.concatenate([rows_of(ref, feature_count) for ref in refs], axis=1)


def near_kernel(feature_count, *refs):
    plane_refs, line_refs = refs[:2], refs[2:-5]
    noise_ref, probes_ref, rows_ref, columns_ref, total_ref = refs[-5:]
    rows = side_by_side(plane_refs, feature_count)
    rows_ref[...] = rows
    start = noise_ref[...] * probes_ref[...]
    total = jnp.concatenate([start, jnp.zeros_like(start)], axis=1)
    if line_refs:
        columns = [columns_of(ref[...], feature_count) for ref in line_refs]
        for number, value in enumerate(columns):
            columns_ref[number] = value
        probes = jnp.concatenate([ref[feature_count:, :] for ref in line_refs], axis=1)
        total += product(jnp.concatenate(columns, axis=0), probes, rows)
    total_ref[...] = total


def image_kernel(feature_count, plane_count, *refs):
    rows_ref, total_ref = refs[:2]
    plane_refs = refs[2:plane_count]
    columns_ref, *line_refs = refs[plane_count:-1]
    partial_ref = refs[-1]
    width = partial_ref.shape[2]
    rows = [rows_ref[...]]
    for place in range(0, len(plane_refs), 2):
        rows.append(side_by_side(plane_refs[place : place + 2], feature_count))
    totals = [total_ref[...]] + [jnp.zeros(total_ref.shape, jnp.float32)] * (len(rows) - 1)
    if len(line_refs[0].shape) == 2:
        *early, late = [ref[...] for ref in line_refs]
        late_columns = columns_of(late, feature_count)
        columns = [columns_ref[number] for number in range(len(early))]
        columns = jnp.concatenate(columns + [late_columns], axis=0)
        probes = jnp.concatenate([block[feature_count:, :] for block in early + [late]], axis=1)
        near = totals[0] + product(late_columns, late[feature_count:, :], rows[0])
        totals = [near] + [product(columns, probes, pair) for pair in rows[1:]]
    else:

        def add_block(number, totals):
            block = line_refs[0][number]
            columns = columns_of(block, feature_count)
            return [
                total + product(columns, block[feature_count:, :], pair)
                for pair, total in zip(rows, totals)
            ]

        totals = lax.fori_loop(0, line_refs[0].shape[0], add_block, totals)
    for number in range(plane_count):
        place = number % 2 * width
        partial_ref[number] = totals[number // 2][:, place : place + width]


def combine_kernel(feature_count, plane_count, *refs):
    plane_refs, probes_ref = refs[:plane_count], refs[plane_count]
    partial_refs = in_order(refs[plane_count + 1 : -2], PARTIALS_BACK)
    image_ref, sums_ref = refs[-2:]
    probe_count = image_ref.shape[0]
    lane = lax.broadcasted_iota(jnp.int32, sums_ref.shape, 1)
    products = [0.0, 0.0, 0.0]
    for number, plane_ref in enumerate(plane_refs):
        image = sum(
            ref[place_of(step, number, plane_count)] for step, ref in enumerate(partial_refs)
        )
        if number == 0:
            image_ref[...] = image
            probes = probes_ref[...]
        else:
            middle = feature_count + probe_count
            probes = plane_ref[feature_count:middle, :].astype(jnp.float32)
            probes = probes + plane_ref[middle:, :].astype(jnp.float32)
        products[0] += probes * probes
        products[1] += probes * image
        products[2] += image * image
    sums = jnp.zeros(sums_ref.shape, jnp.float32)
    for number, product in enumerate(products):
        sums = jnp.where(lane == number, jnp.sum(product, axis=1, keepdims=True), sums)
    sums_ref[...] = sums


def finish_kernel(image_ref, probes_ref, *refs):
    *sums_refs, solution_ref, residual_ref, direction_ref = refs
    sums = jnp.zeros(sums_refs[0].shape[-2:], jnp.float32)
    for ref in sums_refs:
        value = ref[...]
        sums = sums + (value if value.ndim == 2 else jnp.sum(value, axis=0))
    start_norms, curvature, image_norms = sums[:, 0:1], sums[:, 1:2], sums[:, 2:3]
    alpha = start_norms / curvature
    new_norms = start_norms - 2.0 * alpha * curvature + alpha * alpha * image_norms
    probes = probes_ref[...]
    residual = probes - alpha * image_ref[...]
    solution_ref[...] = alpha * probes
    residual_ref[...] = residual
    direction_ref[...] = residual + (new_norms / start_norms) * probes


def paired(count):
    return count & (count - 1) == 0


def source_of(device, step, count):
    return device ^ step if paired(count) else (device - step) % count


def place_of(step, number, count):
    return step ^ number if paired(count) else (number - step) % count


def in_order(blocks, places):
    return [blocks[place] for place in places] if len(blocks) == len(places) else blocks


def everywhere(value, axes, count):
    if count > DIRECT:
        return [lax.all_gather(value, axes, axis=0, tiled=False)]
    return [value] + [
        lax.ppermute(value, axes, [(source_of(i, step, count), i) for i in range(count)])
        for step in range(1, count)
    ]


def along_line(value, line_count, sub_count):
    if line_count > DIRECT or sub_count != 2:
        return everywhere(value, LINE, line_count)
    blocks = [value]
    for step in range(1, line_count):
        pairs = [
            (2 * source_of(place, step, line_count) + 1 - core, 2 * place + core)
            for place in range(line_count)
            for core in range(2)
        ]
        blocks.append(lax.ppermute(value, LINE + ("sub",), pairs))
    return blocks


def plane_blocks(value, shape):
    grp_count, sub_count = shape
    if sub_count != 2 or not paired(grp_count):
        return everywhere(value, PLANE, grp_count * sub_count)
    blocks = everywhere(value, ("sub",), sub_count)
    moved = [everywhere(block, ("grp",), grp_count) for block in blocks]
    return [moved[sub][grp] for grp in range(grp_count) for sub in range(sub_count)]


def make_local(plane_shape, line_count):
    plane_count = plane_shape[0] * plane_shape[1]

    def local(features, lengthscale, noise_var, probes):
        feature_count, width = features.shape
        probe_count = probes.shape[0]
        scaled = (features.astype(jnp.float32) / lengthscale[:, None]).astype(jnp.bfloat16)
        line, plane = pl.pallas_call(
            pack_kernel,
            out_shape=(
                jax.ShapeDtypeStruct((feature_count + probe_count, width), jnp.bfloat16),
                jax.ShapeDtypeStruct((feature_count + 2 * probe_count, width), jnp.bfloat16),
            ),
            compiler_params=VMEM,
        )(scaled, probes)
        lines = along_line(line, line_count, plane_shape[1])
        planes = plane_blocks(plane, plane_shape)
        if len(lines) > 1:
            early, late = lines[:1] + lines[2:], lines[1]
        else:
            early, late = [], lines[0]
        depth = feature_count + 2 * HALF
        work = plane_count * width * width
        rows, columns, total = pl.pallas_call(
            lambda *refs: near_kernel(feature_count, *refs),
            out_shape=(
                jax.ShapeDtypeStruct((depth, 2 * width), jnp.bfloat16),
                jax.ShapeDtypeStruct((max(len(early), 1), width, depth), jnp.bfloat16),
                jax.ShapeDtypeStruct((probe_count, 2 * width), jnp.float32),
            ),
            compiler_params=VMEM,
            cost_estimate=pl.CostEstimate(
                flops=6 * work * depth, bytes_accessed=4 * plane_count * width, transcendentals=3 * work
            ),
        )(*planes[:2], *early, noise_var[None, :], probes)
        partial = pl.pallas_call(
            lambda *refs: image_kernel(feature_count, plane_count, *refs),
            out_shape=jax.ShapeDtypeStruct((plane_count, probe_count, width), jnp.float32),
            compiler_params=VMEM,
        )(rows, total, *planes[2:], columns, *early, late)
        partials = everywhere(partial, PLANE, plane_count)
        image, sums = pl.pallas_call(
            lambda *refs: combine_kernel(feature_count, plane_count, *refs),
            out_shape=(
                jax.ShapeDtypeStruct(probes.shape, jnp.float32),
                jax.ShapeDtypeStruct((probe_count, 128), jnp.float32),
            ),
            compiler_params=VMEM,
        )(*planes, probes, *in_order(partials, PARTIALS))
        outs = (jax.ShapeDtypeStruct(probes.shape, jnp.float32),) * 3
        return pl.pallas_call(finish_kernel, out_shape=outs, compiler_params=VMEM)(
            image, probes, *in_order(along_line(sums, line_count, plane_shape[1]), SUMS)
        )

    return local


def solution(mesh):
    plane_shape = (mesh.shape["grp"], mesh.shape["sub"])
    spread = P(None, ("parts", "blk", "grp", "sub"))
    return jax.shard_map(
        make_local(plane_shape, mesh.shape["blk"]),
        mesh=mesh,
        in_specs=(spread, P("parts"), P(("parts", "blk", "grp", "sub")), spread),
        out_specs=(spread, spread, spread),
        check_vma=False,
    )
```

```python
import jax
import jax.numpy as jnp
from jax import lax
from jax.experimental import pallas as pl
from jax.experimental.pallas import tpu as pltpu
from jax.sharding import PartitionSpec as P

PLANE = ("grp", "sub")
LINE = ("blk",)
DIRECT = 8
VMEM = pltpu.CompilerParams(vmem_limit_bytes=40 * 1024 * 1024)
PARTIALS, PARTIALS_BACK = (0, 1, 2, 3), (0, 1, 2, 3)
SUMS = (0, 1, 2, 3)
HALF = 8


def pieces_of(value):
    pieces = []
    for _ in range(3):
        piece = value.astype(jnp.bfloat16).astype(jnp.float32)
        pieces.append(piece)
        value = value - piece
    return pieces


def norm_rows(scaled, place):
    norms = -0.5 * jnp.sum(jnp.square(scaled.astype(jnp.float32)), axis=0, keepdims=True)
    row = lax.broadcasted_iota(jnp.int32, (2 * HALF, scaled.shape[1]), 0)
    here, there = place * HALF, (1 - place) * HALF
    rows = jnp.where((row >= there) & (row < there + 3), 1.0, 0.0)
    for number, piece in enumerate(pieces_of(norms)):
        rows = jnp.where(row == here + number, piece, rows)
    return rows.astype(jnp.bfloat16)


def pack_kernel(scaled_ref, probes_ref, line_ref, plane_ref):
    high, low, _ = pieces_of(probes_ref[...])
    high, low = high.astype(jnp.bfloat16), low.astype(jnp.bfloat16)
    line_ref[...] = jnp.concatenate([scaled_ref[...], high], axis=0)
    plane_ref[...] = jnp.concatenate([scaled_ref[...], high, low], axis=0)


def columns_of(block, feature_count):
    scaled = block[:feature_count, :]
    columns = jnp.concatenate([scaled, norm_rows(scaled, 0)], axis=0)
    return columns.astype(jnp.float32).T.astype(jnp.bfloat16)


def rows_of(ref, feature_count):
    scaled = ref[:feature_count, :]
    return jnp.concatenate([scaled, norm_rows(scaled, 1)], axis=0)


def product(columns, probes, rows):
    exponent = jnp.dot(columns, rows, preferred_element_type=jnp.float32)
    weights = jnp.exp(exponent).astype(jnp.bfloat16)
    return jnp.dot(probes, weights, preferred_element_type=jnp.float32)


def side_by_side(refs, feature_count):
    return jnp.concatenate([rows_of(ref, feature_count) for ref in refs], axis=1)


def near_kernel(feature_count, *refs):
    plane_refs, line_refs = refs[:2], refs[2:-5]
    noise_ref, probes_ref, rows_ref, columns_ref, total_ref = refs[-5:]
    rows = side_by_side(plane_refs, feature_count)
    rows_ref[...] = rows
    start = noise_ref[...] * probes_ref[...]
    total = jnp.concatenate([start, jnp.zeros_like(start)], axis=1)
    if line_refs:
        columns = [columns_of(ref[...], feature_count) for ref in line_refs]
        for number, value in enumerate(columns):
            columns_ref[number] = value
        probes = jnp.concatenate([ref[feature_count:, :] for ref in line_refs], axis=1)
        total += product(jnp.concatenate(columns, axis=0), probes, rows)
    total_ref[...] = total


def image_kernel(feature_count, plane_count, *refs):
    rows_ref, total_ref = refs[:2]
    plane_refs = refs[2:plane_count]
    columns_ref, *line_refs = refs[plane_count:-1]
    partial_ref = refs[-1]
    width = partial_ref.shape[2]
    rows = [rows_ref[...]]
    for place in range(0, len(plane_refs), 2):
        rows.append(side_by_side(plane_refs[place : place + 2], feature_count))
    totals = [total_ref[...]] + [jnp.zeros(total_ref.shape, jnp.float32)] * (len(rows) - 1)
    if len(line_refs[0].shape) == 2:
        *early, late = [ref[...] for ref in line_refs]
        late_columns = columns_of(late, feature_count)
        columns = [columns_ref[number] for number in range(len(early))]
        columns = jnp.concatenate(columns + [late_columns], axis=0)
        probes = jnp.concatenate([block[feature_count:, :] for block in early + [late]], axis=1)
        near = totals[0] + product(late_columns, late[feature_count:, :], rows[0])
        totals = [near] + [product(columns, probes, pair) for pair in rows[1:]]
    else:

        def add_block(number, totals):
            block = line_refs[0][number]
            columns = columns_of(block, feature_count)
            return [
                total + product(columns, block[feature_count:, :], pair)
                for pair, total in zip(rows, totals)
            ]

        totals = lax.fori_loop(0, line_refs[0].shape[0], add_block, totals)
    for number in range(plane_count):
        place = number % 2 * width
        partial_ref[number] = totals[number // 2][:, place : place + width]


def combine_kernel(feature_count, plane_count, *refs):
    plane_refs, probes_ref = refs[:plane_count], refs[plane_count]
    partial_refs = in_order(refs[plane_count + 1 : -2], PARTIALS_BACK)
    image_ref, sums_ref = refs[-2:]
    probe_count = image_ref.shape[0]
    lane = lax.broadcasted_iota(jnp.int32, sums_ref.shape, 1)
    products = [0.0, 0.0, 0.0]
    for number, plane_ref in enumerate(plane_refs):
        image = sum(
            ref[place_of(step, number, plane_count)] for step, ref in enumerate(partial_refs)
        )
        if number == 0:
            image_ref[...] = image
            probes = probes_ref[...]
        else:
            middle = feature_count + probe_count
            probes = plane_ref[feature_count:middle, :].astype(jnp.float32)
            probes = probes + plane_ref[middle:, :].astype(jnp.float32)
        products[0] += probes * probes
        products[1] += probes * image
        products[2] += image * image
    sums = jnp.zeros(sums_ref.shape, jnp.float32)
    for number, product in enumerate(products):
        sums = jnp.where(lane == number, jnp.sum(product, axis=1, keepdims=True), sums)
    sums_ref[...] = sums


def finish_kernel(image_ref, probes_ref, *refs):
    *sums_refs, solution_ref, residual_ref, direction_ref = refs
    sums = jnp.zeros(sums_refs[0].shape[-2:], jnp.float32)
    for ref in sums_refs:
        value = ref[...]
        sums = sums + (value if value.ndim == 2 else jnp.sum(value, axis=0))
    start_norms, curvature, image_norms = sums[:, 0:1], sums[:, 1:2], sums[:, 2:3]
    alpha = start_norms / curvature
    new_norms = start_norms - 2.0 * alpha * curvature + alpha * alpha * image_norms
    probes = probes_ref[...]
    residual = probes - alpha * image_ref[...]
    solution_ref[...] = alpha * probes
    residual_ref[...] = residual
    direction_ref[...] = residual + (new_norms / start_norms) * probes


def paired(count):
    return count & (count - 1) == 0


def source_of(device, step, count):
    return device ^ step if paired(count) else (device - step) % count


def place_of(step, number, count):
    return step ^ number if paired(count) else (number - step) % count


def in_order(blocks, places):
    return [blocks[place] for place in places] if len(blocks) == len(places) else blocks


def everywhere(value, axes, count):
    if count > DIRECT:
        return [lax.all_gather(value, axes, axis=0, tiled=False)]
    return [value] + [
        lax.ppermute(value, axes, [(source_of(i, step, count), i) for i in range(count)])
        for step in range(1, count)
    ]


def along_line(value, line_count, sub_count, same_core=()):
    if line_count > DIRECT or sub_count != 2:
        return everywhere(value, LINE, line_count)
    blocks = [value]
    for step in range(1, line_count):
        pairs = [
            (
                2 * source_of(place, step, line_count) + (core if step in same_core else 1 - core),
                2 * place + core,
            )
            for place in range(line_count)
            for core in range(2)
        ]
        blocks.append(lax.ppermute(value, LINE + ("sub",), pairs))
    return blocks


def plane_blocks(value, shape):
    grp_count, sub_count = shape
    if sub_count != 2 or not paired(grp_count):
        return everywhere(value, PLANE, grp_count * sub_count)
    blocks = everywhere(value, ("sub",), sub_count)
    moved = [everywhere(block, ("grp",), grp_count) for block in blocks]
    return [moved[sub][grp] for grp in range(grp_count) for sub in range(sub_count)]


def make_local(plane_shape, line_count):
    plane_count = plane_shape[0] * plane_shape[1]

    def local(features, lengthscale, noise_var, probes):
        feature_count, width = features.shape
        probe_count = probes.shape[0]
        scaled = (features.astype(jnp.float32) / lengthscale[:, None]).astype(jnp.bfloat16)
        line, plane = pl.pallas_call(
            pack_kernel,
            out_shape=(
                jax.ShapeDtypeStruct((feature_count + probe_count, width), jnp.bfloat16),
                jax.ShapeDtypeStruct((feature_count + 2 * probe_count, width), jnp.bfloat16),
            ),
            compiler_params=VMEM,
        )(scaled, probes)
        lines = along_line(line, line_count, plane_shape[1])
        planes = plane_blocks(plane, plane_shape)
        if len(lines) > 1:
            early, late = lines[:1] + lines[2:], lines[1]
        else:
            early, late = [], lines[0]
        depth = feature_count + 2 * HALF
        work = plane_count * width * width
        rows, columns, total = pl.pallas_call(
            lambda *refs: near_kernel(feature_count, *refs),
            out_shape=(
                jax.ShapeDtypeStruct((depth, 2 * width), jnp.bfloat16),
                jax.ShapeDtypeStruct((max(len(early), 1), width, depth), jnp.bfloat16),
                jax.ShapeDtypeStruct((probe_count, 2 * width), jnp.float32),
            ),
            compiler_params=VMEM,
            cost_estimate=pl.CostEstimate(
                flops=6 * work * depth, bytes_accessed=4 * plane_count * width, transcendentals=3 * work
            ),
        )(*planes[:2], *early, noise_var[None, :], probes)
        partial = pl.pallas_call(
            lambda *refs: image_kernel(feature_count, plane_count, *refs),
            out_shape=jax.ShapeDtypeStruct((plane_count, probe_count, width), jnp.float32),
            compiler_params=VMEM,
        )(rows, total, *planes[2:], columns, *early, late)
        partials = everywhere(partial, PLANE, plane_count)
        image, sums = pl.pallas_call(
            lambda *refs: combine_kernel(feature_count, plane_count, *refs),
            out_shape=(
                jax.ShapeDtypeStruct(probes.shape, jnp.float32),
                jax.ShapeDtypeStruct((probe_count, 128), jnp.float32),
            ),
            compiler_params=VMEM,
        )(*planes, probes, *in_order(partials, PARTIALS))
        outs = (jax.ShapeDtypeStruct(probes.shape, jnp.float32),) * 3
        return pl.pallas_call(finish_kernel, out_shape=outs, compiler_params=VMEM)(
            image, probes, *in_order(along_line(sums, line_count, plane_shape[1], (3,)), SUMS)
        )

    return local


def solution(mesh):
    plane_shape = (mesh.shape["grp"], mesh.shape["sub"])
    spread = P(None, ("parts", "blk", "grp", "sub"))
    return jax.shard_map(
        make_local(plane_shape, mesh.shape["blk"]),
        mesh=mesh,
        in_specs=(spread, P("parts"), P(("parts", "blk", "grp", "sub")), spread),
        out_specs=(spread, spread, spread),
        check_vma=False,
    )
```

```python
import jax
import jax.numpy as jnp
from jax import lax
from jax.experimental import pallas as pl
from jax.experimental.pallas import tpu as pltpu
from jax.sharding import PartitionSpec as P

PLANE = ("grp", "sub")
LINE = ("blk",)
DIRECT = 8
VMEM = pltpu.CompilerParams(vmem_limit_bytes=40 * 1024 * 1024)
PARTIALS, PARTIALS_BACK = (0, 1, 2, 3), (0, 1, 2, 3)
SUMS = (0, 1, 2, 3)
HALF = 8


def pieces_of(value):
    pieces = []
    for _ in range(3):
        piece = value.astype(jnp.bfloat16).astype(jnp.float32)
        pieces.append(piece)
        value = value - piece
    return pieces


def norm_rows(scaled, place):
    norms = -0.5 * jnp.sum(jnp.square(scaled.astype(jnp.float32)), axis=0, keepdims=True)
    row = lax.broadcasted_iota(jnp.int32, (2 * HALF, scaled.shape[1]), 0)
    here, there = place * HALF, (1 - place) * HALF
    rows = jnp.where((row >= there) & (row < there + 3), 1.0, 0.0)
    for number, piece in enumerate(pieces_of(norms)):
        rows = jnp.where(row == here + number, piece, rows)
    return rows.astype(jnp.bfloat16)


def pack_kernel(scaled_ref, probes_ref, line_ref, plane_ref):
    high, low, _ = pieces_of(probes_ref[...])
    high, low = high.astype(jnp.bfloat16), low.astype(jnp.bfloat16)
    line_ref[...] = jnp.concatenate([scaled_ref[...], high], axis=0)
    plane_ref[...] = jnp.concatenate([scaled_ref[...], high, low], axis=0)


def columns_of(block, feature_count):
    scaled = block[:feature_count, :]
    columns = jnp.concatenate([scaled, norm_rows(scaled, 0)], axis=0)
    return columns.astype(jnp.float32).T.astype(jnp.bfloat16)


def rows_of(ref, feature_count):
    scaled = ref[:feature_count, :]
    return jnp.concatenate([scaled, norm_rows(scaled, 1)], axis=0)


def product(columns, probes, rows):
    exponent = jnp.dot(columns, rows, preferred_element_type=jnp.float32)
    weights = jnp.exp(exponent).astype(jnp.bfloat16)
    return jnp.dot(probes, weights, preferred_element_type=jnp.float32)


def side_by_side(refs, feature_count):
    return jnp.concatenate([rows_of(ref, feature_count) for ref in refs], axis=1)


def near_kernel(feature_count, *refs):
    plane_refs, line_refs = refs[:2], refs[2:-5]
    noise_ref, probes_ref, rows_ref, columns_ref, total_ref = refs[-5:]
    rows = side_by_side(plane_refs, feature_count)
    rows_ref[...] = rows
    start = noise_ref[...] * probes_ref[...]
    total = jnp.concatenate([start, jnp.zeros_like(start)], axis=1)
    if line_refs:
        columns = [columns_of(ref[...], feature_count) for ref in line_refs]
        for number, value in enumerate(columns):
            columns_ref[number] = value
        probes = jnp.concatenate([ref[feature_count:, :] for ref in line_refs], axis=1)
        total += product(jnp.concatenate(columns, axis=0), probes, rows)
    total_ref[...] = total


def far_kernel(feature_count, *refs):
    *plane_refs, far_ref = refs
    for place in range(0, len(plane_refs), 2):
        far_ref[place // 2] = side_by_side(plane_refs[place : place + 2], feature_count)


def image_kernel(feature_count, plane_count, *refs):
    rows_ref, total_ref = refs[:2]
    far_ref, columns_ref, *line_refs = refs[2:-1]
    partial_ref = refs[-1]
    width = partial_ref.shape[2]
    rows = [rows_ref[...]] + [far_ref[number] for number in range(plane_count // 2 - 1)]
    totals = [total_ref[...]] + [jnp.zeros(total_ref.shape, jnp.float32)] * (len(rows) - 1)
    if len(line_refs[0].shape) == 2:
        *early, late = [ref[...] for ref in line_refs]
        late_columns = columns_of(late, feature_count)
        columns = [columns_ref[number] for number in range(len(early))]
        columns = jnp.concatenate(columns + [late_columns], axis=0)
        probes = jnp.concatenate([block[feature_count:, :] for block in early + [late]], axis=1)
        near = totals[0] + product(late_columns, late[feature_count:, :], rows[0])
        totals = [near] + [product(columns, probes, pair) for pair in rows[1:]]
    else:

        def add_block(number, totals):
            block = line_refs[0][number]
            columns = columns_of(block, feature_count)
            return [
                total + product(columns, block[feature_count:, :], pair)
                for pair, total in zip(rows, totals)
            ]

        totals = lax.fori_loop(0, line_refs[0].shape[0], add_block, totals)
    for number in range(plane_count):
        place = number % 2 * width
        partial_ref[number] = totals[number // 2][:, place : place + width]


def combine_kernel(feature_count, plane_count, *refs):
    plane_refs, probes_ref = refs[:plane_count], refs[plane_count]
    partial_refs = in_order(refs[plane_count + 1 : -2], PARTIALS_BACK)
    image_ref, sums_ref = refs[-2:]
    probe_count = image_ref.shape[0]
    lane = lax.broadcasted_iota(jnp.int32, sums_ref.shape, 1)
    products = [0.0, 0.0, 0.0]
    for number, plane_ref in enumerate(plane_refs):
        image = sum(
            ref[place_of(step, number, plane_count)] for step, ref in enumerate(partial_refs)
        )
        if number == 0:
            image_ref[...] = image
            probes = probes_ref[...]
        else:
            middle = feature_count + probe_count
            probes = plane_ref[feature_count:middle, :].astype(jnp.float32)
            probes = probes + plane_ref[middle:, :].astype(jnp.float32)
        products[0] += probes * probes
        products[1] += probes * image
        products[2] += image * image
    sums = jnp.zeros(sums_ref.shape, jnp.float32)
    for number, product in enumerate(products):
        sums = jnp.where(lane == number, jnp.sum(product, axis=1, keepdims=True), sums)
    sums_ref[...] = sums


def finish_kernel(image_ref, probes_ref, *refs):
    *sums_refs, solution_ref, residual_ref, direction_ref = refs
    sums = jnp.zeros(sums_refs[0].shape[-2:], jnp.float32)
    for ref in sums_refs:
        value = ref[...]
        sums = sums + (value if value.ndim == 2 else jnp.sum(value, axis=0))
    start_norms, curvature, image_norms = sums[:, 0:1], sums[:, 1:2], sums[:, 2:3]
    alpha = start_norms / curvature
    new_norms = start_norms - 2.0 * alpha * curvature + alpha * alpha * image_norms
    probes = probes_ref[...]
    residual = probes - alpha * image_ref[...]
    solution_ref[...] = alpha * probes
    residual_ref[...] = residual
    direction_ref[...] = residual + (new_norms / start_norms) * probes


def paired(count):
    return count & (count - 1) == 0


def source_of(device, step, count):
    return device ^ step if paired(count) else (device - step) % count


def place_of(step, number, count):
    return step ^ number if paired(count) else (number - step) % count


def in_order(blocks, places):
    return [blocks[place] for place in places] if len(blocks) == len(places) else blocks


def everywhere(value, axes, count):
    if count > DIRECT:
        return [lax.all_gather(value, axes, axis=0, tiled=False)]
    return [value] + [
        lax.ppermute(value, axes, [(source_of(i, step, count), i) for i in range(count)])
        for step in range(1, count)
    ]


def along_line(value, line_count, sub_count):
    if line_count > DIRECT or sub_count != 2:
        return everywhere(value, LINE, line_count)
    blocks = [value]
    for step in range(1, line_count):
        pairs = [
            (2 * source_of(place, step, line_count) + 1 - core, 2 * place + core)
            for place in range(line_count)
            for core in range(2)
        ]
        blocks.append(lax.ppermute(value, LINE + ("sub",), pairs))
    return blocks


def plane_blocks(value, shape):
    grp_count, sub_count = shape
    if sub_count != 2 or not paired(grp_count):
        return everywhere(value, PLANE, grp_count * sub_count)
    blocks = everywhere(value, ("sub",), sub_count)
    moved = [everywhere(block, ("grp",), grp_count) for block in blocks]
    return [moved[sub][grp] for grp in range(grp_count) for sub in range(sub_count)]


def make_local(plane_shape, line_count):
    plane_count = plane_shape[0] * plane_shape[1]

    def local(features, lengthscale, noise_var, probes):
        feature_count, width = features.shape
        probe_count = probes.shape[0]
        scaled = (features.astype(jnp.float32) / lengthscale[:, None]).astype(jnp.bfloat16)
        line, plane = pl.pallas_call(
            pack_kernel,
            out_shape=(
                jax.ShapeDtypeStruct((feature_count + probe_count, width), jnp.bfloat16),
                jax.ShapeDtypeStruct((feature_count + 2 * probe_count, width), jnp.bfloat16),
            ),
            compiler_params=VMEM,
        )(scaled, probes)
        lines = along_line(line, line_count, plane_shape[1])
        planes = plane_blocks(plane, plane_shape)
        if len(lines) > 1:
            early, late = lines[:1] + lines[2:], lines[1]
        else:
            early, late = [], lines[0]
        depth = feature_count + 2 * HALF
        work = plane_count * width * width
        rows, columns, total = pl.pallas_call(
            lambda *refs: near_kernel(feature_count, *refs),
            out_shape=(
                jax.ShapeDtypeStruct((depth, 2 * width), jnp.bfloat16),
                jax.ShapeDtypeStruct((max(len(early), 1), width, depth), jnp.bfloat16),
                jax.ShapeDtypeStruct((probe_count, 2 * width), jnp.float32),
            ),
            compiler_params=VMEM,
            cost_estimate=pl.CostEstimate(
                flops=6 * work * depth, bytes_accessed=4 * plane_count * width, transcendentals=3 * work
            ),
        )(*planes[:2], *early, noise_var[None, :], probes)
        far = pl.pallas_call(
            lambda *refs: far_kernel(feature_count, *refs),
            out_shape=jax.ShapeDtypeStruct(
                (plane_count // 2 - 1, depth, 2 * width), jnp.bfloat16
            ),
            compiler_params=VMEM,
        )(*planes[2:])
        partial = pl.pallas_call(
            lambda *refs: image_kernel(feature_count, plane_count, *refs),
            out_shape=jax.ShapeDtypeStruct((plane_count, probe_count, width), jnp.float32),
            compiler_params=VMEM,
        )(rows, total, far, columns, *early, late)
        partials = everywhere(partial, PLANE, plane_count)
        image, sums = pl.pallas_call(
            lambda *refs: combine_kernel(feature_count, plane_count, *refs),
            out_shape=(
                jax.ShapeDtypeStruct(probes.shape, jnp.float32),
                jax.ShapeDtypeStruct((probe_count, 128), jnp.float32),
            ),
            compiler_params=VMEM,
        )(*planes, probes, *in_order(partials, PARTIALS))
        outs = (jax.ShapeDtypeStruct(probes.shape, jnp.float32),) * 3
        return pl.pallas_call(finish_kernel, out_shape=outs, compiler_params=VMEM)(
            image, probes, *in_order(along_line(sums, line_count, plane_shape[1]), SUMS)
        )

    return local


def solution(mesh):
    plane_shape = (mesh.shape["grp"], mesh.shape["sub"])
    spread = P(None, ("parts", "blk", "grp", "sub"))
    return jax.shard_map(
        make_local(plane_shape, mesh.shape["blk"]),
        mesh=mesh,
        in_specs=(spread, P("parts"), P(("parts", "blk", "grp", "sub")), spread),
        out_specs=(spread, spread, spread),
        check_vma=False,
    )
```

```python
import jax
import jax.numpy as jnp
from jax import lax
from jax.experimental import pallas as pl
from jax.experimental.pallas import tpu as pltpu
from jax.sharding import PartitionSpec as P

PLANE = ("grp", "sub")
LINE = ("blk",)
DIRECT = 8
VMEM = pltpu.CompilerParams(vmem_limit_bytes=40 * 1024 * 1024)
PARTIALS, PARTIALS_BACK = (0, 3, 2, 1), (0, 3, 2, 1)
SUMS = (0, 3, 2, 1)
HALF = 8


def pieces_of(value):
    pieces = []
    for _ in range(3):
        piece = value.astype(jnp.bfloat16).astype(jnp.float32)
        pieces.append(piece)
        value = value - piece
    return pieces


def norm_rows(scaled, place):
    norms = -0.5 * jnp.sum(jnp.square(scaled.astype(jnp.float32)), axis=0, keepdims=True)
    row = lax.broadcasted_iota(jnp.int32, (2 * HALF, scaled.shape[1]), 0)
    here, there = place * HALF, (1 - place) * HALF
    rows = jnp.where((row >= there) & (row < there + 3), 1.0, 0.0)
    for number, piece in enumerate(pieces_of(norms)):
        rows = jnp.where(row == here + number, piece, rows)
    return rows.astype(jnp.bfloat16)


def pack_kernel(scaled_ref, probes_ref, line_ref, plane_ref):
    high, low, _ = pieces_of(probes_ref[...])
    high, low = high.astype(jnp.bfloat16), low.astype(jnp.bfloat16)
    line_ref[...] = jnp.concatenate([scaled_ref[...], high], axis=0)
    plane_ref[...] = jnp.concatenate([scaled_ref[...], high, low], axis=0)


def columns_of(block, feature_count):
    scaled = block[:feature_count, :]
    columns = jnp.concatenate([scaled, norm_rows(scaled, 0)], axis=0)
    return columns.astype(jnp.float32).T.astype(jnp.bfloat16)


def rows_of(ref, feature_count):
    scaled = ref[:feature_count, :]
    return jnp.concatenate([scaled, norm_rows(scaled, 1)], axis=0)


def product(columns, probes, rows):
    exponent = jnp.dot(columns, rows, preferred_element_type=jnp.float32)
    weights = jnp.exp(exponent).astype(jnp.bfloat16)
    return jnp.dot(probes, weights, preferred_element_type=jnp.float32)


def side_by_side(refs, feature_count):
    return jnp.concatenate([rows_of(ref, feature_count) for ref in refs], axis=1)


def near_kernel(feature_count, *refs):
    plane_refs, line_refs = refs[:2], refs[2:-5]
    noise_ref, probes_ref, rows_ref, columns_ref, total_ref = refs[-5:]
    rows = side_by_side(plane_refs, feature_count)
    rows_ref[...] = rows
    start = noise_ref[...] * probes_ref[...]
    total = jnp.concatenate([start, jnp.zeros_like(start)], axis=1)
    if line_refs:
        columns = [columns_of(ref[...], feature_count) for ref in line_refs]
        for number, value in enumerate(columns):
            columns_ref[number] = value
        probes = jnp.concatenate([ref[feature_count:, :] for ref in line_refs], axis=1)
        total += product(jnp.concatenate(columns, axis=0), probes, rows)
    total_ref[...] = total


def far_kernel(feature_count, plane_count, *refs):
    plane_refs, columns_ref = refs[: plane_count - 2], refs[plane_count - 2]
    line_refs, (far_ref, totals_ref) = refs[plane_count - 1 : -2], refs[-2:]
    totals_ref[...] = jnp.zeros(totals_ref.shape, jnp.float32)
    for number in range(len(plane_refs) // 2):
        rows = side_by_side(plane_refs[2 * number : 2 * number + 2], feature_count)
        far_ref[number] = rows
        if line_refs:
            columns = [columns_ref[place] for place in range(len(line_refs))]
            probes = jnp.concatenate([ref[feature_count:, :] for ref in line_refs], axis=1)
            totals_ref[number] = product(jnp.concatenate(columns, axis=0), probes, rows)


def image_kernel(feature_count, plane_count, *refs):
    rows_ref, total_ref = refs[:2]
    far_ref, far_total_ref, line_ref, partial_ref = refs[2:]
    width = partial_ref.shape[2]
    rows = [rows_ref[...]] + [far_ref[number] for number in range(plane_count // 2 - 1)]
    totals = [total_ref[...]] + [far_total_ref[number] for number in range(len(rows) - 1)]

    def add_block(block, totals):
        columns = columns_of(block, feature_count)
        return [
            total + product(columns, block[feature_count:, :], pair)
            for pair, total in zip(rows, totals)
        ]

    if len(line_ref.shape) == 2:
        totals = add_block(line_ref[...], totals)
    else:
        totals = lax.fori_loop(
            0, line_ref.shape[0], lambda number, value: add_block(line_ref[number], value), totals
        )
    for number in range(plane_count):
        place = number % 2 * width
        partial_ref[number] = totals[number // 2][:, place : place + width]


def combine_kernel(feature_count, plane_count, *refs):
    plane_refs, probes_ref = refs[:plane_count], refs[plane_count]
    partial_refs = in_order(refs[plane_count + 1 : -2], PARTIALS_BACK)
    image_ref, sums_ref = refs[-2:]
    probe_count = image_ref.shape[0]
    lane = lax.broadcasted_iota(jnp.int32, sums_ref.shape, 1)
    products = [0.0, 0.0, 0.0]
    for number, plane_ref in enumerate(plane_refs):
        image = sum(
            ref[place_of(step, number, plane_count)] for step, ref in enumerate(partial_refs)
        )
        if number == 0:
            image_ref[...] = image
            probes = probes_ref[...]
        else:
            middle = feature_count + probe_count
            probes = plane_ref[feature_count:middle, :].astype(jnp.float32)
            probes = probes + plane_ref[middle:, :].astype(jnp.float32)
        products[0] += probes * probes
        products[1] += probes * image
        products[2] += image * image
    sums = jnp.zeros(sums_ref.shape, jnp.float32)
    for number, product in enumerate(products):
        sums = jnp.where(lane == number, jnp.sum(product, axis=1, keepdims=True), sums)
    sums_ref[...] = sums


def finish_kernel(image_ref, probes_ref, *refs):
    *sums_refs, solution_ref, residual_ref, direction_ref = refs
    sums = jnp.zeros(sums_refs[0].shape[-2:], jnp.float32)
    for ref in sums_refs:
        value = ref[...]
        sums = sums + (value if value.ndim == 2 else jnp.sum(value, axis=0))
    start_norms, curvature, image_norms = sums[:, 0:1], sums[:, 1:2], sums[:, 2:3]
    alpha = start_norms / curvature
    new_norms = start_norms - 2.0 * alpha * curvature + alpha * alpha * image_norms
    probes = probes_ref[...]
    residual = probes - alpha * image_ref[...]
    solution_ref[...] = alpha * probes
    residual_ref[...] = residual
    direction_ref[...] = residual + (new_norms / start_norms) * probes


def paired(count):
    return count & (count - 1) == 0


def source_of(device, step, count):
    return device ^ step if paired(count) else (device - step) % count


def place_of(step, number, count):
    return step ^ number if paired(count) else (number - step) % count


def in_order(blocks, places):
    return [blocks[place] for place in places] if len(blocks) == len(places) else blocks


def everywhere(value, axes, count):
    if count > DIRECT:
        return [lax.all_gather(value, axes, axis=0, tiled=False)]
    return [value] + [
        lax.ppermute(value, axes, [(source_of(i, step, count), i) for i in range(count)])
        for step in range(1, count)
    ]


def along_line(value, line_count, sub_count):
    if line_count > DIRECT or sub_count != 2:
        return everywhere(value, LINE, line_count)
    blocks = [value]
    for step in range(1, line_count):
        pairs = [
            (2 * source_of(place, step, line_count) + 1 - core, 2 * place + core)
            for place in range(line_count)
            for core in range(2)
        ]
        blocks.append(lax.ppermute(value, LINE + ("sub",), pairs))
    return blocks


def plane_blocks(value, shape):
    grp_count, sub_count = shape
    if sub_count != 2 or not paired(grp_count):
        return everywhere(value, PLANE, grp_count * sub_count)
    blocks = everywhere(value, ("sub",), sub_count)
    moved = [everywhere(block, ("grp",), grp_count) for block in blocks]
    return [moved[sub][grp] for grp in range(grp_count) for sub in range(sub_count)]


def make_local(plane_shape, line_count):
    plane_count = plane_shape[0] * plane_shape[1]

    def local(features, lengthscale, noise_var, probes):
        feature_count, width = features.shape
        probe_count = probes.shape[0]
        scaled = (features.astype(jnp.float32) / lengthscale[:, None]).astype(jnp.bfloat16)
        line, plane = pl.pallas_call(
            pack_kernel,
            out_shape=(
                jax.ShapeDtypeStruct((feature_count + probe_count, width), jnp.bfloat16),
                jax.ShapeDtypeStruct((feature_count + 2 * probe_count, width), jnp.bfloat16),
            ),
            compiler_params=VMEM,
        )(scaled, probes)
        lines = along_line(line, line_count, plane_shape[1])
        planes = plane_blocks(plane, plane_shape)
        if len(lines) > 1:
            early, late = lines[:1] + lines[:1:-1], lines[1]
        else:
            early, late = [], lines[0]
        depth = feature_count + 2 * HALF
        work = plane_count * width * width
        rows, columns, total = pl.pallas_call(
            lambda *refs: near_kernel(feature_count, *refs),
            out_shape=(
                jax.ShapeDtypeStruct((depth, 2 * width), jnp.bfloat16),
                jax.ShapeDtypeStruct((max(len(early), 1), width, depth), jnp.bfloat16),
                jax.ShapeDtypeStruct((probe_count, 2 * width), jnp.float32),
            ),
            compiler_params=VMEM,
            cost_estimate=pl.CostEstimate(
                flops=6 * work * depth, bytes_accessed=4 * plane_count * width, transcendentals=3 * work
            ),
        )(*planes[:2], *early, noise_var[None, :], probes)
        pairs = plane_count // 2 - 1
        far, far_totals = pl.pallas_call(
            lambda *refs: far_kernel(feature_count, plane_count, *refs),
            out_shape=(
                jax.ShapeDtypeStruct((pairs, depth, 2 * width), jnp.bfloat16),
                jax.ShapeDtypeStruct((pairs, probe_count, 2 * width), jnp.float32),
            ),
            compiler_params=VMEM,
        )(*planes[2:], columns, *early)
        partial = pl.pallas_call(
            lambda *refs: image_kernel(feature_count, plane_count, *refs),
            out_shape=jax.ShapeDtypeStruct((plane_count, probe_count, width), jnp.float32),
            compiler_params=VMEM,
        )(rows, total, far, far_totals, late)
        partials = everywhere(partial, PLANE, plane_count)
        image, sums = pl.pallas_call(
            lambda *refs: combine_kernel(feature_count, plane_count, *refs),
            out_shape=(
                jax.ShapeDtypeStruct(probes.shape, jnp.float32),
                jax.ShapeDtypeStruct((probe_count, 128), jnp.float32),
            ),
            compiler_params=VMEM,
        )(*planes, probes, *in_order(partials, PARTIALS))
        outs = (jax.ShapeDtypeStruct(probes.shape, jnp.float32),) * 3
        return pl.pallas_call(finish_kernel, out_shape=outs, compiler_params=VMEM)(
            image, probes, *in_order(along_line(sums, line_count, plane_shape[1]), SUMS)
        )

    return local


def solution(mesh):
    plane_shape = (mesh.shape["grp"], mesh.shape["sub"])
    spread = P(None, ("parts", "blk", "grp", "sub"))
    return jax.shard_map(
        make_local(plane_shape, mesh.shape["blk"]),
        mesh=mesh,
        in_specs=(spread, P("parts"), P(("parts", "blk", "grp", "sub")), spread),
        out_specs=(spread, spread, spread),
        check_vma=False,
    )
```

```python
import jax
import jax.numpy as jnp
from jax import lax
from jax.experimental import pallas as pl
from jax.experimental.pallas import tpu as pltpu
from jax.sharding import PartitionSpec as P

PLANE = ("grp", "sub")
LINE = ("blk",)
DIRECT = 8
VMEM = pltpu.CompilerParams(vmem_limit_bytes=40 * 1024 * 1024)
PARTIALS, PARTIALS_BACK = (0, 1, 3, 2), (0, 1, 3, 2)
SUMS = (0, 1, 2, 3)
HALF = 8


def pieces_of(value):
    pieces = []
    for _ in range(3):
        piece = value.astype(jnp.bfloat16).astype(jnp.float32)
        pieces.append(piece)
        value = value - piece
    return pieces


def norm_rows(scaled, place):
    norms = -0.5 * jnp.sum(jnp.square(scaled.astype(jnp.float32)), axis=0, keepdims=True)
    row = lax.broadcasted_iota(jnp.int32, (2 * HALF, scaled.shape[1]), 0)
    here, there = place * HALF, (1 - place) * HALF
    rows = jnp.where((row >= there) & (row < there + 3), 1.0, 0.0)
    for number, piece in enumerate(pieces_of(norms)):
        rows = jnp.where(row == here + number, piece, rows)
    return rows.astype(jnp.bfloat16)


def pack_kernel(scaled_ref, probes_ref, line_ref, plane_ref):
    high, low, _ = pieces_of(probes_ref[...])
    high, low = high.astype(jnp.bfloat16), low.astype(jnp.bfloat16)
    line_ref[...] = jnp.concatenate([scaled_ref[...], high], axis=0)
    plane_ref[...] = jnp.concatenate([scaled_ref[...], high, low], axis=0)


def columns_of(block, feature_count):
    scaled = block[:feature_count, :]
    columns = jnp.concatenate([scaled, norm_rows(scaled, 0)], axis=0)
    return columns.astype(jnp.float32).T.astype(jnp.bfloat16)


def rows_of(ref, feature_count):
    scaled = ref[:feature_count, :]
    return jnp.concatenate([scaled, norm_rows(scaled, 1)], axis=0)


def product(columns, probes, rows):
    exponent = jnp.dot(columns, rows, preferred_element_type=jnp.float32)
    weights = jnp.exp(exponent).astype(jnp.bfloat16)
    return jnp.dot(probes, weights, preferred_element_type=jnp.float32)


def side_by_side(refs, feature_count):
    return jnp.concatenate([rows_of(ref, feature_count) for ref in refs], axis=1)


def near_kernel(feature_count, *refs):
    plane_refs, line_refs = refs[:2], refs[2:-5]
    noise_ref, probes_ref, rows_ref, columns_ref, total_ref = refs[-5:]
    rows = side_by_side(plane_refs, feature_count)
    rows_ref[...] = rows
    start = noise_ref[...] * probes_ref[...]
    total = jnp.concatenate([start, jnp.zeros_like(start)], axis=1)
    if line_refs:
        columns = [columns_of(ref[...], feature_count) for ref in line_refs]
        for number, value in enumerate(columns):
            columns_ref[number] = value
        probes = jnp.concatenate([ref[feature_count:, :] for ref in line_refs], axis=1)
        total += product(jnp.concatenate(columns, axis=0), probes, rows)
    total_ref[...] = total


def far_kernel(feature_count, *refs):
    *plane_refs, far_ref = refs
    for place in range(0, len(plane_refs), 2):
        far_ref[place // 2] = side_by_side(plane_refs[place : place + 2], feature_count)


def image_kernel(feature_count, plane_count, *refs):
    rows_ref, total_ref = refs[:2]
    far_ref, columns_ref, *line_refs = refs[2:-1]
    partial_ref = refs[-1]
    width = partial_ref.shape[2]
    rows = [rows_ref[...]] + [far_ref[number] for number in range(plane_count // 2 - 1)]
    totals = [total_ref[...]] + [jnp.zeros(total_ref.shape, jnp.float32)] * (len(rows) - 1)
    if len(line_refs[0].shape) == 2:
        *early, late = [ref[...] for ref in line_refs]
        late_columns = columns_of(late, feature_count)
        columns = [columns_ref[number] for number in range(len(early))]
        columns = jnp.concatenate(columns + [late_columns], axis=0)
        probes = jnp.concatenate([block[feature_count:, :] for block in early + [late]], axis=1)
        near = totals[0] + product(late_columns, late[feature_count:, :], rows[0])
        totals = [near] + [product(columns, probes, pair) for pair in rows[1:]]
    else:

        def add_block(number, totals):
            block = line_refs[0][number]
            columns = columns_of(block, feature_count)
            return [
                total + product(columns, block[feature_count:, :], pair)
                for pair, total in zip(rows, totals)
            ]

        totals = lax.fori_loop(0, line_refs[0].shape[0], add_block, totals)
    for number in range(plane_count):
        place = number % 2 * width
        partial_ref[number] = totals[number // 2][:, place : place + width]


def combine_kernel(feature_count, plane_count, *refs):
    plane_refs, probes_ref = refs[:plane_count], refs[plane_count]
    partial_refs = in_order(refs[plane_count + 1 : -2], PARTIALS_BACK)
    image_ref, sums_ref = refs[-2:]
    probe_count = image_ref.shape[0]
    lane = lax.broadcasted_iota(jnp.int32, sums_ref.shape, 1)
    products = [0.0, 0.0, 0.0]
    for number, plane_ref in enumerate(plane_refs):
        image = sum(
            ref[place_of(step, number, plane_count)] for step, ref in enumerate(partial_refs)
        )
        if number == 0:
            image_ref[...] = image
            probes = probes_ref[...]
        else:
            middle = feature_count + probe_count
            probes = plane_ref[feature_count:middle, :].astype(jnp.float32)
            probes = probes + plane_ref[middle:, :].astype(jnp.float32)
        products[0] += probes * probes
        products[1] += probes * image
        products[2] += image * image
    sums = jnp.zeros(sums_ref.shape, jnp.float32)
    for number, product in enumerate(products):
        sums = jnp.where(lane == number, jnp.sum(product, axis=1, keepdims=True), sums)
    sums_ref[...] = sums


def finish_kernel(image_ref, probes_ref, *refs):
    *sums_refs, solution_ref, residual_ref, direction_ref = refs
    sums = jnp.zeros(sums_refs[0].shape[-2:], jnp.float32)
    for ref in sums_refs:
        value = ref[...]
        sums = sums + (value if value.ndim == 2 else jnp.sum(value, axis=0))
    start_norms, curvature, image_norms = sums[:, 0:1], sums[:, 1:2], sums[:, 2:3]
    alpha = start_norms / curvature
    new_norms = start_norms - 2.0 * alpha * curvature + alpha * alpha * image_norms
    probes = probes_ref[...]
    residual = probes - alpha * image_ref[...]
    solution_ref[...] = alpha * probes
    residual_ref[...] = residual
    direction_ref[...] = residual + (new_norms / start_norms) * probes


def paired(count):
    return count & (count - 1) == 0


def source_of(device, step, count):
    return device ^ step if paired(count) else (device - step) % count


def place_of(step, number, count):
    return step ^ number if paired(count) else (number - step) % count


def in_order(blocks, places):
    return [blocks[place] for place in places] if len(blocks) == len(places) else blocks


def everywhere(value, axes, count):
    if count > DIRECT:
        return [lax.all_gather(value, axes, axis=0, tiled=False)]
    return [value] + [
        lax.ppermute(value, axes, [(source_of(i, step, count), i) for i in range(count)])
        for step in range(1, count)
    ]


def along_line(value, line_count, sub_count):
    if line_count > DIRECT or sub_count != 2:
        return everywhere(value, LINE, line_count)
    blocks = [value]
    for step in range(1, line_count):
        pairs = [
            (2 * source_of(place, step, line_count) + 1 - core, 2 * place + core)
            for place in range(line_count)
            for core in range(2)
        ]
        blocks.append(lax.ppermute(value, LINE + ("sub",), pairs))
    return blocks


def plane_blocks(value, shape):
    grp_count, sub_count = shape
    if sub_count != 2 or not paired(grp_count):
        return everywhere(value, PLANE, grp_count * sub_count)
    blocks = everywhere(value, ("sub",), sub_count)
    moved = [everywhere(block, ("grp",), grp_count) for block in blocks]
    return [moved[sub][grp] for grp in range(grp_count) for sub in range(sub_count)]


def make_local(plane_shape, line_count):
    plane_count = plane_shape[0] * plane_shape[1]

    def local(features, lengthscale, noise_var, probes):
        feature_count, width = features.shape
        probe_count = probes.shape[0]
        scaled = (features.astype(jnp.float32) / lengthscale[:, None]).astype(jnp.bfloat16)
        line, plane = pl.pallas_call(
            pack_kernel,
            out_shape=(
                jax.ShapeDtypeStruct((feature_count + probe_count, width), jnp.bfloat16),
                jax.ShapeDtypeStruct((feature_count + 2 * probe_count, width), jnp.bfloat16),
            ),
            compiler_params=VMEM,
        )(scaled, probes)
        lines = along_line(line, line_count, plane_shape[1])
        planes = plane_blocks(plane, plane_shape)
        if len(lines) > 1:
            early, late = lines[:1] + lines[2:], lines[1]
        else:
            early, late = [], lines[0]
        depth = feature_count + 2 * HALF
        work = plane_count * width * width
        rows, columns, total = pl.pallas_call(
            lambda *refs: near_kernel(feature_count, *refs),
            out_shape=(
                jax.ShapeDtypeStruct((depth, 2 * width), jnp.bfloat16),
                jax.ShapeDtypeStruct((max(len(early), 1), width, depth), jnp.bfloat16),
                jax.ShapeDtypeStruct((probe_count, 2 * width), jnp.float32),
            ),
            compiler_params=VMEM,
            cost_estimate=pl.CostEstimate(
                flops=6 * work * depth, bytes_accessed=4 * plane_count * width, transcendentals=3 * work
            ),
        )(*planes[:2], *early, noise_var[None, :], probes)
        far = pl.pallas_call(
            lambda *refs: far_kernel(feature_count, *refs),
            out_shape=jax.ShapeDtypeStruct(
                (plane_count // 2 - 1, depth, 2 * width), jnp.bfloat16
            ),
            compiler_params=VMEM,
        )(*planes[2:])
        partial = pl.pallas_call(
            lambda *refs: image_kernel(feature_count, plane_count, *refs),
            out_shape=jax.ShapeDtypeStruct((plane_count, probe_count, width), jnp.float32),
            compiler_params=VMEM,
        )(rows, total, far, columns, *early, late)
        partials = everywhere(partial, PLANE, plane_count)
        image, sums = pl.pallas_call(
            lambda *refs: combine_kernel(feature_count, plane_count, *refs),
            out_shape=(
                jax.ShapeDtypeStruct(probes.shape, jnp.float32),
                jax.ShapeDtypeStruct((probe_count, 128), jnp.float32),
            ),
            compiler_params=VMEM,
        )(*planes, probes, *in_order(partials, PARTIALS))
        outs = (jax.ShapeDtypeStruct(probes.shape, jnp.float32),) * 3
        return pl.pallas_call(finish_kernel, out_shape=outs, compiler_params=VMEM)(
            image, probes, *in_order(along_line(sums, line_count, plane_shape[1]), SUMS)
        )

    return local


def solution(mesh):
    plane_shape = (mesh.shape["grp"], mesh.shape["sub"])
    spread = P(None, ("parts", "blk", "grp", "sub"))
    return jax.shard_map(
        make_local(plane_shape, mesh.shape["blk"]),
        mesh=mesh,
        in_specs=(spread, P("parts"), P(("parts", "blk", "grp", "sub")), spread),
        out_specs=(spread, spread, spread),
        check_vma=False,
    )
```

```python
import jax
import jax.numpy as jnp
from jax import lax
from jax.experimental import pallas as pl
from jax.experimental.pallas import tpu as pltpu
from jax.sharding import PartitionSpec as P

PLANE = ("grp", "sub")
LINE = ("blk",)
DIRECT = 8
VMEM = pltpu.CompilerParams(vmem_limit_bytes=40 * 1024 * 1024)
PARTIALS, PARTIALS_BACK = (0, 1, 2, 3), (0, 1, 2, 3)
SUMS = (0, 2, 1, 3)
HALF = 8


def pieces_of(value):
    pieces = []
    for _ in range(3):
        piece = value.astype(jnp.bfloat16).astype(jnp.float32)
        pieces.append(piece)
        value = value - piece
    return pieces


def norm_rows(scaled, place):
    norms = -0.5 * jnp.sum(jnp.square(scaled.astype(jnp.float32)), axis=0, keepdims=True)
    row = lax.broadcasted_iota(jnp.int32, (2 * HALF, scaled.shape[1]), 0)
    here, there = place * HALF, (1 - place) * HALF
    rows = jnp.where((row >= there) & (row < there + 3), 1.0, 0.0)
    for number, piece in enumerate(pieces_of(norms)):
        rows = jnp.where(row == here + number, piece, rows)
    return rows.astype(jnp.bfloat16)


def pack_kernel(scaled_ref, probes_ref, line_ref, plane_ref):
    high, low, _ = pieces_of(probes_ref[...])
    high, low = high.astype(jnp.bfloat16), low.astype(jnp.bfloat16)
    line_ref[...] = jnp.concatenate([scaled_ref[...], high], axis=0)
    plane_ref[...] = jnp.concatenate([scaled_ref[...], high, low], axis=0)


def columns_of(block, feature_count):
    scaled = block[:feature_count, :]
    columns = jnp.concatenate([scaled, norm_rows(scaled, 0)], axis=0)
    return columns.astype(jnp.float32).T.astype(jnp.bfloat16)


def rows_of(ref, feature_count):
    scaled = ref[:feature_count, :]
    return jnp.concatenate([scaled, norm_rows(scaled, 1)], axis=0)


def product(columns, probes, rows):
    exponent = jnp.dot(columns, rows, preferred_element_type=jnp.float32)
    weights = jnp.exp(exponent).astype(jnp.bfloat16)
    return jnp.dot(probes, weights, preferred_element_type=jnp.float32)


def side_by_side(refs, feature_count):
    return jnp.concatenate([rows_of(ref, feature_count) for ref in refs], axis=1)


def near_kernel(feature_count, *refs):
    plane_refs, line_refs = refs[:2], refs[2:-5]
    noise_ref, probes_ref, rows_ref, columns_ref, total_ref = refs[-5:]
    rows = side_by_side(plane_refs, feature_count)
    rows_ref[...] = rows
    start = noise_ref[...] * probes_ref[...]
    total = jnp.concatenate([start, jnp.zeros_like(start)], axis=1)
    if line_refs:
        columns = [columns_of(ref[...], feature_count) for ref in line_refs]
        for number, value in enumerate(columns):
            columns_ref[number] = value
        probes = jnp.concatenate([ref[feature_count:, :] for ref in line_refs], axis=1)
        total += product(jnp.concatenate(columns, axis=0), probes, rows)
    total_ref[...] = total


def far_kernel(feature_count, *refs):
    *plane_refs, far_ref = refs
    for place in range(0, len(plane_refs), 2):
        far_ref[place // 2] = side_by_side(plane_refs[place : place + 2], feature_count)


def image_kernel(feature_count, plane_count, *refs):
    rows_ref, total_ref = refs[:2]
    far_ref, columns_ref, *line_refs = refs[2:-1]
    partial_ref = refs[-1]
    width = partial_ref.shape[2]
    rows = [rows_ref[...]] + [far_ref[number] for number in range(plane_count // 2 - 1)]
    totals = [total_ref[...]] + [jnp.zeros(total_ref.shape, jnp.float32)] * (len(rows) - 1)
    if len(line_refs[0].shape) == 2:
        *early, late = [ref[...] for ref in line_refs]
        late_columns = columns_of(late, feature_count)
        columns = [columns_ref[number] for number in range(len(early))]
        columns = jnp.concatenate(columns + [late_columns], axis=0)
        probes = jnp.concatenate([block[feature_count:, :] for block in early + [late]], axis=1)
        near = totals[0] + product(late_columns, late[feature_count:, :], rows[0])
        totals = [near] + [product(columns, probes, pair) for pair in rows[1:]]
    else:

        def add_block(number, totals):
            block = line_refs[0][number]
            columns = columns_of(block, feature_count)
            return [
                total + product(columns, block[feature_count:, :], pair)
                for pair, total in zip(rows, totals)
            ]

        totals = lax.fori_loop(0, line_refs[0].shape[0], add_block, totals)
    for number in range(plane_count):
        place = number % 2 * width
        partial_ref[number] = totals[number // 2][:, place : place + width]


def combine_kernel(feature_count, plane_count, *refs):
    plane_refs, probes_ref = refs[:plane_count], refs[plane_count]
    partial_refs = in_order(refs[plane_count + 1 : -2], PARTIALS_BACK)
    image_ref, sums_ref = refs[-2:]
    probe_count = image_ref.shape[0]
    lane = lax.broadcasted_iota(jnp.int32, sums_ref.shape, 1)
    products = [0.0, 0.0, 0.0]
    for number, plane_ref in enumerate(plane_refs):
        image = sum(
            ref[place_of(step, number, plane_count)] for step, ref in enumerate(partial_refs)
        )
        if number == 0:
            image_ref[...] = image
            probes = probes_ref[...]
        else:
            middle = feature_count + probe_count
            probes = plane_ref[feature_count:middle, :].astype(jnp.float32)
            probes = probes + plane_ref[middle:, :].astype(jnp.float32)
        products[0] += probes * probes
        products[1] += probes * image
        products[2] += image * image
    sums = jnp.zeros(sums_ref.shape, jnp.float32)
    for number, product in enumerate(products):
        sums = jnp.where(lane == number, jnp.sum(product, axis=1, keepdims=True), sums)
    sums_ref[...] = sums


def finish_kernel(image_ref, probes_ref, *refs):
    *sums_refs, solution_ref, residual_ref, direction_ref = refs
    sums = jnp.zeros(sums_refs[0].shape[-2:], jnp.float32)
    for ref in sums_refs:
        value = ref[...]
        sums = sums + (value if value.ndim == 2 else jnp.sum(value, axis=0))
    start_norms, curvature, image_norms = sums[:, 0:1], sums[:, 1:2], sums[:, 2:3]
    alpha = start_norms / curvature
    new_norms = start_norms - 2.0 * alpha * curvature + alpha * alpha * image_norms
    probes = probes_ref[...]
    residual = probes - alpha * image_ref[...]
    solution_ref[...] = alpha * probes
    residual_ref[...] = residual
    direction_ref[...] = residual + (new_norms / start_norms) * probes


def paired(count):
    return count & (count - 1) == 0


def source_of(device, step, count):
    return device ^ step if paired(count) else (device - step) % count


def place_of(step, number, count):
    return step ^ number if paired(count) else (number - step) % count


def in_order(blocks, places):
    return [blocks[place] for place in places] if len(blocks) == len(places) else blocks


def everywhere(value, axes, count):
    if count > DIRECT:
        return [lax.all_gather(value, axes, axis=0, tiled=False)]
    return [value] + [
        lax.ppermute(value, axes, [(source_of(i, step, count), i) for i in range(count)])
        for step in range(1, count)
    ]


def along_line(value, line_count, sub_count):
    if line_count > DIRECT or sub_count != 2:
        return everywhere(value, LINE, line_count)
    blocks = [value]
    for step in range(1, line_count):
        pairs = [
            (2 * source_of(place, step, line_count) + 1 - core, 2 * place + core)
            for place in range(line_count)
            for core in range(2)
        ]
        blocks.append(lax.ppermute(value, LINE + ("sub",), pairs))
    return blocks


def plane_blocks(value, shape):
    grp_count, sub_count = shape
    if sub_count != 2 or not paired(grp_count):
        return everywhere(value, PLANE, grp_count * sub_count)
    blocks = everywhere(value, ("sub",), sub_count)
    moved = [everywhere(block, ("grp",), grp_count) for block in blocks]
    return [moved[sub][grp] for grp in range(grp_count) for sub in range(sub_count)]


def make_local(plane_shape, line_count):
    plane_count = plane_shape[0] * plane_shape[1]

    def local(features, lengthscale, noise_var, probes):
        feature_count, width = features.shape
        probe_count = probes.shape[0]
        scaled = (features.astype(jnp.float32) / lengthscale[:, None]).astype(jnp.bfloat16)
        line, plane = pl.pallas_call(
            pack_kernel,
            out_shape=(
                jax.ShapeDtypeStruct((feature_count + probe_count, width), jnp.bfloat16),
                jax.ShapeDtypeStruct((feature_count + 2 * probe_count, width), jnp.bfloat16),
            ),
            compiler_params=VMEM,
        )(scaled, probes)
        lines = along_line(line, line_count, plane_shape[1])
        planes = plane_blocks(plane, plane_shape)
        if len(lines) > 1:
            early, late = lines[:1] + lines[2:], lines[1]
        else:
            early, late = [], lines[0]
        depth = feature_count + 2 * HALF
        work = plane_count * width * width
        rows, columns, total = pl.pallas_call(
            lambda *refs: near_kernel(feature_count, *refs),
            out_shape=(
                jax.ShapeDtypeStruct((depth, 2 * width), jnp.bfloat16),
                jax.ShapeDtypeStruct((max(len(early), 1), width, depth), jnp.bfloat16),
                jax.ShapeDtypeStruct((probe_count, 2 * width), jnp.float32),
            ),
            compiler_params=VMEM,
            cost_estimate=pl.CostEstimate(
                flops=6 * work * depth, bytes_accessed=4 * plane_count * width, transcendentals=3 * work
            ),
        )(*planes[:2], *early, noise_var[None, :], probes)
        far = pl.pallas_call(
            lambda *refs: far_kernel(feature_count, *refs),
            out_shape=jax.ShapeDtypeStruct(
                (plane_count // 2 - 1, depth, 2 * width), jnp.bfloat16
            ),
            compiler_params=VMEM,
        )(*planes[2:])
        partial = pl.pallas_call(
            lambda *refs: image_kernel(feature_count, plane_count, *refs),
            out_shape=jax.ShapeDtypeStruct((plane_count, probe_count, width), jnp.float32),
            compiler_params=VMEM,
        )(rows, total, far, columns, *early, late)
        partials = everywhere(partial, PLANE, plane_count)
        image, sums = pl.pallas_call(
            lambda *refs: combine_kernel(feature_count, plane_count, *refs),
            out_shape=(
                jax.ShapeDtypeStruct(probes.shape, jnp.float32),
                jax.ShapeDtypeStruct((probe_count, 128), jnp.float32),
            ),
            compiler_params=VMEM,
        )(*planes, probes, *in_order(partials, PARTIALS))
        outs = (jax.ShapeDtypeStruct(probes.shape, jnp.float32),) * 3
        return pl.pallas_call(finish_kernel, out_shape=outs, compiler_params=VMEM)(
            image, probes, *in_order(along_line(sums, line_count, plane_shape[1]), SUMS)
        )

    return local


def solution(mesh):
    plane_shape = (mesh.shape["grp"], mesh.shape["sub"])
    spread = P(None, ("parts", "blk", "grp", "sub"))
    return jax.shard_map(
        make_local(plane_shape, mesh.shape["blk"]),
        mesh=mesh,
        in_specs=(spread, P("parts"), P(("parts", "blk", "grp", "sub")), spread),
        out_specs=(spread, spread, spread),
        check_vma=False,
    )
```
